32 devices in a mesh: seq: 8 (over z, y), head: 4 (over x, core).
Axes of the slice: x: 2, y: 2, z: 4, core: 2. Of those that a mesh axis runs over, the one named last changes fastest.
Arguments:
- tokens: bfloat16 [65536, 512], P(('seq', 'head')), may hold values from -6 to 6
- gain_first: float32 [512], replicated, may hold values from 0.5 to 1.5
- w_query: bfloat16 [512, 512], P(None, 'head'), may hold values from -0.5 to 0.5
- w_key: bfloat16 [512, 512], P(None, 'head'), may hold values from -0.25 to 0.25
- w_value: bfloat16 [512, 512], P(None, 'head'), may hold values from -0.25 to 0.25
- w_out: bfloat16 [512, 512], P('head'), may hold values from -1 to 1
- gain_second: float32 [512], replicated, may hold values from 0.5 to 1.5
- w_control: bfloat16 [512, 8], replicated, may hold values from -0.125 to 0.125
- w_expand: bfloat16 [8, 512, 2048], P('seq'), may hold values from -1.5 to 1.5
- b_expand: float32 [8, 2048], P('seq'), may hold values from -1 to 1
- w_reduce: bfloat16 [8, 2048, 512], P('seq'), may hold values from -1 to 1
- b_reduce: float32 [8, 512], P('seq'), may hold values from -3 to 3
- lengths: int32 [8, 32], P('seq'), may hold values from 0 to 1024, as said below
- grad_output: bfloat16 [65536, 512], P(('seq', 'head')), may hold values from -6 to 6
Outputs:
- output: bfloat16 [65536, 512], P(('seq', 'head'))
- grad_tokens: float32 [65536, 512], P(('seq', 'head'))
- grad_gain_first: float32 [512], replicated
- grad_query: float32 [512, 512], P(None, 'head')
- grad_key: float32 [512, 512], P(None, 'head')
- grad_value: float32 [512, 512], P(None, 'head')
- grad_w_out: float32 [512, 512], P('head')
- grad_gain_second: float32 [512], replicated
- grad_control: float32 [512, 8], replicated
- grad_expand: float32 [8, 512, 2048], P('seq')
- grad_expand_bias: float32 [8, 2048], P('seq')
- grad_reduce: float32 [8, 2048, 512], P('seq')
- grad_reduce_bias: float32 [8, 512], P('seq')
The draws below stay inside these ranges and needn't reach their ends.
Inputs may be any that keep to these rules, and one draw needn't show every extreme that they name: Row s lists, in order, the lengths of the sequences packed in the 8192 places of index s of seq, 8 blocks of four entries, one block for each 1024 places; a block is either one sequence of 1024 tokens followed by three zeros or four sequences of 64 to 448 tokens that sum to 1024. A row is of one kind throughout, and both kinds occur in every draw.
All inputs are finite; a program needn't handle non-finite values.
Results may differ from the reference program's by a relative error of at most 0.028.
Values may be sent and summed in bfloat16 or wider, within the bound.
No kernel may reach another device: no remote copies, remote signals or barrier semaphores. Data moves between devices by JAX's collectives and lax.ppermute only.
A program may use at most 192 MiB of HBM per device.

```python
from functools import partial
import jax
import jax.numpy as jnp
from jax import lax

D = 512
HEADS = 8
HEAD_DIM = 64
FF = 2048
GROUP = 32
LONG = 1024
TOK_DEV = 8192
ROWS = 2048
TOKENS = 65536
EXPERTS = 8
N_SEQ = 8
N_HEAD = 4


def draw_lengths(key, part):
    key = jax.random.fold_in(key, 11)
    pick_key, other_key, kind_key, spread_key = jax.random.split(key, 4)
    long_slot = jax.random.randint(pick_key, (), 0, N_SEQ)
    short_slot = (long_slot + jax.random.randint(other_key, (), 1, N_SEQ)) % N_SEQ
    kind_bits = jax.random.randint(kind_key, (N_SEQ,), 0, 2)
    slot_ids = jnp.arange(N_SEQ)
    kind_bits = jnp.where(slot_ids == long_slot, 1, jnp.where(slot_ids == short_slot, 0, kind_bits))
    blocks = TOK_DEV // LONG
    spread = LONG // 16
    three_parts = LONG // 4 + jax.random.randint(spread_key, (N_SEQ, blocks, 3), -spread, spread + 1)
    tail_length = LONG - jnp.sum(three_parts, axis=2, keepdims=True)
    short_rows = jnp.concatenate([three_parts, tail_length], axis=2)
    long_pattern = jnp.concatenate([jnp.full((N_SEQ, blocks, 1), LONG, jnp.int32), jnp.zeros((N_SEQ, blocks, 3), jnp.int32)], axis=2)
    chosen = jnp.where(kind_bits[:, None, None] == 1, long_pattern, short_rows)
    return chosen.reshape(N_SEQ, blocks * 4).astype(jnp.int32)


def levels(own_key, dims, cuts, low, largest):
    loudness = 1.0
    for position, parts in cuts:
        draws = jax.random.uniform(jax.random.fold_in(jax.random.fold_in(own_key, 6), position), (parts,), jnp.float32, low / len(cuts), largest / len(cuts))
        loudness = loudness * jnp.repeat(jnp.exp(draws), dims[position] // parts).reshape((-1,) + (1,) * (len(dims) - 1 - position))
    return loudness


def normal_values(own_key, shape, scale, limit, cuts=(), held_as=jnp.bfloat16):
    values = jax.random.normal(own_key, shape, jnp.float32) * scale
    if len(cuts) > 0:
        values = levels(own_key, shape, cuts, -0.22, 0.18) * values
    return jnp.clip(values, min=-limit, max=limit).astype(held_as)


def setup_inputs(seed: int = 0) -> dict:
    keys = jax.random.split(jax.random.key(seed), 15)
    return {
        "tokens": normal_values(keys[0], (TOKENS, D), 1.0, 6.0, ((0, 32),)),
        "gain_first": jnp.clip(1.0 + 0.1 * jax.random.normal(keys[1], (D,), jnp.float32), 0.5, 1.5),
        "w_query": normal_values(keys[2], (D, D), (D // 4) ** -0.5, 0.5, ((1, 4),)),
        "w_key": normal_values(keys[3], (D, D), D ** -0.5, 0.25, ((1, 4),)),
        "w_value": normal_values(keys[4], (D, D), D ** -0.5, 0.25, ((1, 4),)),
        "w_out": normal_values(keys[5], (D, D), (D // 16) ** -0.5, 1.0, ((0, 4),)),
        "gain_second": jnp.clip(1.0 + 0.1 * jax.random.normal(keys[6], (D,), jnp.float32), 0.5, 1.5),
        "w_control": normal_values(keys[7], (D, EXPERTS), (4 * D) ** -0.5, 0.125),
        "w_expand": normal_values(keys[8], (EXPERTS, D, FF), (D // 32) ** -0.5, 1.5, ((0, 8),)),
        "b_expand": normal_values(keys[9], (EXPERTS, FF), 0.2, 1.0, ((0, 8),), jnp.float32),
        "w_reduce": normal_values(keys[10], (EXPERTS, FF, D), (FF // 64) ** -0.5, 1.0, ((0, 8),)),
        "b_reduce": normal_values(keys[11], (EXPERTS, D), 0.5, 3.0, ((0, 8),), jnp.float32),
        "lengths": draw_lengths(jax.random.fold_in(keys[14], 71), 0),
        "grad_output": normal_values(keys[13], (TOKENS, D), 1.0, 6.0, ((0, 32),)),
    }


@jax.custom_vjp
def low(v):
    return lax.optimization_barrier(v.astype(jnp.bfloat16)).astype(jnp.float32)

@jax.custom_vjp
def low_back(v):
    return v

def low_keep(v):
    return (low(v), None)

def low_pass(kept, grad):
    return (grad,)

def back_keep(v):
    return (v, None)

def back_low(kept, grad):
    return (low(grad),)
low.defvjp(low_keep, low_pass)
low_back.defvjp(back_keep, back_low)
EPSILON = 1e-05
MASKED = -1000000000.0
PRECISE = lax.Precision.HIGHEST

def normalize(matrix, gain):
    centre = lax.optimization_barrier(jnp.mean(matrix, axis=-1, keepdims=True))
    shifted = matrix - centre
    return shifted * lax.rsqrt(lax.optimization_barrier(jnp.mean(shifted * shifted, axis=-1, keepdims=True)) + EPSILON) * gain

def document_ids(lengths, extent):
    bounds = jnp.cumsum(lengths, axis=-1)
    places = jnp.arange(extent, dtype=jnp.int32)
    return lax.optimization_barrier(jnp.sum((places[None, :, None] >= bounds[:, None, :]).astype(jnp.int32), axis=-1)).astype(jnp.int32)

def attend(operands):
    queries, key_rows, value_rows, doc_block = operands
    scaling = queries.shape[-1] ** (-0.5)
    scores = low_back(jnp.einsum('qhd,khd->hqk', queries, key_rows, precision=PRECISE) * scaling)
    extent = doc_block.shape[0]
    row_ids = lax.broadcasted_iota(jnp.int32, (extent, extent), 0)
    col_ids = lax.broadcasted_iota(jnp.int32, (extent, extent), 1)
    allowed = (doc_block[:, None] == doc_block[None, :]) & (row_ids >= col_ids)
    scores = jnp.where(allowed[None], scores, MASKED)
    probs = low(jax.nn.softmax(scores, axis=-1))
    return jnp.einsum('hqk,khd->qhd', probs, value_rows, precision=PRECISE)

def expert(operands):
    mixed_rows, w_expand, b_expand, w_reduce, b_reduce = operands
    pre_act = low_back(jnp.dot(mixed_rows, w_expand, precision=PRECISE) + b_expand)
    activated = low(jax.nn.gelu(pre_act))
    return low(low_back(jnp.dot(activated, w_reduce, precision=PRECISE) + b_reduce))

def forward(doc_all, inputs, gain_first, w_query, w_key, w_value, w_out, gain_second, w_control, w_expand, b_expand, w_reduce, b_reduce):
    normed_first = low(normalize(inputs, gain_first))
    blocks = TOKENS // LONG

    def heads_of(weight):
        product = jnp.dot(normed_first, weight, precision=PRECISE)
        return low(low_back(product)).reshape(blocks, LONG, HEADS, HEAD_DIM)
    attended = lax.map(jax.checkpoint(attend), (heads_of(w_query), heads_of(w_key), heads_of(w_value), doc_all.reshape(blocks, LONG)))
    attended = low(low_back(attended)).reshape(TOKENS, D)
    resid = inputs + low_back(jnp.dot(attended, w_out, precision=PRECISE))
    normed_second = low(low_back(normalize(resid, gain_second)))
    stride = GROUP // N_SEQ
    group_rows = ROWS // GROUP
    members = normed_second.reshape(N_SEQ, N_HEAD, N_SEQ, group_rows, stride, D)
    logits = low_back(jnp.einsum('shjqtd,de->shjqte', members, w_control, precision=PRECISE))
    mixing = low(jax.nn.softmax(logits, axis=(0, 4)))
    mixed_rows = low(low_back(jnp.einsum('shjqte,shjqtd->ehjqd', mixing, members, precision=PRECISE)))
    expert_out = lax.map(jax.checkpoint(expert), (mixed_rows.reshape(EXPERTS, N_HEAD * N_SEQ * group_rows, D), w_expand, b_expand, w_reduce, b_reduce))
    expert_out = expert_out.reshape(EXPERTS, N_HEAD, N_SEQ, group_rows, D)
    merged = low(low_back(jnp.einsum('shjqte,ehjqd->shjqtd', mixing, expert_out, precision=PRECISE)))
    return resid + merged.reshape(TOKENS, D)

def widen(matrix):
    return matrix.astype(jnp.float32)

def reference(tokens, gain_first, w_query, w_key, w_value, w_out, gain_second, w_control, w_expand, b_expand, w_reduce, b_reduce, lengths, grad_output):
    doc_all = document_ids(lengths, TOK_DEV).reshape(TOKENS)
    floats = tuple(map(widen, (tokens, gain_first, w_query, w_key, w_value, w_out, gain_second, w_control, w_expand, b_expand, w_reduce, b_reduce)))
    result, pullback = jax.vjp(partial(forward, doc_all), *floats)
    grads = pullback(widen(grad_output))
    return (result.astype(jnp.bfloat16), grads[0], grads[1], grads[2], grads[3], grads[4], grads[5], grads[6], grads[7], grads[8], grads[9], grads[10], grads[11])
```

```python
import functools
import jax
import jax.numpy as jnp
from jax import lax
from jax.sharding import PartitionSpec as P
from jax.experimental import pallas as pl
from jax.experimental.pallas import tpu as pltpu

HEAD_DIM = 64
GROUP = 32
LONG = 1024
TILE = 256
QUEUE = 32
EPSILON = 1e-05
MASKED = -1000000000.0
BF = jnp.bfloat16
F32 = jnp.float32
ROWS_BY_ROWS = (((0,), (0,)), ((), ()))
COLS_BY_COLS = (((1,), (1,)), ((), ()))
VMEM_LIMIT = 48 * 1024 * 1024


def dot(left, right):
    return jnp.dot(left, right, preferred_element_type=F32)


def dot_rows(left, right):
    return lax.dot_general(left, right, ROWS_BY_ROWS, preferred_element_type=F32)


def dot_cols(left, right):
    return lax.dot_general(left, right, COLS_BY_COLS, preferred_element_type=F32)


def normalize(matrix):
    centre = jnp.mean(matrix, axis=1, keepdims=True)
    shifted = matrix - centre
    scaling = lax.rsqrt(jnp.mean(shifted * shifted, axis=1, keepdims=True) + EPSILON)
    return shifted * scaling, scaling


def normalize_back(grad_norm, gain, unit_rows, scaling):
    inner_grad = grad_norm * gain
    centred = (
        inner_grad
        - jnp.mean(inner_grad, axis=1, keepdims=True)
        - unit_rows * jnp.mean(inner_grad * unit_rows, axis=1, keepdims=True)
    )
    return scaling * centred, jnp.sum(grad_norm * unit_rows, axis=0, keepdims=True)


def whole(*shape):
    return pl.BlockSpec(shape, lambda *_: (0,) * len(shape))


def scalars():
    return pl.BlockSpec(memory_space=pltpu.SMEM)


def call(kernel, name, grid, in_specs, out_specs, out_shape, scratch=(), cost=(0, 0, 0), aliases=None):
    return pl.pallas_call(
        kernel,
        grid=grid,
        in_specs=in_specs,
        out_specs=out_specs,
        out_shape=out_shape,
        scratch_shapes=list(scratch),
        input_output_aliases=aliases or {},
        cost_estimate=pl.CostEstimate(
            flops=int(cost[0]), bytes_accessed=int(cost[1]), transcendentals=int(cost[2])
        ),
        compiler_params=pltpu.CompilerParams(vmem_limit_bytes=VMEM_LIMIT),
        name=name,
    )


def shape(dims, dtype):
    return jax.ShapeDtypeStruct(dims, dtype)


def tile_slot(row_tile, col_tile):
    return row_tile * (row_tile + 1) // 2 + col_tile


def halves(dtype):
    lane = lax.broadcasted_iota(jnp.int32, (1, 2 * HEAD_DIM), 1)
    first = (lane < HEAD_DIM).astype(F32)
    return first.astype(dtype), (1.0 - first).astype(dtype)


def forward_kernel(slots, pairs, chunk, chunks, *refs):
    refs = list(refs)
    place, lengths, tokens, gain_first = refs[:4]
    w_parts = refs[4 : 4 + pairs]
    o_parts = refs[4 + pairs : 4 + 2 * pairs]
    gain_second = refs[4 + 2 * pairs]
    outs = refs[5 + 2 * pairs :]
    normed, qkv_out, exps, inverse, attended, resid = outs[:6]
    second = outs[6 : 6 + slots]
    w_now, bias, attended_all, second_all = outs[6 + slots :]
    step = pl.program_id(0)
    pair_width = attended.shape[2]
    tiles = LONG // TILE

    @pl.when(step == 0)
    def _():
        unit, _ = normalize(tokens[...].astype(F32))
        normed[...] = (unit * gain_first[...]).astype(BF)
        base = 4 * (place[1] * chunks + chunk)
        first = lengths[0, base]
        second_bound = first + lengths[0, base + 1]
        third = second_bound + lengths[0, base + 2]
        for row_tile in range(tiles):
            row = lax.broadcasted_iota(jnp.int32, (TILE, 1), 0) + row_tile * TILE
            begin = jnp.where(row >= first, first, 0)
            begin = jnp.where(row >= second_bound, second_bound, begin)
            begin = jnp.where(row >= third, third, begin)
            col = lax.broadcasted_iota(jnp.int32, (TILE, LONG), 1)
            allowed = (col <= row) & (col >= begin)
            bias[pl.ds(row_tile * TILE, TILE), :] = jnp.where(allowed, 0.0, MASKED)

    for index, part in enumerate(w_parts):

        @pl.when(step == index)
        def _(part=part):
            w_now[...] = part[...]

    qkv = dot(normed[...], w_now[...]).astype(BF)
    qkv_out[0] = qkv
    queries = qkv[:, :pair_width] * BF(HEAD_DIM**-0.5)
    key_rows = qkv[:, pair_width : 2 * pair_width]
    value_rows = qkv[:, 2 * pair_width :]
    low_half, high_half = halves(BF)
    is_low = lax.broadcasted_iota(jnp.int32, (TILE, pair_width), 1) < HEAD_DIM
    masks = ((low_half, high_half), (high_half, low_half))
    head_queries = [queries * own for own, other in masks]
    head_values = [value_rows * own + other for own, other in masks]
    for row_tile in range(tiles):
        begin, extent = row_tile * TILE, (row_tile + 1) * TILE
        raw = []
        for head in range(2):
            scores = dot_cols(head_queries[head][begin:extent], key_rows[:extent])
            scores = scores + bias[begin:extent, :extent]
            highest = jnp.max(scores, axis=1, keepdims=True)
            powers = jnp.exp(scores - highest).astype(BF)
            for col_tile in range(row_tile + 1):
                exps[0, head, tile_slot(row_tile, col_tile)] = powers[
                    :, col_tile * TILE : (col_tile + 1) * TILE
                ]
            raw.append(dot(powers, head_values[head][:extent]))
        totals = jnp.where(
            is_low, pltpu.roll(raw[0], HEAD_DIM, 1), pltpu.roll(raw[1], HEAD_DIM, 1)
        )
        inverted = 1.0 / totals
        inverse[0, begin:extent] = inverted
        attended_tile = (jnp.where(is_low, raw[0], raw[1]) * inverted).astype(BF)
        attended[0, begin:extent] = attended_tile
        attended_all[step, begin:extent] = attended_tile

    @pl.when(step == pairs - 1)
    def _():
        total = tokens[...].astype(F32)
        rows = jnp.concatenate([attended_all[index] for index in range(pairs)], axis=1)
        weights = jnp.concatenate([part[...] for part in o_parts], axis=0)
        total = total + dot(rows, weights)
        resid[...] = total
        unit, _ = normalize(total)
        second_all[...] = (unit * gain_second[...]).astype(BF)
        share = LONG // slots
        for index in range(slots):
            begin = pl.multiple_of((place[0] ^ index) * share, share)
            second[index][...] = second_all[pl.ds(begin, share), :]


def forward_part(chunk, place, lengths, tokens, gain_first, w_parts, o_parts, gain_second, slots):
    rows, width = tokens.shape
    pairs = len(w_parts)
    triple = w_parts[0].shape[1]
    pair_width = triple // 3
    share = LONG // slots
    kept = LONG // TILE * (LONG // TILE + 1) // 2
    per_pair = lambda *dims: pl.BlockSpec((1,) + dims, lambda i: (i,) + (0,) * len(dims))
    outs = call(
        functools.partial(forward_kernel, slots, pairs, chunk, rows // LONG),
        f"forward_{chunk}",
        (pairs,),
        [scalars(), scalars(), pl.BlockSpec((LONG, width), lambda i: (chunk, 0)), whole(1, width)]
        + [whole(width, triple)] * pairs
        + [whole(pair_width, width)] * pairs
        + [whole(1, width)],
        [
            whole(LONG, width),
            per_pair(LONG, triple),
            per_pair(2, kept, TILE, TILE),
            per_pair(LONG, pair_width),
            per_pair(LONG, pair_width),
            whole(LONG, width),
        ]
        + [whole(share, width)] * slots,
        [
            shape((LONG, width), BF),
            shape((pairs, LONG, triple), BF),
            shape((pairs, 2, kept, TILE, TILE), BF),
            shape((pairs, LONG, pair_width), F32),
            shape((pairs, LONG, pair_width), BF),
            shape((LONG, width), F32),
        ]
        + [shape((share, width), BF)] * slots,
        [
            pltpu.VMEM((width, triple), BF),
            pltpu.VMEM((LONG, LONG), F32),
            pltpu.VMEM((pairs, LONG, pair_width), BF),
            pltpu.VMEM((LONG, width), BF),
        ],
        (10e9, 25e6, 5e6),
    )(place, lengths, tokens, gain_first, *w_parts, *o_parts, gain_second)
    return outs[:6], list(outs[6:])


def pack_kernel(slots, chunks, place, rows, *outs):
    share = LONG // slots
    for chunk in range(chunks):
        for index in range(slots):
            begin = pl.multiple_of(chunk * LONG + (place[0] ^ index) * share, share)
            outs[index][chunk] = rows[pl.ds(begin, share), :]


def pack_rows(place, rows, slots):
    total, width = rows.shape
    chunks, share = total // LONG, LONG // slots
    return call(
        functools.partial(pack_kernel, slots, chunks),
        "pack_cotangent",
        (1,),
        [scalars(), whole(total, width)],
        [whole(chunks, share, width)] * slots,
        [shape((chunks, share, width), BF)] * slots,
        cost=(0, 4 * total * width, 0),
    )(place, rows)


def group_mask(slots, columns):
    share = LONG // slots
    stride = share // QUEUE
    row = lax.broadcasted_iota(jnp.int32, (LONG, columns), 0)
    col = lax.broadcasted_iota(jnp.int32, (LONG, columns), 1)
    return ((row % share) // stride) == (col % QUEUE)


def mixing_kernel(slots, *refs):
    control = refs[0]
    members = refs[1 : 1 + slots]
    cotangents = refs[1 + slots : 1 + 2 * slots]
    mixing_out = refs[1 + 2 * slots]
    messages = refs[2 + 2 * slots :]
    columns = control.shape[1]
    rows = jnp.concatenate([part[...] for part in members], axis=0)
    grads = jnp.concatenate([part[0] for part in cotangents], axis=0)
    logits = jnp.where(group_mask(slots, columns), dot(rows, control[...]), -1e30)
    powers = jnp.exp(logits - jnp.max(logits, axis=0, keepdims=True))
    mixing = powers / jnp.sum(powers, axis=0, keepdims=True)
    mixing_out[...] = mixing
    low = mixing.astype(BF)
    mixed = dot_rows(low, rows).astype(BF)
    grad_out = dot_rows(low, grads).astype(BF)
    for index in range(slots):
        messages[index][:QUEUE] = mixed[index * QUEUE : (index + 1) * QUEUE]
        messages[index][QUEUE:] = grad_out[index * QUEUE : (index + 1) * QUEUE]


def mixing_part(chunk, control, members, cotangents):
    slots = len(members)
    width, columns = control.shape
    share = LONG // slots
    outs = call(
        functools.partial(mixing_kernel, slots),
        f"mixing_{chunk}",
        (1,),
        [whole(width, columns)]
        + [whole(share, width)] * slots
        + [pl.BlockSpec((1, share, width), lambda i: (chunk, 0, 0))] * slots,
        [whole(LONG, columns)] + [whole(2 * QUEUE, width)] * slots,
        [shape((LONG, columns), F32)] + [shape((2 * QUEUE, width), BF)] * slots,
        cost=(6 * LONG * columns * width, 4e6, LONG * columns),
    )(control, *members, *cotangents)
    return outs[0], list(outs[1:])


def expert_kernel(slots, *refs):
    messages = refs[:slots]
    w_expand, b_expand, w_reduce, b_reduce = refs[slots : slots + 4]
    answers = refs[slots + 4 : 2 * slots + 4]
    taken, grads, activated_out, grad_pre_out, out_sum, mixed_sum = refs[2 * slots + 4 :]
    step = pl.program_id(0)

    @pl.when(step == 0)
    def _():
        for index in range(slots):
            taken[index * QUEUE : (index + 1) * QUEUE] = messages[index][:QUEUE]
            grads[index * QUEUE : (index + 1) * QUEUE] = messages[index][QUEUE:]
        out_sum[...] = jnp.zeros_like(out_sum)
        mixed_sum[...] = jnp.zeros_like(mixed_sum)

    pre = dot(taken[...], w_expand[0]) + b_expand[...]
    slope = 0.7978845608028654
    square = pre * pre
    bend = jnp.tanh(slope * (pre + 0.044715 * (pre * square)))
    half = 0.5 * (1.0 + bend)
    activated = (pre * half).astype(BF)
    activated_out[...] = activated
    out_sum[...] += dot(activated, w_reduce[0])
    derivative = half + (0.5 * slope) * pre * (1.0 - bend * bend) * (1.0 + 0.134145 * square)
    grad_pre = (dot_cols(grads[...], w_reduce[0]) * derivative).astype(BF)
    grad_pre_out[...] = grad_pre
    mixed_sum[...] += dot_cols(grad_pre, w_expand[0])

    @pl.when(step == pl.num_programs(0) - 1)
    def _():
        for index in range(slots):
            part = slice(index * QUEUE, (index + 1) * QUEUE)
            answers[index][:QUEUE] = (out_sum[part] + b_reduce[...]).astype(BF)
            answers[index][QUEUE:] = mixed_sum[part].astype(BF)


def expert_part(chunk, messages, w_expand, b_expand, w_reduce, b_reduce):
    slots = len(messages)
    _, width, hidden = w_expand.shape
    count = slots * QUEUE
    cut = min(512, hidden)
    outs = call(
        functools.partial(expert_kernel, slots),
        f"expert_{chunk}",
        (hidden // cut,),
        [whole(2 * QUEUE, width)] * slots
        + [
            pl.BlockSpec((1, width, cut), lambda i: (0, 0, i)),
            pl.BlockSpec((1, cut), lambda i: (0, i)),
            pl.BlockSpec((1, cut, width), lambda i: (0, i, 0)),
            whole(1, width),
        ],
        [whole(2 * QUEUE, width)] * slots
        + [
            whole(count, width),
            whole(count, width),
            pl.BlockSpec((count, cut), lambda i: (0, i)),
            pl.BlockSpec((count, cut), lambda i: (0, i)),
        ],
        [shape((2 * QUEUE, width), BF)] * slots
        + [shape((count, width), BF)] * 2
        + [shape((count, hidden), BF)] * 2,
        [pltpu.VMEM((count, width), F32), pltpu.VMEM((count, width), F32)],
        (8 * count * width * hidden, 8e6, count * hidden),
    )(*messages, w_expand, b_expand, w_reduce, b_reduce)
    return list(outs[:slots]), outs[slots:]


def expert_weights_kernel(chunks, place, *refs):
    taken = refs[:chunks]
    grads = refs[chunks : 2 * chunks]
    activated = refs[2 * chunks : 3 * chunks]
    grad_pre = refs[3 * chunks : 4 * chunks]
    own_e, other_e, own_r, other_r, bias_e, bias_r, full_e, full_r = refs[4 * chunks :]
    join = lambda parts: jnp.concatenate([part[...] for part in parts], axis=0)
    pre = join(grad_pre)
    cotangent = join(grads)
    full_e[...] = dot_rows(join(taken), pre).astype(BF)
    full_r[...] = dot_rows(join(activated), cotangent).astype(BF)
    bias_e[...] = jnp.sum(pre.astype(F32), axis=0, keepdims=True)
    bias_r[...] = jnp.sum(cotangent.astype(F32), axis=0, keepdims=True)
    side = place[1] % 2
    for full, own, other in ((full_e, own_e, other_e), (full_r, own_r, other_r)):
        cut = full.shape[0] // 2
        own[...] = full[pl.ds(pl.multiple_of(side * cut, cut), cut), :]
        other[...] = full[pl.ds(pl.multiple_of((1 - side) * cut, cut), cut), :]


def expert_weights(place, saved):
    chunks = len(saved)
    taken, grads, activated, grad_pre = zip(*saved)
    count, width = taken[0].shape
    hidden = activated[0].shape[1]
    cut = min(512, hidden)
    wide = lambda rows: pl.BlockSpec((rows, cut), lambda i: (0, i))
    tall = pl.BlockSpec((cut // 2, width), lambda i: (i, 0))
    return call(
        functools.partial(expert_weights_kernel, chunks),
        "expert_weights",
        (hidden // cut,),
        [scalars()] + [whole(count, width)] * (2 * chunks) + [wide(count)] * (2 * chunks),
        [wide(width // 2), wide(width // 2), tall, tall, wide(1), whole(1, width)],
        [shape((width // 2, hidden), BF)] * 2
        + [shape((hidden // 2, width), BF)] * 2
        + [shape((1, hidden), F32), shape((1, width), F32)],
        [pltpu.VMEM((width, cut), BF), pltpu.VMEM((cut, width), BF)],
        (4 * chunks * count * width * hidden, 9e6, 0),
    )(place, *taken, *grads, *activated, *grad_pre)


def place_weights_kernel(place, own_e, other_e, own_r, other_r, out_e, out_r):
    side = place[1] % 2
    cut = own_e.shape[0]
    out_e[0, pl.ds(pl.multiple_of(side * cut, cut), cut), :] = own_e[...].astype(F32)
    out_e[0, pl.ds(pl.multiple_of((1 - side) * cut, cut), cut), :] = other_e[...].astype(F32)
    cut = own_r.shape[0]
    out_r[0, pl.ds(pl.multiple_of(side * cut, cut), cut), :] = own_r[...].astype(F32)
    out_r[0, pl.ds(pl.multiple_of((1 - side) * cut, cut), cut), :] = other_r[...].astype(F32)


def place_weights(place, own_e, other_e, own_r, other_r):
    half, hidden = own_e.shape
    width = own_r.shape[1]
    cut = min(512, hidden)
    wide = pl.BlockSpec((half, cut), lambda i: (0, i))
    tall = pl.BlockSpec((cut // 2, width), lambda i: (i, 0))
    return call(
        place_weights_kernel,
        "place_expert_weights",
        (hidden // cut,),
        [scalars(), wide, wide, tall, tall],
        [
            pl.BlockSpec((1, 2 * half, cut), lambda i: (0, 0, i)),
            pl.BlockSpec((1, cut, width), lambda i: (0, i, 0)),
        ],
        [shape((1, 2 * half, hidden), F32), shape((1, hidden, width), F32)],
        cost=(0, 12 * width * hidden, 0),
    )(place, own_e, other_e, own_r, other_r)


def unmix_kernel(slots, *refs):
    place, control, mixing_ref = refs[:3]
    members = refs[3 : 3 + slots]
    cotangents = refs[3 + slots : 3 + 2 * slots]
    answers = refs[3 + 2 * slots : 3 + 3 * slots]
    outs = refs[3 + 3 * slots :]
    back, merged, control_out = outs[:slots], outs[slots : 2 * slots], outs[2 * slots]
    rows = jnp.concatenate([part[...] for part in members], axis=0)
    grads = jnp.concatenate([part[0] for part in cotangents], axis=0)
    expert_out = jnp.concatenate([part[:QUEUE] for part in answers], axis=0)
    grad_mixed = jnp.concatenate([part[QUEUE:] for part in answers], axis=0)
    mixing = mixing_ref[...]
    low = mixing.astype(BF)
    grad_mixing = dot_cols(grads, expert_out) + dot_cols(rows, grad_mixed)
    weighted = mixing * grad_mixing
    grad_logits = weighted - mixing * jnp.sum(weighted, axis=0, keepdims=True)
    grad_logits = grad_logits.astype(BF)
    grad_rows = (dot(low, grad_mixed) + dot_cols(grad_logits, control[...])).astype(BF)
    merged_rows = dot(low, expert_out).astype(BF)
    grad_control = dot_rows(grad_logits, rows)
    share = LONG // slots
    for index in range(slots):
        back[index][...] = grad_rows[index * share : (index + 1) * share]
        merged[index][...] = merged_rows[index * share : (index + 1) * share]
        control_out[pl.ds(place[0] ^ index, 1), :] = jnp.sum(
            grad_control[index * QUEUE : (index + 1) * QUEUE], axis=0, keepdims=True
        )


def unmix_part(chunk, place, control, mixing, members, cotangents, answers):
    slots = len(members)
    width, columns = control.shape
    share = LONG // slots
    outs = call(
        functools.partial(unmix_kernel, slots),
        f"unmix_{chunk}",
        (1,),
        [scalars(), whole(width, columns), whole(LONG, columns)]
        + [whole(share, width)] * slots
        + [pl.BlockSpec((1, share, width), lambda i: (chunk, 0, 0))] * slots
        + [whole(2 * QUEUE, width)] * slots,
        [whole(share, width)] * (2 * slots) + [whole(slots, width)],
        [shape((share, width), BF)] * (2 * slots) + [shape((slots, width), F32)],
        cost=(12 * LONG * columns * width, 6e6, 0),
    )(place, control, mixing, *members, *cotangents, *answers)
    return list(outs[:slots]), list(outs[slots : 2 * slots]), outs[2 * slots]


def output_kernel(slots, place, *refs):
    resid = refs[0]
    merged = refs[1 : 1 + slots]
    out = refs[-1]
    share = LONG // slots
    for index in range(slots):
        begin = pl.multiple_of((place[0] ^ index) * share, share)
        rows = resid[pl.ds(begin, share), :] + merged[index][...].astype(F32)
        out[pl.ds(begin, share), :] = rows.astype(BF)


def output_part(chunk, chunks, place, resid, merged, previous):
    slots = len(merged)
    width = resid.shape[1]
    share = LONG // slots
    kernel = functools.partial(output_kernel, slots)
    ins = [place, resid, *merged]
    specs = [scalars(), whole(LONG, width)] + [whole(share, width)] * slots
    aliases = {}
    if previous is not None:
        aliases = {len(ins): 0}
        ins.append(previous)
        specs.append(pl.BlockSpec(memory_space=pl.ANY))
        kernel = functools.partial(output_kernel, slots)
        kernel = without_previous(kernel, len(ins) - 1)
    return call(
        kernel,
        f"output_{chunk}",
        (1,),
        specs,
        pl.BlockSpec((LONG, width), lambda i: (chunk, 0)),
        shape((chunks * LONG, width), BF),
        cost=(0, 4e6, 0),
        aliases=aliases,
    )(*ins)


def without_previous(kernel, position):
    def inner(*refs):
        return kernel(*refs[:position], *refs[position + 1 :])

    return inner


def backward_kernel(slots, pairs, later, *refs):
    refs = list(refs)
    place = refs[0]
    back = refs[1 : 1 + slots]
    (resid, grad_output, gain_second) = refs[1 + slots : 4 + slots]
    w_parts = refs[4 + slots : 4 + slots + pairs]
    o_parts = refs[4 + slots + pairs : 4 + slots + 2 * pairs]
    rest = refs[4 + slots + 2 * pairs :]
    normed, qkv, exps, inverse, attended, tokens, gain_first = rest[:7]
    rest = rest[7:]
    weights_before = None
    if later:
        weights_before = rest[0]
        rest = rest[1:]
    grad_tokens, weights_out, gains_out = rest[:3]
    (grad_resid, resid_low, normed_turned, first_sum, w_now, o_now, queries_sum, keys_turned, values_turned) = rest[3:]
    step = pl.program_id(0)
    pair_width = attended.shape[2]
    tiles = LONG // TILE
    share = LONG // slots

    @pl.when(step == 0)
    def _():
        for index in range(slots):
            begin = pl.multiple_of((place[0] ^ index) * share, share)
            grad_resid[pl.ds(begin, share), :] = back[index][...].astype(F32)
        unit, scaling = normalize(resid[...])
        through, gain_grad = normalize_back(grad_resid[...], gain_second[...], unit, scaling)
        gains_out[...] = jnp.zeros_like(gains_out)
        gains_out[1:2] = gain_grad
        total = grad_output[...].astype(F32) + through
        grad_resid[...] = total
        resid_low[...] = total.astype(BF)
        normed_turned[...] = normed[...].T
        first_sum[...] = jnp.zeros_like(first_sum)

    for index in range(pairs):

        @pl.when(step == pairs - 1 - index)
        def _(index=index):
            w_now[...] = w_parts[index][...]
            o_now[...] = o_parts[index][...]

    low = resid_low[...]
    grad_attended = dot_cols(low, o_now[...]).astype(BF)
    grad_out_weights = dot_rows(attended[0], low)
    wide = grad_attended.astype(F32)
    inverted = inverse[0]
    scaled = wide * inverted
    products = scaled * attended[0].astype(F32)
    scaled = scaled.astype(BF)
    low_half, high_half = halves(BF)
    low_wide, high_wide = halves(F32)
    queries = qkv[0, :, :pair_width] * BF(HEAD_DIM**-0.5)
    key_rows = qkv[0, :, pair_width : 2 * pair_width]
    value_rows = qkv[0, :, 2 * pair_width :]
    scaled_keys = key_rows * BF(HEAD_DIM**-0.5)
    queries_sum[...] = jnp.zeros_like(queries_sum)
    keys_turned[...] = jnp.zeros_like(keys_turned)
    values_turned[...] = jnp.zeros_like(values_turned)
    for head, (half, half_wide) in enumerate(((low_half, low_wide), (high_half, high_wide))):
        head_grads = scaled * half
        head_queries = queries * half
        head_keys = scaled_keys * half
        deltas = jnp.sum(products * half_wide, axis=1, keepdims=True)
        for row_tile in range(tiles):
            begin, extent = row_tile * TILE, (row_tile + 1) * TILE
            powers = jnp.concatenate(
                [exps[0, head, tile_slot(row_tile, col_tile)] for col_tile in range(row_tile + 1)],
                axis=1,
            )
            grad_probs = dot_cols(head_grads[begin:extent], value_rows[:extent])
            grad_scores = (powers.astype(F32) * (grad_probs - deltas[begin:extent])).astype(BF)
            queries_sum[begin:extent] += dot(grad_scores, head_keys[:extent])
            keys_turned[:, :extent] += dot_rows(head_queries[begin:extent], grad_scores)
            values_turned[:, :extent] += dot_rows(head_grads[begin:extent], powers)
    grads = jnp.concatenate(
        [queries_sum[...].astype(BF), keys_turned[...].T.astype(BF), values_turned[...].T.astype(BF)],
        axis=1,
    )
    first_sum[...] += dot_cols(grads, w_now[...])
    grad_weights = dot(normed_turned[...], grads)
    width = normed.shape[1]
    blocks = [grad_weights[:, index * pair_width : (index + 1) * pair_width] for index in range(3)]
    blocks += [
        grad_out_weights[:, index * pair_width : (index + 1) * pair_width]
        for index in range(width // pair_width)
    ]
    begin = 0
    for block in blocks:
        extent = begin + block.shape[0]
        if later:
            block = block + weights_before[0, begin:extent]
        weights_out[0, begin:extent] = block.astype(weights_out.dtype)
        begin = extent

    @pl.when(step == pairs - 1)
    def _():
        unit, scaling = normalize(tokens[...].astype(F32))
        through, gain_grad = normalize_back(first_sum[...], gain_first[...], unit, scaling)
        gains_out[0:1] = gain_grad
        grad_tokens[...] = grad_resid[...] + through


def backward_part(
    chunk, place, back, resid, grad_output, gain_second, w_parts, o_parts, saved, tokens, gain_first, before
):
    normed, qkv, exps, inverse, attended = saved
    rows, width = tokens.shape
    slots, pairs = len(back), len(w_parts)
    triple = w_parts[0].shape[1]
    pair_width = triple // 3
    share = LONG // slots
    kept = exps.shape[2]
    later = before is not None
    packed = 3 * width + width * pair_width // pair_width
    per_pair = lambda *dims: pl.BlockSpec((1,) + dims, lambda i: (pairs - 1 - i,) + (0,) * len(dims))
    chunk_rows = pl.BlockSpec((LONG, width), lambda i: (chunk, 0))
    ins = [place, *back, resid, grad_output, gain_second, *w_parts, *o_parts]
    ins += [normed, qkv, exps, inverse, attended, tokens, gain_first]
    specs = [scalars()] + [whole(share, width)] * slots + [whole(LONG, width), chunk_rows, whole(1, width)]
    specs += [whole(width, triple)] * pairs + [whole(pair_width, width)] * pairs
    specs += [
        whole(LONG, width),
        per_pair(LONG, triple),
        per_pair(2, kept, TILE, TILE),
        per_pair(LONG, pair_width),
        per_pair(LONG, pair_width),
        chunk_rows,
        whole(1, width),
    ]
    kernel = functools.partial(backward_kernel, slots, pairs, later)
    aliases = {}
    if later:
        ins += [before[1], before[0]]
        specs += [per_pair(packed, pair_width), pl.BlockSpec(memory_space=pl.ANY)]
        aliases = {len(ins) - 1: 0}
        kernel = without_previous(kernel, len(ins) - 1)
    return call(
        kernel,
        f"backward_{chunk}",
        (pairs,),
        specs,
        [chunk_rows, per_pair(packed, pair_width), whole(8, width)],
        [
            shape((rows, width), F32),
            shape((pairs, packed, pair_width), BF if chunk == rows // LONG - 1 else F32),
            shape((8, width), F32),
        ],
        [
            pltpu.VMEM((LONG, width), F32),
            pltpu.VMEM((LONG, width), BF),
            pltpu.VMEM((width, LONG), BF),
            pltpu.VMEM((LONG, width), F32),
            pltpu.VMEM((width, triple), BF),
            pltpu.VMEM((pair_width, width), BF),
            pltpu.VMEM((LONG, pair_width), F32),
            pltpu.VMEM((pair_width, LONG), F32),
            pltpu.VMEM((pair_width, LONG), F32),
        ],
        (25e9, 25e6, 0),
        aliases,
    )(*ins)


def split_kernel(slots, place, *refs):
    parts, outs, total = refs[: -slots - 1], refs[-slots - 1 : -1], refs[-1]
    added = parts[0][...].astype(F32)
    for part in parts[1:]:
        added = added + part[...].astype(F32)
    total[...] = added.astype(BF)
    share = total.shape[0] // slots
    for index in range(slots):
        begin = pl.multiple_of((place[0] ^ index) * share, share)
        outs[index][...] = total[pl.ds(begin, share), :]


def split_sum(place, parts, slots):
    rows, width = parts[0].shape
    share = rows // slots
    return call(
        functools.partial(split_kernel, slots),
        "split_weights",
        (1,),
        [scalars()] + [whole(rows, width)] * len(parts),
        [whole(share, width)] * slots,
        [shape((share, width), BF)] * slots,
        [pltpu.VMEM((rows, width), BF)],
        (0, 6e6, 0),
    )(place, *parts)


def gather_kernel(slots, place, *refs):
    parts, outs, total = refs[:slots], refs[slots:-1], refs[-1]
    share = parts[0].shape[0]
    for index in range(slots):
        begin = pl.multiple_of((place[0] ^ index) * share, share)
        total[pl.ds(begin, share), :] = parts[index][...].astype(F32)
    begin = 0
    for out in outs[:3]:
        out[...] = total[begin : begin + out.shape[0]]
        begin += out.shape[0]
    last = outs[3]
    cut = total.shape[1]
    for index in range(last.shape[1] // cut):
        last[:, index * cut : (index + 1) * cut] = total[begin : begin + last.shape[0]]
        begin += last.shape[0]


def gather_weights(place, parts, width):
    slots = len(parts)
    share, cut = parts[0].shape
    return call(
        functools.partial(gather_kernel, slots),
        "gather_weights",
        (1,),
        [scalars()] + [whole(share, cut)] * slots,
        [whole(width, cut)] * 3 + [whole(cut, width)],
        [shape((width, cut), F32)] * 3 + [shape((cut, width), F32)],
        [pltpu.VMEM((share * slots, cut), F32)],
        (0, 3e6, 0),
    )(place, *parts)


def partner(value, axis, offset):
    count = lax.axis_size(axis)
    return lax.ppermute(value, axis, [(index, index ^ offset) for index in range(count)])


def exchange(parts, axis):
    return [parts[0]] + [partner(part, axis, index) for index, part in enumerate(parts) if index]


def tree_sum(parts):
    while len(parts) > 1:
        parts = [parts[index] + parts[index + 1] for index in range(0, len(parts), 2)]
    return parts[0]


def gather_head(part):
    sibling = partner(part, "head", 1)
    across = partner(part, "head", 2)
    return [part, sibling, across, partner(across, "head", 1)]


def body(
    tokens,
    gain_first,
    w_query,
    w_key,
    w_value,
    w_out,
    gain_second,
    w_control,
    w_expand,
    b_expand,
    w_reduce,
    b_reduce,
    lengths,
    grad_output,
):
    rows_local, width = tokens.shape
    slots = lax.axis_size("seq")
    chunks = rows_local // LONG
    place = jnp.stack([lax.axis_index("seq"), lax.axis_index("head")]).astype(jnp.int32)
    gain_first = gain_first[None]
    gain_second = gain_second[None]
    w_parts = gather_head(jnp.concatenate([w_query, w_key, w_value], axis=1))
    o_parts = gather_head(w_out)
    experts = w_control.shape[1]
    columns = experts * QUEUE
    chosen = lax.broadcasted_iota(jnp.int32, (experts, columns), 1) // QUEUE
    chosen = (chosen ^ place[0]) == lax.broadcasted_iota(jnp.int32, (experts, columns), 0)
    control = dot(w_control, chosen.astype(BF)).astype(BF)
    cotangents = exchange(pack_rows(place, grad_output, slots), "seq")

    forwards, members = [], []
    for chunk in range(chunks):
        saved, second = forward_part(
            chunk, place, lengths, tokens, gain_first, w_parts, o_parts, gain_second, slots
        )
        forwards.append(saved)
        members.append(exchange(second, "seq"))
    mixings, answers, kept = [], [], []
    for chunk in range(chunks):
        mixing, messages = mixing_part(chunk, control, members[chunk], cotangents)
        mixings.append(mixing)
        replies, saved = expert_part(
            chunk, exchange(messages, "seq"), w_expand, b_expand, w_reduce, b_reduce
        )
        kept.append(saved)
        answers.append(exchange(replies, "seq"))
    backs, mergeds, controls = [], [], []
    for chunk in range(chunks):
        back, merged, grad_control = unmix_part(
            chunk, place, control, mixings[chunk], members[chunk], cotangents, answers[chunk]
        )
        backs.append(exchange(back, "seq"))
        mergeds.append(merged)
        controls.append(grad_control)

    own_e, other_e, own_r, other_r, bias_e, bias_r = expert_weights(place, kept)
    add_low = lambda one, two: (one.astype(F32) + two.astype(F32)).astype(BF)
    own_e = add_low(own_e, partner(other_e, "head", 1))
    own_r = add_low(own_r, partner(other_r, "head", 1))
    own_e = add_low(own_e, partner(own_e, "head", 2))
    own_r = add_low(own_r, partner(own_r, "head", 2))
    grad_expand, grad_reduce = place_weights(
        place, own_e, partner(own_e, "head", 1), own_r, partner(own_r, "head", 1)
    )

    before, gains = None, []
    for chunk in range(chunks):
        normed, qkv, exps, inverse, attended, resid = forwards[chunk]
        grad_tokens, grad_weights, gain_grads = backward_part(
            chunk,
            place,
            backs[chunk],
            resid,
            grad_output,
            gain_second,
            w_parts,
            o_parts,
            (normed, qkv, exps, inverse, attended),
            tokens,
            gain_first,
            before,
        )
        before = (grad_tokens, grad_weights)
        gains.append(gain_grads)

    output = None
    for chunk in range(chunks):
        output = output_part(
            chunk, chunks, place, forwards[chunk][5], exchange(mergeds[chunk], "seq"), output
        )

    pieces = exchange([grad_weights[index] for index in range(len(w_parts))], "head")
    pieces = exchange(split_sum(place, pieces, slots), "seq")
    own = tree_sum([piece.astype(F32) for piece in pieces]).astype(BF)
    pieces = [own] + [partner(own, "seq", index) for index in range(1, slots)]
    grad_query, grad_key, grad_value, grad_w_out = gather_weights(place, pieces, width)

    small = jnp.concatenate([sum(gains)[:2], sum(controls)], axis=0)
    small = tree_sum([small] + [partner(small, "seq", index) for index in range(1, slots)])
    small = jnp.concatenate([small, bias_e.reshape(-1, width), bias_r], axis=0)
    small = tree_sum([small] + [partner(small, "head", index) for index in range(1, len(w_parts))])
    hidden_rows = bias_e.shape[1] // width
    after = 2 + experts
    return (
        output,
        grad_tokens,
        small[0],
        grad_query,
        grad_key,
        grad_value,
        grad_w_out,
        small[1],
        small[2:after].T,
        grad_expand,
        small[after : after + hidden_rows].reshape(1, -1),
        grad_reduce,
        small[after + hidden_rows :],
    )


def solution(mesh):
    in_specs = (
        P(("seq", "head"), None),
        P(),
        P(None, "head"),
        P(None, "head"),
        P(None, "head"),
        P("head", None),
        P(),
        P(),
        P("seq", None, None),
        P("seq", None),
        P("seq", None, None),
        P("seq", None),
        P("seq", None),
        P(("seq", "head"), None),
    )
    out_specs = (
        P(("seq", "head"), None),
        P(("seq", "head"), None),
        P(),
        P(None, "head"),
        P(None, "head"),
        P(None, "head"),
        P("head", None),
        P(),
        P(),
        P("seq", None, None),
        P("seq", None),
        P("seq", None, None),
        P("seq", None),
    )
    return jax.shard_map(body, mesh=mesh, in_specs=in_specs, out_specs=out_specs, check_vma=False)
```

```python
import functools
import jax
import jax.numpy as jnp
from jax import lax
from jax.sharding import PartitionSpec as P
from jax.experimental import pallas as pl
from jax.experimental.pallas import tpu as pltpu

HEAD_DIM = 64
GROUP = 32
LONG = 1024
TILE = 256
QUEUE = 32
EPSILON = 1e-05
MASKED = -1000000000.0
BF = jnp.bfloat16
F32 = jnp.float32
ROWS_BY_ROWS = (((0,), (0,)), ((), ()))
COLS_BY_COLS = (((1,), (1,)), ((), ()))
VMEM_LIMIT = 62 * 1024 * 1024


def dot(left, right):
    return jnp.dot(left, right, preferred_element_type=F32)


def dot_rows(left, right):
    return lax.dot_general(left, right, ROWS_BY_ROWS, preferred_element_type=F32)


def dot_cols(left, right):
    return lax.dot_general(left, right, COLS_BY_COLS, preferred_element_type=F32)


def normalize(matrix):
    centre = jnp.mean(matrix, axis=1, keepdims=True)
    shifted = matrix - centre
    scaling = lax.rsqrt(jnp.mean(shifted * shifted, axis=1, keepdims=True) + EPSILON)
    return shifted * scaling, scaling


def normalize_back(grad_norm, gain, unit_rows, scaling):
    inner_grad = grad_norm * gain
    centred = (
        inner_grad
        - jnp.mean(inner_grad, axis=1, keepdims=True)
        - unit_rows * jnp.mean(inner_grad * unit_rows, axis=1, keepdims=True)
    )
    return scaling * centred, jnp.sum(grad_norm * unit_rows, axis=0, keepdims=True)


def whole(*shape):
    return pl.BlockSpec(shape, lambda *_: (0,) * len(shape))


def scalars():
    return pl.BlockSpec(memory_space=pltpu.SMEM)


def call(kernel, name, grid, in_specs, out_specs, out_shape, scratch=(), cost=(0, 0, 0), aliases=None):
    return pl.pallas_call(
        kernel,
        grid=grid,
        in_specs=in_specs,
        out_specs=out_specs,
        out_shape=out_shape,
        scratch_shapes=list(scratch),
        input_output_aliases=aliases or {},
        cost_estimate=pl.CostEstimate(
            flops=int(cost[0]), bytes_accessed=int(cost[1]), transcendentals=int(cost[2])
        ),
        compiler_params=pltpu.CompilerParams(vmem_limit_bytes=VMEM_LIMIT),
        name=name,
    )


def shape(dims, dtype):
    return jax.ShapeDtypeStruct(dims, dtype)


def tile_slot(row_tile, col_tile):
    return row_tile * (row_tile + 1) // 2 + col_tile


def halves(dtype):
    lane = lax.broadcasted_iota(jnp.int32, (1, 2 * HEAD_DIM), 1)
    first = (lane < HEAD_DIM).astype(F32)
    return first.astype(dtype), (1.0 - first).astype(dtype)


def load_weights(step, order, parts, w_now, o_now):
    width = w_now.shape[0] if w_now is not None else o_now.shape[1]
    for index, part in enumerate(parts):

        @pl.when(step == order(index))
        def _(part=part):
            cut = part.shape[1]
            if w_now is not None:
                for block in range(3):
                    w_now[:, block * cut : (block + 1) * cut] = part[block * width : (block + 1) * width]
            if o_now is not None:
                for block in range(width // cut):
                    begin = 3 * width + block * cut
                    o_now[:, block * cut : (block + 1) * cut] = part[begin : begin + cut]


def forward_kernel(pairs, chunk, chunks, *refs):
    place, lengths, tokens, gain_first = refs[:4]
    parts = refs[4 : 4 + pairs]
    gain_second = refs[4 + pairs]
    normed, qkv_out, exps, inverse, attended, resid, second = refs[5 + pairs : 12 + pairs]
    w_now, bias, attended_all = refs[12 + pairs :]
    step = pl.program_id(0)
    width = tokens.shape[1]
    pair_width = attended.shape[2]
    tiles = LONG // TILE

    @pl.when(step == 0)
    def _():
        unit, _ = normalize(tokens[...].astype(F32))
        normed[...] = (unit * gain_first[...]).astype(BF)
        base = 4 * (place[1] * chunks + chunk)
        first = lengths[0, base]
        second_bound = first + lengths[0, base + 1]
        third = second_bound + lengths[0, base + 2]
        for row_tile in range(tiles):
            row = lax.broadcasted_iota(jnp.int32, (TILE, 1), 0) + row_tile * TILE
            begin = jnp.where(row >= first, first, 0)
            begin = jnp.where(row >= second_bound, second_bound, begin)
            begin = jnp.where(row >= third, third, begin)
            col = lax.broadcasted_iota(jnp.int32, (TILE, LONG), 1)
            allowed = (col <= row) & (col >= begin)
            bias[pl.ds(row_tile * TILE, TILE), :] = jnp.where(allowed, 0.0, MASKED)

    load_weights(step, lambda index: index, parts, w_now, None)
    qkv = dot(normed[...], w_now[...]).astype(BF)
    qkv_out[0] = qkv
    queries = qkv[:, :pair_width] * BF(HEAD_DIM**-0.5)
    key_rows = qkv[:, pair_width : 2 * pair_width]
    value_rows = qkv[:, 2 * pair_width :]
    low_half, high_half = halves(BF)
    is_low = lax.broadcasted_iota(jnp.int32, (TILE, pair_width), 1) < HEAD_DIM
    masks = ((low_half, high_half), (high_half, low_half))
    head_queries = [queries * own for own, other in masks]
    head_values = [value_rows * own + other for own, other in masks]
    for row_tile in range(tiles):
        begin, extent = row_tile * TILE, (row_tile + 1) * TILE
        raw = []
        for head in range(2):
            scores = dot_cols(head_queries[head][begin:extent], key_rows[:extent])
            scores = scores + bias[begin:extent, :extent]
            highest = jnp.max(scores, axis=1, keepdims=True)
            powers = jnp.exp(scores - highest).astype(BF)
            for col_tile in range(row_tile + 1):
                exps[0, head, tile_slot(row_tile, col_tile)] = powers[
                    :, col_tile * TILE : (col_tile + 1) * TILE
                ]
            raw.append(dot(powers, head_values[head][:extent]))
        totals = jnp.where(
            is_low, pltpu.roll(raw[0], HEAD_DIM, 1), pltpu.roll(raw[1], HEAD_DIM, 1)
        )
        inverted = 1.0 / totals
        inverse[0, begin:extent] = inverted
        attended_tile = (jnp.where(is_low, raw[0], raw[1]) * inverted).astype(BF)
        attended[0, begin:extent] = attended_tile
        attended_all[step, begin:extent] = attended_tile

    @pl.when(step == pairs - 1)
    def _():
        rows = jnp.concatenate([attended_all[index] for index in range(pairs)], axis=1)
        blocks = width // pair_width
        weights = jnp.concatenate(
            [
                jnp.concatenate(
                    [
                        part[3 * width + block * pair_width : 3 * width + (block + 1) * pair_width]
                        for block in range(blocks)
                    ],
                    axis=1,
                )
                for part in parts
            ],
            axis=0,
        )
        total = tokens[...].astype(F32) + dot(rows, weights)
        resid[...] = total
        unit, _ = normalize(total)
        second[...] = (unit * gain_second[...]).astype(BF)


def forward_part(chunk, place, lengths, tokens, gain_first, parts, gain_second):
    rows, width = tokens.shape
    pairs = len(parts)
    packed, pair_width = parts[0].shape
    triple = 3 * pair_width
    kept = LONG // TILE * (LONG // TILE + 1) // 2
    per_pair = lambda *dims: pl.BlockSpec((1,) + dims, lambda i: (i,) + (0,) * len(dims))
    return call(
        functools.partial(forward_kernel, pairs, chunk, rows // LONG),
        f"forward_{chunk}",
        (pairs,),
        [scalars(), scalars(), pl.BlockSpec((LONG, width), lambda i: (chunk, 0)), whole(1, width)]
        + [whole(packed, pair_width)] * pairs
        + [whole(1, width)],
        [
            whole(LONG, width),
            per_pair(LONG, triple),
            per_pair(2, kept, TILE, TILE),
            per_pair(LONG, pair_width),
            per_pair(LONG, pair_width),
            whole(LONG, width),
            whole(LONG, width),
        ],
        [
            shape((LONG, width), BF),
            shape((pairs, LONG, triple), BF),
            shape((pairs, 2, kept, TILE, TILE), BF),
            shape((pairs, LONG, pair_width), F32),
            shape((pairs, LONG, pair_width), BF),
            shape((LONG, width), F32),
            shape((LONG, width), BF),
        ],
        [
            pltpu.VMEM((width, triple), BF),
            pltpu.VMEM((LONG, LONG), F32),
            pltpu.VMEM((pairs, LONG, pair_width), BF),
        ],
        (10e9, 25e6, 5e6),
    )(place, lengths, tokens, gain_first, *parts, gain_second)


def pack_kernel(slots, chunks, rows, out):
    share = LONG // slots
    for chunk in range(chunks):
        for index in range(slots):
            begin = chunk * LONG + index * share
            out[index, chunk] = rows[begin : begin + share, :]


def pack_rows(rows, slots):
    total, width = rows.shape
    chunks, share = total // LONG, LONG // slots
    return call(
        functools.partial(pack_kernel, slots, chunks),
        "pack_cotangent",
        (1,),
        [whole(total, width)],
        whole(slots, chunks, share, width),
        shape((slots, chunks, share, width), BF),
        cost=(0, 4 * total * width, 0),
    )(rows)


def pack_weights_kernel(query, key, value, out, packed):
    width, cut = query.shape
    for index, part in enumerate((query, key, value)):
        packed[index * width : (index + 1) * width] = part[...]
    for index in range(width // cut):
        begin = 3 * width + index * cut
        packed[begin : begin + cut] = out[:, index * cut : (index + 1) * cut]


def pack_weights(query, key, value, out):
    width, cut = query.shape
    return call(
        pack_weights_kernel,
        "pack_weights",
        (1,),
        [whole(width, cut)] * 3 + [whole(cut, width)],
        whole(4 * width, cut),
        shape((4 * width, cut), BF),
        cost=(0, 16 * width * cut, 0),
    )(query, key, value, out)


def group_mask(slots, columns):
    share = LONG // slots
    stride = share // QUEUE
    row = lax.broadcasted_iota(jnp.int32, (LONG, columns), 0)
    col = lax.broadcasted_iota(jnp.int32, (LONG, columns), 1)
    return ((row % share) // stride) == (col % QUEUE)


def mixing_kernel(slots, control, members, cotangents, mixing_out, messages):
    width, columns = control.shape
    rows = members[...]
    grads = cotangents[...].reshape(LONG, width)
    logits = jnp.where(group_mask(slots, columns), dot(rows, control[...]), -1e30)
    powers = jnp.exp(logits - jnp.max(logits, axis=0, keepdims=True))
    mixing = powers / jnp.sum(powers, axis=0, keepdims=True)
    mixing_out[...] = mixing
    low = mixing.astype(BF)
    mixed = dot_rows(low, rows).astype(BF)
    grad_out = dot_rows(low, grads).astype(BF)
    for index in range(slots):
        part = slice(index * QUEUE, (index + 1) * QUEUE)
        messages[index, 0, :QUEUE] = mixed[part]
        messages[index, 0, QUEUE:] = grad_out[part]


def chunk_block(slots, rows, width, chunk):
    return pl.BlockSpec((slots, 1, rows, width), lambda i: (0, chunk, 0, 0))


def mixing_part(chunk, control, members, cotangents, previous):
    slots, chunks, share, _ = cotangents.shape
    width, columns = control.shape
    kernel = functools.partial(mixing_kernel, slots)
    ins = [control, members, cotangents]
    specs = [whole(width, columns), whole(LONG, width), chunk_block(slots, share, width, chunk)]
    aliases = {}
    if previous is not None:
        aliases = {len(ins): 1}
        kernel = without_previous(kernel, len(ins))
        ins.append(previous)
        specs.append(pl.BlockSpec(memory_space=pl.ANY))
    return call(
        kernel,
        f"mixing_{chunk}",
        (1,),
        specs,
        [whole(LONG, columns), chunk_block(slots, 2 * QUEUE, width, chunk)],
        [shape((LONG, columns), F32), shape((slots, chunks, 2 * QUEUE, width), BF)],
        (),
        (6 * LONG * columns * width, 4e6, LONG * columns),
        aliases,
    )(*ins)


def expert_kernel(slots, messages, w_expand, b_expand, w_reduce, b_reduce, *refs):
    answers, taken, grads, activated_out, grad_pre_out, out_sum, mixed_sum = refs
    step = pl.program_id(0)

    @pl.when(step == 0)
    def _():
        for index in range(slots):
            begin = 2 * QUEUE * index
            part = slice(index * QUEUE, (index + 1) * QUEUE)
            taken[part] = messages[begin : begin + QUEUE]
            grads[part] = messages[begin + QUEUE : begin + 2 * QUEUE]
        out_sum[...] = jnp.zeros_like(out_sum)
        mixed_sum[...] = jnp.zeros_like(mixed_sum)

    pre = dot(taken[...], w_expand[0]) + b_expand[...]
    slope = 0.7978845608028654
    square = pre * pre
    bend = jnp.tanh(slope * (pre + 0.044715 * (pre * square)))
    half = 0.5 * (1.0 + bend)
    activated = (pre * half).astype(BF)
    activated_out[...] = activated
    out_sum[...] += dot(activated, w_reduce[0])
    derivative = half + (0.5 * slope) * pre * (1.0 - bend * bend) * (1.0 + 0.134145 * square)
    grad_pre = (dot_cols(grads[...], w_reduce[0]) * derivative).astype(BF)
    grad_pre_out[...] = grad_pre
    mixed_sum[...] += dot_cols(grad_pre, w_expand[0])

    @pl.when(step == pl.num_programs(0) - 1)
    def _():
        for index in range(slots):
            begin = 2 * QUEUE * index
            part = slice(index * QUEUE, (index + 1) * QUEUE)
            answers[begin : begin + QUEUE] = (out_sum[part] + b_reduce[...]).astype(BF)
            answers[begin + QUEUE : begin + 2 * QUEUE] = mixed_sum[part].astype(BF)


def expert_part(messages, w_expand, b_expand, w_reduce, b_reduce):
    _, width, hidden = w_expand.shape
    count = messages.shape[0] // 2
    slots = count // QUEUE
    cut = min(512, hidden)
    outs = call(
        functools.partial(expert_kernel, slots),
        "expert",
        (hidden // cut,),
        [
            whole(2 * count, width),
            pl.BlockSpec((1, width, cut), lambda i: (0, 0, i)),
            pl.BlockSpec((1, cut), lambda i: (0, i)),
            pl.BlockSpec((1, cut, width), lambda i: (0, i, 0)),
            whole(1, width),
        ],
        [
            whole(2 * count, width),
            whole(count, width),
            whole(count, width),
            pl.BlockSpec((count, cut), lambda i: (0, i)),
            pl.BlockSpec((count, cut), lambda i: (0, i)),
        ],
        [shape((2 * count, width), BF)]
        + [shape((count, width), BF)] * 2
        + [shape((count, hidden), BF)] * 2,
        [pltpu.VMEM((count, width), F32), pltpu.VMEM((count, width), F32)],
        (8 * count * width * hidden, 8e6, count * hidden),
    )(messages, w_expand, b_expand, w_reduce, b_reduce)
    return outs[0], outs[1:]


def expert_weights_kernel(chunks, place, *refs):
    taken = refs[:chunks]
    grads = refs[chunks : 2 * chunks]
    activated = refs[2 * chunks : 3 * chunks]
    grad_pre = refs[3 * chunks : 4 * chunks]
    own, other, bias_e, bias_r, full_e, full_r = refs[4 * chunks :]
    join = lambda parts: jnp.concatenate([part[...] for part in parts], axis=0)
    pre = join(grad_pre)
    cotangent = join(grads)
    full_e[...] = dot_rows(join(taken), pre).astype(BF)
    full_r[...] = dot_rows(join(activated), cotangent).astype(BF)
    bias_e[...] = jnp.sum(pre.astype(F32), axis=0, keepdims=True)
    bias_r[...] = jnp.sum(cotangent.astype(F32), axis=0, keepdims=True)
    begin = 0
    for full in (full_e, full_r):
        cut = full.shape[0] // 2
        for out, side in ((own, place[1] % 2), (other, 1 - place[1] % 2)):
            out[begin : begin + cut] = full[pl.ds(pl.multiple_of(side * cut, cut), cut), :]
        begin += cut


def expert_weights(place, saved):
    chunks = len(saved)
    taken, grads, activated, grad_pre = zip(*saved)
    count, width = taken[0].shape
    hidden = activated[0].shape[1]
    cut = width
    steps = hidden // cut
    wide = lambda rows: pl.BlockSpec((rows, cut), lambda i: (0, i))
    tall = pl.BlockSpec((cut, width), lambda i: (i, 0))
    return call(
        functools.partial(expert_weights_kernel, chunks),
        "expert_weights",
        (steps,),
        [scalars()] + [whole(count, width)] * (2 * chunks) + [wide(count)] * (2 * chunks),
        [tall, tall, wide(1), whole(1, width)],
        [shape((hidden, width), BF)] * 2 + [shape((1, hidden), F32), shape((1, width), F32)],
        [pltpu.VMEM((width, cut), BF), pltpu.VMEM((cut, width), BF)],
        (4 * chunks * count * width * hidden, 9e6, 0),
    )(place, *taken, *grads, *activated, *grad_pre)


def place_weights_kernel(place, own, own_across, other, other_across, out_e, out_r):
    begin = 0
    for out in (out_e, out_r):
        cut = out.shape[1] // 2
        part = slice(begin, begin + cut)
        for one, two, side in (
            (own, own_across, place[1] % 2),
            (other, other_across, 1 - place[1] % 2),
        ):
            total = one[part].astype(F32) + two[part].astype(F32)
            out[0, pl.ds(pl.multiple_of(side * cut, cut), cut), :] = total
        begin += cut


def place_weights(place, *parts):
    hidden, width = parts[0].shape
    cut = width
    tall = pl.BlockSpec((cut, width), lambda i: (i, 0))
    return call(
        place_weights_kernel,
        "place_expert_weights",
        (hidden // cut,),
        [scalars()] + [tall] * len(parts),
        [
            pl.BlockSpec((1, width, cut), lambda i: (0, 0, i)),
            pl.BlockSpec((1, cut, width), lambda i: (0, i, 0)),
        ],
        [shape((1, width, hidden), F32), shape((1, hidden, width), F32)],
        cost=(0, 16 * width * hidden, 0),
    )(place, *parts)


def unmix_kernel(slots, control, mixing_ref, members, cotangents, answers, back, merged, control_out):
    rows = members[...]
    grads = cotangents[...].reshape(rows.shape)
    pick = lambda part: jnp.concatenate([answers[index, 0, part] for index in range(slots)], axis=0)
    expert_out, grad_mixed = pick(slice(0, QUEUE)), pick(slice(QUEUE, 2 * QUEUE))
    mixing = mixing_ref[...]
    low = mixing.astype(BF)
    grad_mixing = dot_cols(grads, expert_out) + dot_cols(rows, grad_mixed)
    weighted = mixing * grad_mixing
    grad_logits = weighted - mixing * jnp.sum(weighted, axis=0, keepdims=True)
    grad_logits = grad_logits.astype(BF)
    back[...] = (dot(low, grad_mixed) + dot_cols(grad_logits, control[...])).astype(BF)
    merged[...] = dot(low, expert_out).astype(BF).reshape(merged.shape)
    grad_control = dot_rows(grad_logits, rows)
    for index in range(slots):
        control_out[index : index + 1, :] = jnp.sum(
            grad_control[index * QUEUE : (index + 1) * QUEUE], axis=0, keepdims=True
        )


def without_previous(kernel, position):
    def inner(*refs):
        return kernel(*refs[:position], *refs[position + 1 :])

    return inner


def unmix_part(chunk, control, mixing, members, cotangents, answers, previous):
    slots, chunks, _, width = answers.shape
    columns = control.shape[1]
    share = LONG // slots
    kernel = functools.partial(unmix_kernel, slots)
    ins = [control, mixing, members, cotangents, answers]
    specs = [
        whole(width, columns),
        whole(LONG, columns),
        whole(LONG, width),
        chunk_block(slots, share, width, chunk),
        chunk_block(slots, 2 * QUEUE, width, chunk),
    ]
    aliases = {}
    if previous is not None:
        aliases = {len(ins): 1}
        kernel = without_previous(kernel, len(ins))
        ins.append(previous)
        specs.append(pl.BlockSpec(memory_space=pl.ANY))
    return call(
        kernel,
        f"unmix_{chunk}",
        (1,),
        specs,
        [whole(LONG, width), chunk_block(slots, share, width, chunk), whole(slots, width)],
        [
            shape((LONG, width), BF),
            shape((slots, chunks, share, width), BF),
            shape((slots, width), F32),
        ],
        (),
        (12 * LONG * columns * width, 6e6, 0),
        aliases,
    )(*ins)


def output_kernel(chunks, *refs):
    merged, out = refs[chunks:]
    for chunk in range(chunks):
        rows = merged[:, chunk].reshape(LONG, out.shape[1]).astype(F32)
        out[chunk * LONG : (chunk + 1) * LONG] = (refs[chunk][...] + rows).astype(BF)


def output_part(resids, merged):
    slots, chunks, share, width = merged.shape
    return call(
        functools.partial(output_kernel, chunks),
        "output",
        (1,),
        [whole(LONG, width)] * chunks + [whole(slots, chunks, share, width)],
        whole(chunks * LONG, width),
        shape((chunks * LONG, width), BF),
        cost=(0, 8e6, 0),
    )(*resids, merged)


def backward_kernel(pairs, begins, later, *refs):
    refs = list(refs)
    take = lambda count: [refs.pop(0) for _ in range(count)]
    if begins:
        back, resid, grad_output, gain_second = take(4)
    else:
        (resid_low,) = take(1)
    parts = take(len(pairs))
    normed, qkv, exps, inverse, attended = take(5)
    weights_before = take(len(pairs)) if later else None
    weights_out = take(len(pairs))
    (grads_out,) = take(1)
    if begins:
        gains_out, grad_resid, resid_low = take(3)
    normed_turned, w_now, o_now, queries_sum, keys_turned, values_turned = take(6)
    step = pl.program_id(0)
    pair_width = attended.shape[2]
    tiles = LONG // TILE

    @pl.when(step == 0)
    def _():
        normed_turned[...] = normed[...].T
        if begins:
            unit, scaling = normalize(resid[...])
            through, gain_grad = normalize_back(
                back[...].astype(F32), gain_second[...], unit, scaling
            )
            gains_out[...] = gain_grad
            total = grad_output[...].astype(F32) + through
            grad_resid[...] = total
            resid_low[...] = total.astype(BF)

    load_weights(step, lambda index: index, parts, None, o_now)
    low = resid_low[...]
    grad_attended = dot_cols(low, o_now[...]).astype(BF)
    grad_out_weights = dot_rows(attended[0], low)
    wide = grad_attended.astype(F32)
    inverted = inverse[0]
    scaled = wide * inverted
    products = scaled * attended[0].astype(F32)
    scaled = scaled.astype(BF)
    low_half, high_half = halves(BF)
    low_wide, high_wide = halves(F32)
    queries = qkv[0, :, :pair_width] * BF(HEAD_DIM**-0.5)
    key_rows = qkv[0, :, pair_width : 2 * pair_width]
    value_rows = qkv[0, :, 2 * pair_width :]
    scaled_keys = key_rows * BF(HEAD_DIM**-0.5)
    queries_sum[...] = jnp.zeros_like(queries_sum)
    keys_turned[...] = jnp.zeros_like(keys_turned)
    values_turned[...] = jnp.zeros_like(values_turned)
    for head, (half, half_wide) in enumerate(((low_half, low_wide), (high_half, high_wide))):
        head_grads = scaled * half
        head_queries = queries * half
        head_keys = scaled_keys * half
        deltas = jnp.sum(products * half_wide, axis=1, keepdims=True)
        for row_tile in range(tiles):
            begin, extent = row_tile * TILE, (row_tile + 1) * TILE
            powers = jnp.concatenate(
                [exps[0, head, tile_slot(row_tile, col_tile)] for col_tile in range(row_tile + 1)],
                axis=1,
            )
            grad_probs = dot_cols(head_grads[begin:extent], value_rows[:extent])
            grad_scores = (powers.astype(F32) * (grad_probs - deltas[begin:extent])).astype(BF)
            queries_sum[begin:extent] += dot(grad_scores, head_keys[:extent])
            keys_turned[:, :extent] += dot_rows(head_queries[begin:extent], grad_scores)
            values_turned[:, :extent] += dot_rows(head_grads[begin:extent], powers)
    grads = jnp.concatenate(
        [queries_sum[...].astype(BF), keys_turned[...].T.astype(BF), values_turned[...].T.astype(BF)],
        axis=1,
    )
    grads_out[0] = grads
    grad_weights = dot(normed_turned[...], grads)
    width = normed.shape[1]
    blocks = [grad_weights[:, index * pair_width : (index + 1) * pair_width] for index in range(3)]
    blocks += [
        grad_out_weights[:, index * pair_width : (index + 1) * pair_width]
        for index in range(width // pair_width)
    ]
    for index, out in enumerate(weights_out):

        @pl.when(step == index)
        def _(index=index, out=out):
            begin = 0
            for block in blocks:
                extent = begin + block.shape[0]
                if later:
                    block = block + weights_before[index][begin:extent]
                out[begin:extent] = block.astype(out.dtype)
                begin = extent


def backward_part(chunk, pairs, start, low, parts, saved, before, last):
    exps = saved[2]
    width = saved[0].shape[1]
    packed, pair_width = parts[0].shape
    triple = 3 * pair_width
    kept = exps.shape[2]
    first = pairs[0]
    per_pair = lambda *dims: pl.BlockSpec((1,) + dims, lambda i: (first - i,) + (0,) * len(dims))
    rows = whole(LONG, width)
    begins, later = start is not None, before is not None
    if begins:
        ins = [*start]
        specs = [rows, rows, pl.BlockSpec((LONG, width), lambda i: (chunk, 0)), whole(1, width)]
    else:
        ins, specs = [low], [rows]
    ins += [parts[pair] for pair in pairs] + list(saved)
    specs += [whole(packed, pair_width)] * len(pairs)
    specs += [
        rows,
        per_pair(LONG, triple),
        per_pair(2, kept, TILE, TILE),
        per_pair(LONG, pair_width),
        per_pair(LONG, pair_width),
    ]
    if later:
        ins += [before[pair] for pair in pairs]
        specs += [whole(packed, pair_width)] * len(pairs)
    out_specs = [whole(packed, pair_width)] * len(pairs)
    outs = [shape((packed, pair_width), BF if last else F32)] * len(pairs)
    out_specs.append(pl.BlockSpec((1, LONG, triple), lambda i: (i, 0, 0)))
    outs.append(shape((len(pairs), LONG, triple), BF))
    if begins:
        out_specs += [whole(1, width), rows, rows]
        outs += [shape((1, width), F32), shape((LONG, width), F32), shape((LONG, width), BF)]
    results = call(
        functools.partial(backward_kernel, pairs, begins, later),
        f"backward_{chunk}_{first}",
        (len(pairs),),
        specs,
        out_specs,
        outs,
        [
            pltpu.VMEM((width, LONG), BF),
            pltpu.VMEM((width, triple), BF),
            pltpu.VMEM((pair_width, width), BF),
            pltpu.VMEM((LONG, pair_width), F32),
            pltpu.VMEM((pair_width, LONG), F32),
            pltpu.VMEM((pair_width, LONG), F32),
        ],
        (6e9 * len(pairs), 6e6 * len(pairs), 0),
    )(*ins)
    count = len(pairs)
    return dict(zip(pairs, results[:count])), results[count], results[count + 1 :]


def finish_kernel(groups, *refs):
    chunks = len(groups)
    refs = list(refs)
    take = lambda count: [refs.pop(0) for _ in range(count)]
    tokens, gain_first = take(2)
    parts = take(sum(len(group) for group in groups[0]))
    grads = [take(len(groups[chunk])) for chunk in range(chunks)]
    resids = take(chunks)
    grad_tokens, gain_out, weights = refs
    step = pl.program_id(0)
    width = tokens.shape[1]
    pairs, triple = len(parts), weights.shape[1] // len(parts)

    @pl.when(step == 0)
    def _():
        gain_out[...] = jnp.zeros_like(gain_out)
        for pair, part in enumerate(parts):
            cut = triple // 3
            for block in range(3):
                begin = pair * triple + block * cut
                weights[:, begin : begin + cut] = part[block * width : (block + 1) * width]

    for chunk in range(chunks):

        @pl.when(step == chunk)
        def _(chunk=chunk):
            columns = {}
            for group, ref in zip(groups[chunk], grads[chunk]):
                for index, pair in enumerate(group):
                    columns[pair] = ref[index]
            joined = jnp.concatenate([columns[pair] for pair in range(pairs)], axis=1)
            unit, scaling = normalize(tokens[...].astype(F32))
            through, gain_grad = normalize_back(
                dot_cols(joined, weights[...]), gain_first[...], unit, scaling
            )
            gain_out[...] += gain_grad
            grad_tokens[...] = resids[chunk][...] + through


def finish_part(tokens, gain_first, parts, groups, grads, resids):
    total, width = tokens.shape
    chunks = total // LONG
    packed, pair_width = parts[0].shape
    rows = pl.BlockSpec((LONG, width), lambda i: (i, 0))
    flat = [ref for chunk in grads for ref in chunk]
    return call(
        functools.partial(finish_kernel, groups),
        "finish",
        (chunks,),
        [rows, whole(1, width)]
        + [whole(packed, pair_width)] * len(parts)
        + [whole(*ref.shape) for ref in flat]
        + [whole(LONG, width)] * chunks,
        [rows, whole(1, width)],
        [shape((total, width), F32), shape((1, width), F32)],
        [pltpu.VMEM((width, 3 * pair_width * len(parts)), BF)],
        (2 * total * width * 3 * pair_width * len(parts), 2e7, 0),
    )(tokens, gain_first, *parts, *flat, *resids)


def tail_pack_kernel(*refs):
    total = refs[0][...].astype(F32)
    for part in refs[1:-1]:
        total = total + part[...].astype(F32)
    refs[-1][...] = total.astype(BF)


def tail_pack(parts):
    rows, cut = parts[0].shape
    return call(
        tail_pack_kernel,
        "tail_pack",
        (1,),
        [whole(rows, cut)] * len(parts),
        whole(rows, cut),
        shape((rows, cut), BF),
        cost=(0, 3e6, 0),
    )(*parts)


def tail_sum_kernel(slots, pieces, small, out):
    share, cut = pieces.shape[1:]
    total = pieces[0].astype(F32)
    for index in range(1, slots):
        total = total + pieces[index].astype(F32)
    total = total.astype(BF)
    packed = jnp.concatenate(
        [small[:, begin : begin + cut] for begin in range(0, small.shape[1], cut)], axis=0
    ).astype(BF)
    for index in range(slots):
        out[index, :share] = total
        out[index, share:] = packed


def tail_sum(pieces, small):
    slots, share, cut = pieces.shape
    count, width = small.shape
    rows = share + count * width // cut
    return call(
        functools.partial(tail_sum_kernel, slots),
        "tail_sum",
        (1,),
        [whole(slots, share, cut), whole(count, width)],
        whole(slots, rows, cut),
        shape((slots, rows, cut), BF),
        cost=(0, 2e6, 0),
    )(pieces, small)


def gather_kernel(slots, share, pieces, *refs):
    outs, gain_first, gain_second, control, total = refs[:4], refs[4], refs[5], refs[6], refs[7]
    for index in range(slots):
        total[index * share : (index + 1) * share] = pieces[index, :share].astype(F32)
    cut = total.shape[1]
    begin = 0
    for out in outs[:3]:
        out[...] = total[begin : begin + out.shape[0]]
        begin += out.shape[0]
    last = outs[3]
    blocks = last.shape[1] // cut
    for index in range(blocks):
        last[:, index * cut : (index + 1) * cut] = total[begin : begin + last.shape[0]]
        begin += last.shape[0]
    small = pieces[0, share:].astype(F32)
    for index in range(1, slots):
        small = small + pieces[index, share:].astype(F32)
    count = small.shape[0] // blocks
    small = jnp.concatenate(
        [small[index * count : (index + 1) * count] for index in range(blocks)], axis=1
    )
    experts = control.shape[1]
    gain_first[...] = small[experts : experts + 1]
    gain_second[...] = small[experts + 1 : experts + 2]
    control[...] = small[:experts].T


def gather_weights(pieces, share, width, experts):
    slots, _, cut = pieces.shape
    outs = [(width, cut)] * 3 + [(cut, width), (1, width), (1, width), (width, experts)]
    return call(
        functools.partial(gather_kernel, slots, share),
        "gather_weights",
        (1,),
        [whole(*pieces.shape)],
        [whole(*dims) for dims in outs],
        [shape(dims, F32) for dims in outs],
        [pltpu.VMEM((share * slots, cut), F32)],
        (0, 3e6, 0),
    )(pieces)


def partner(value, axis, offset):
    count = lax.axis_size(axis)
    return lax.ppermute(value, axis, [(index, index ^ offset) for index in range(count)])


def exchange(value, axis):
    return lax.all_to_all(value, axis, 0, 0, tiled=True)


def tree_sum(parts):
    while len(parts) > 1:
        parts = [parts[index] + parts[index + 1] for index in range(0, len(parts), 2)]
    return parts[0]


def gather_head(part):
    sibling = partner(part, "head", 1)
    across = partner(part, "head", 2)
    return [part, sibling, across, partner(across, "head", 1)]


def add_low(*parts):
    return sum(part.astype(F32) for part in parts).astype(BF)


def after(value, *earlier):
    return lax.optimization_barrier((value, *earlier))[0]


def body(
    tokens,
    gain_first,
    w_query,
    w_key,
    w_value,
    w_out,
    gain_second,
    w_control,
    w_expand,
    b_expand,
    w_reduce,
    b_reduce,
    lengths,
    grad_output,
):
    rows_local, width = tokens.shape
    pair_width = w_query.shape[1]
    slots = lax.axis_size("seq")
    chunks = rows_local // LONG
    place = jnp.stack([lax.axis_index("seq"), lax.axis_index("head")]).astype(jnp.int32)
    gain_first = gain_first[None]
    gain_second = gain_second[None]
    parts = gather_head(pack_weights(w_query, w_key, w_value, w_out))
    experts = w_control.shape[1]
    control = jnp.repeat(w_control, QUEUE, axis=1)
    cotangents = exchange(pack_rows(grad_output, slots), "seq")

    forwards, members = [], []
    for chunk in range(chunks):
        *saved, second = forward_part(
            chunk, place, lengths, tokens, gain_first, parts, gain_second
        )
        forwards.append(saved)
        second = after(second, cotangents)
        members.append(exchange(second, "seq"))
    mixings, messages = [], None
    for chunk in range(chunks):
        mixing, messages = mixing_part(
            chunk, control, members[chunk], cotangents, messages
        )
        mixings.append(mixing)
    messages = exchange(messages, "seq")
    replies, kept = expert_part(
        messages.reshape(-1, width), w_expand, b_expand, w_reduce, b_reduce
    )
    answers = exchange(replies.reshape(messages.shape), "seq")
    backs, merged, controls = [], None, []
    for chunk in range(chunks):
        back, merged, grad_control = unmix_part(
            chunk, control, mixings[chunk], members[chunk], cotangents, answers, merged
        )
        backs.append(exchange(back, "seq"))
        controls.append(grad_control)

    own, other, bias_e, bias_r = expert_weights(place, [kept])
    own = add_low(own, partner(other, "head", 1))
    across = partner(own, "head", 2)
    placed = (own, across, partner(own, "head", 1), partner(across, "head", 1))

    pairs = tuple(reversed(range(len(parts))))
    early, late = pairs[: len(pairs) // 2], pairs[len(pairs) // 2 :]
    before, gains, groups, grads, resids = None, [], [], [], []
    for chunk in range(chunks):
        *saved, resid = forwards[chunk]
        back = backs[chunk]
        if chunk == chunks - 1:
            if gains:
                merged = after(merged, gains[-1])
            merged = exchange(merged, "seq")
            back = after(back, across)
            start = (back, resid, grad_output, gain_second)
            first_weights, first_grads, (gain, grad_resid, low) = backward_part(
                chunk, early, start, None, parts, saved, before, True
            )
            pieces = [partner(first_weights[pair], "head", pair) for pair in early]
            second_weights, second_grads, _ = backward_part(
                chunk, late, None, low, parts, saved, before, True
            )
            groups.append((early, late))
            grads.append((first_grads, second_grads))
        else:
            start = (back, resid, grad_output, gain_second)
            before, chunk_grads, (gain, grad_resid, low) = backward_part(
                chunk, pairs, start, None, parts, saved, before, False
            )
            groups.append((pairs,))
            grads.append((chunk_grads,))
        gains.append(gain)
        resids.append(grad_resid)
    resids[-1] = after(resids[-1], *pieces)
    grad_tokens, gain = finish_part(tokens, gain_first, parts, groups, grads, resids)

    pieces += [partner(second_weights[pair], "head", pair) for pair in late if pair]
    packed = tail_pack([second_weights[0]] + pieces)
    packed = after(packed, merged, *placed)
    pieces = exchange(packed, "seq").reshape(slots, -1, pair_width)

    hidden_rows = bias_e.shape[1] // width
    small = [sum(controls), gain, sum(gains), bias_e.reshape(-1, width), bias_r]
    used = experts + 3 + hidden_rows
    small = jnp.concatenate(small + [jnp.zeros((-used % 8, width), F32)], axis=0)
    small = tree_sum([small] + [partner(small, "head", index) for index in range(1, len(parts))])
    sent = -(-(experts + 2) // 8) * 8
    pieces = exchange(tail_sum(pieces, small[:sent]), "seq")
    share = parts[0].shape[0] // slots
    *weights, gain_first, gain_second, control = gather_weights(pieces, share, width, experts)
    grad_query, grad_key, grad_value, grad_w_out = weights
    grad_expand, grad_reduce = place_weights(place, *placed)
    output = output_part([saved[5] for saved in forwards], merged)
    after_gains = experts + 2
    return (
        output,
        grad_tokens,
        gain_first[0],
        grad_query,
        grad_key,
        grad_value,
        grad_w_out,
        gain_second[0],
        control,
        grad_expand,
        small[after_gains : after_gains + hidden_rows].reshape(1, -1),
        grad_reduce,
        small[after_gains + hidden_rows : used],
    )


def solution(mesh):
    in_specs = (
        P(("seq", "head"), None),
        P(),
        P(None, "head"),
        P(None, "head"),
        P(None, "head"),
        P("head", None),
        P(),
        P(),
        P("seq", None, None),
        P("seq", None),
        P("seq", None, None),
        P("seq", None),
        P("seq", None),
        P(("seq", "head"), None),
    )
    out_specs = (
        P(("seq", "head"), None),
        P(("seq", "head"), None),
        P(),
        P(None, "head"),
        P(None, "head"),
        P(None, "head"),
        P("head", None),
        P(),
        P(),
        P("seq", None, None),
        P("seq", None),
        P("seq", None, None),
        P("seq", None),
    )
    return jax.shard_map(body, mesh=mesh, in_specs=in_specs, out_specs=out_specs, check_vma=False)
```

```python
import functools
import jax
import jax.numpy as jnp
from jax import lax
from jax.sharding import PartitionSpec as P
from jax.experimental import pallas as pl
from jax.experimental.pallas import tpu as pltpu

HEAD_DIM = 64
GROUP = 32
LONG = 1024
TILE = 256
QUEUE = 32
EPSILON = 1e-05
MASKED = -1000000000.0
BF = jnp.bfloat16
F32 = jnp.float32
ROWS_BY_ROWS = (((0,), (0,)), ((), ()))
COLS_BY_COLS = (((1,), (1,)), ((), ()))
LARGE = 62 * 1024 * 1024
SMALL = 28 * 1024 * 1024


def dot(left, right):
    return jnp.dot(left, right, preferred_element_type=F32)


def dot_rows(left, right):
    return lax.dot_general(left, right, ROWS_BY_ROWS, preferred_element_type=F32)


def dot_cols(left, right):
    return lax.dot_general(left, right, COLS_BY_COLS, preferred_element_type=F32)


def normalize(matrix):
    centre = jnp.mean(matrix, axis=1, keepdims=True)
    shifted = matrix - centre
    scaling = lax.rsqrt(jnp.mean(shifted * shifted, axis=1, keepdims=True) + EPSILON)
    return shifted * scaling, scaling


def normalize_back(grad_norm, gain, unit_rows, scaling):
    inner_grad = grad_norm * gain
    centred = (
        inner_grad
        - jnp.mean(inner_grad, axis=1, keepdims=True)
        - unit_rows * jnp.mean(inner_grad * unit_rows, axis=1, keepdims=True)
    )
    return scaling * centred, jnp.sum(grad_norm * unit_rows, axis=0, keepdims=True)


def whole(*shape):
    return pl.BlockSpec(shape, lambda *_: (0,) * len(shape))


def scalars():
    return pl.BlockSpec(memory_space=pltpu.SMEM)


def call(kernel, name, grid, in_specs, out_specs, out_shape, scratch=(), cost=(0, 0, 0), aliases=None, limit=SMALL):
    return pl.pallas_call(
        kernel,
        grid=grid,
        in_specs=in_specs,
        out_specs=out_specs,
        out_shape=out_shape,
        scratch_shapes=list(scratch),
        input_output_aliases=aliases or {},
        cost_estimate=pl.CostEstimate(
            flops=int(cost[0]), bytes_accessed=int(cost[1]), transcendentals=int(cost[2])
        ),
        compiler_params=pltpu.CompilerParams(vmem_limit_bytes=limit),
        name=name,
    )


def shape(dims, dtype):
    return jax.ShapeDtypeStruct(dims, dtype)


def tile_slot(row_tile, col_tile):
    return row_tile * (row_tile + 1) // 2 + col_tile


def halves(dtype):
    lane = lax.broadcasted_iota(jnp.int32, (1, 2 * HEAD_DIM), 1)
    first = (lane < HEAD_DIM).astype(F32)
    return first.astype(dtype), (1.0 - first).astype(dtype)


def out_weights(part, width):
    cut = part.shape[1]
    base = part.shape[0] - width
    blocks = [part[base + begin : base + begin + cut] for begin in range(0, width, cut)]
    return jnp.concatenate(blocks, axis=1)


def forward_kernel(pairs, chunk, chunks, *refs):
    place, lengths, tokens, gain_first = refs[:4]
    parts = refs[4 : 4 + pairs]
    gain_second = refs[4 + pairs]
    normed_out, qkv_out, exps, inverse, attended, resid, second = refs[5 + pairs : 12 + pairs]
    normed, weights, bias, attended_all, arrived = refs[12 + pairs :]
    step = pl.program_id(0)
    width = tokens.shape[1]
    pair_width = attended.shape[2]
    fetches = [
        pltpu.make_async_copy(part, weights.at[index], arrived.at[index])
        for index, part in enumerate(parts)
    ]
    tiles = LONG // TILE

    @pl.when(step == 0)
    def _():
        for fetch in fetches:
            fetch.start()
        unit, _ = normalize(tokens[...].astype(F32))
        normed[...] = (unit * gain_first[...]).astype(BF)
        base = 4 * (place[1] * chunks + chunk)
        first = lengths[0, base]
        second_bound = first + lengths[0, base + 1]
        third = second_bound + lengths[0, base + 2]
        for row_tile in range(tiles):
            row = lax.broadcasted_iota(jnp.int32, (TILE, 1), 0) + row_tile * TILE
            begin = jnp.where(row >= first, first, 0)
            begin = jnp.where(row >= second_bound, second_bound, begin)
            begin = jnp.where(row >= third, third, begin)
            col = lax.broadcasted_iota(jnp.int32, (TILE, LONG), 1)
            allowed = (col <= row) & (col >= begin)
            bias[pl.ds(row_tile * TILE, TILE), :] = jnp.where(allowed, 0.0, MASKED)

    for index, fetch in enumerate(fetches):

        @pl.when(step == index)
        def _(fetch=fetch):
            fetch.wait()

    share = LONG // pairs
    normed_out[...] = normed[pl.ds(pl.multiple_of(step * share, share), share), :]
    own = weights[step, : 3 * width]
    own = jnp.concatenate([own[begin : begin + width] for begin in range(0, 3 * width, width)], axis=1)
    qkv = dot(normed[...], own).astype(BF)
    qkv_out[0] = qkv
    queries = qkv[:, :pair_width] * BF(HEAD_DIM**-0.5)
    key_rows = qkv[:, pair_width : 2 * pair_width]
    value_rows = qkv[:, 2 * pair_width :]
    low_half, high_half = halves(BF)
    is_low = lax.broadcasted_iota(jnp.int32, (TILE, pair_width), 1) < HEAD_DIM
    masks = ((low_half, high_half), (high_half, low_half))
    head_queries = [queries * own for own, other in masks]
    head_values = [value_rows * own + other for own, other in masks]
    for row_tile in range(tiles):
        begin, extent = row_tile * TILE, (row_tile + 1) * TILE
        raw = []
        for head in range(2):
            scores = dot_cols(head_queries[head][begin:extent], key_rows[:extent])
            scores = scores + bias[begin:extent, :extent]
            highest = jnp.max(scores, axis=1, keepdims=True)
            powers = jnp.exp(scores - highest).astype(BF)
            for col_tile in range(row_tile + 1):
                exps[0, head, tile_slot(row_tile, col_tile)] = powers[
                    :, col_tile * TILE : (col_tile + 1) * TILE
                ]
            raw.append(dot(powers, head_values[head][:extent]))
        totals = jnp.where(
            is_low, pltpu.roll(raw[0], HEAD_DIM, 1), pltpu.roll(raw[1], HEAD_DIM, 1)
        )
        inverted = 1.0 / totals
        inverse[0, begin:extent] = inverted.astype(BF)
        attended_tile = (jnp.where(is_low, raw[0], raw[1]) * inverted).astype(BF)
        attended[0, begin:extent] = attended_tile
        attended_all[step, begin:extent] = attended_tile

    @pl.when(step == pairs - 1)
    def _():
        rows = jnp.concatenate([attended_all[index] for index in range(pairs)], axis=1)
        blocks = width // pair_width
        own = jnp.concatenate([out_weights(weights[index], width) for index in range(pairs)], axis=0)
        total = tokens[...].astype(F32) + dot(rows, own)
        resid[...] = total.astype(BF)
        unit, _ = normalize(total)
        second[...] = (unit * gain_second[...]).astype(BF)


def forward_part(chunk, place, lengths, tokens, gain_first, parts, gain_second):
    rows, width = tokens.shape
    pairs = len(parts)
    packed, pair_width = parts[0].shape
    triple = 3 * pair_width
    kept = LONG // TILE * (LONG // TILE + 1) // 2
    per_pair = lambda *dims: pl.BlockSpec((1,) + dims, lambda i: (i,) + (0,) * len(dims))
    return call(
        functools.partial(forward_kernel, pairs, chunk, rows // LONG),
        f"forward_{chunk}",
        (pairs,),
        [scalars(), scalars(), pl.BlockSpec((LONG, width), lambda i: (chunk, 0)), whole(1, width)]
        + [pl.BlockSpec(memory_space=pl.ANY)] * pairs
        + [whole(1, width)],
        [
            pl.BlockSpec((LONG // pairs, width), lambda i: (i, 0)),
            per_pair(LONG, triple),
            per_pair(2, kept, TILE, TILE),
            per_pair(LONG, pair_width),
            per_pair(LONG, pair_width),
            whole(LONG, width),
            whole(LONG, width),
        ],
        [
            shape((LONG, width), BF),
            shape((pairs, LONG, triple), BF),
            shape((pairs, 2, kept, TILE, TILE), BF),
            shape((pairs, LONG, pair_width), BF),
            shape((pairs, LONG, pair_width), BF),
            shape((LONG, width), BF),
            shape((LONG, width), BF),
        ],
        [
            pltpu.VMEM((LONG, width), BF),
            pltpu.VMEM((pairs, packed, pair_width), BF),
            pltpu.VMEM((LONG, LONG), F32),
            pltpu.VMEM((pairs, LONG, pair_width), BF),
            pltpu.SemaphoreType.DMA((pairs,)),
        ],
        (10e9, 25e6, 5e6),
        limit=LARGE,
    )(place, lengths, tokens, gain_first, *parts, gain_second)


def pack_kernel(rows, out, arrived):
    slots, chunks, share, _ = out.shape
    copies = []
    for chunk in range(chunks):
        for index in range(slots):
            begin = chunk * LONG + index * share
            copies.append(
                pltpu.make_async_copy(
                    rows.at[pl.ds(begin, share)], out.at[index, chunk], arrived.at[len(copies)]
                )
            )
    for copy in copies:
        copy.start()
    for copy in copies:
        copy.wait()


def pack_rows(rows, slots):
    total, width = rows.shape
    chunks, share = total // LONG, LONG // slots
    return call(
        pack_kernel,
        "pack_cotangent",
        (1,),
        [pl.BlockSpec(memory_space=pl.ANY)],
        pl.BlockSpec(memory_space=pl.ANY),
        shape((slots, chunks, share, width), BF),
        [pltpu.SemaphoreType.DMA((slots * chunks,))],
        (0, 4 * total * width, 0),
    )(rows)


def pack_weights_kernel(query, key, value, out, packed):
    width, cut = query.shape
    for index, part in enumerate((query, key, value)):
        packed[index * width : (index + 1) * width] = part[...]
    for index in range(width // cut):
        begin = 3 * width + index * cut
        packed[begin : begin + cut] = out[:, index * cut : (index + 1) * cut]


def pack_weights(query, key, value, out):
    width, cut = query.shape
    return call(
        pack_weights_kernel,
        "pack_weights",
        (1,),
        [whole(width, cut)] * 3 + [whole(cut, width)],
        whole(4 * width, cut),
        shape((4 * width, cut), BF),
        cost=(0, 16 * width * cut, 0),
    )(query, key, value, out)


def group_mask(slots, columns):
    share = LONG // slots
    stride = share // QUEUE
    row = lax.broadcasted_iota(jnp.int32, (LONG, columns), 0)
    col = lax.broadcasted_iota(jnp.int32, (LONG, columns), 1)
    return ((row % share) // stride) == (col % QUEUE)


def mixing_kernel(slots, control, members, cotangents, mixing_out, messages):
    width, columns = control.shape
    rows = members[...]
    grads = cotangents[...].reshape(LONG, width)
    logits = jnp.where(group_mask(slots, columns), dot(rows, control[...]), -1e30)
    powers = jnp.exp(logits - jnp.max(logits, axis=0, keepdims=True))
    low = (powers / jnp.sum(powers, axis=0, keepdims=True)).astype(BF)
    mixing_out[...] = low
    mixed = dot_rows(low, rows).astype(BF)
    grad_out = dot_rows(low, grads).astype(BF)
    for index in range(slots):
        part = slice(index * QUEUE, (index + 1) * QUEUE)
        messages[index, :QUEUE] = mixed[part]
        messages[index, QUEUE:] = grad_out[part]


def chunk_block(slots, rows, width, chunk):
    return pl.BlockSpec((slots, 1, rows, width), lambda i: (0, chunk, 0, 0))


def mixing_part(chunk, control, members, cotangents):
    slots, chunks, share, _ = cotangents.shape
    width, columns = control.shape
    return call(
        functools.partial(mixing_kernel, slots),
        f"mixing_{chunk}",
        (1,),
        [whole(width, columns), whole(LONG, width), chunk_block(slots, share, width, chunk)],
        [whole(LONG, columns), whole(slots, 2 * QUEUE, width)],
        [shape((LONG, columns), BF), shape((slots, 2 * QUEUE, width), BF)],
        cost=(6 * LONG * columns * width, 4e6, LONG * columns),
    )(control, members, cotangents)


def expert_kernel(slots, messages, w_expand, b_expand, w_reduce, b_reduce, *refs):
    answers, activated_out, grad_pre_out, taken, grads, out_sum, mixed_sum = refs
    step = pl.program_id(0)

    @pl.when(step == 0)
    def _():
        for index in range(slots):
            begin = 2 * QUEUE * index
            part = slice(index * QUEUE, (index + 1) * QUEUE)
            taken[part] = messages[begin : begin + QUEUE]
            grads[part] = messages[begin + QUEUE : begin + 2 * QUEUE]
        out_sum[...] = jnp.zeros_like(out_sum)
        mixed_sum[...] = jnp.zeros_like(mixed_sum)

    pre = dot(taken[...], w_expand[0]) + b_expand[...]
    slope = 0.7978845608028654
    square = pre * pre
    bend = jnp.tanh(slope * (pre + 0.044715 * (pre * square)))
    half = 0.5 * (1.0 + bend)
    activated = (pre * half).astype(BF)
    activated_out[...] = activated
    out_sum[...] += dot(activated, w_reduce[0])
    derivative = half + (0.5 * slope) * pre * (1.0 - bend * bend) * (1.0 + 0.134145 * square)
    grad_pre = (dot_cols(grads[...], w_reduce[0]) * derivative).astype(BF)
    grad_pre_out[...] = grad_pre
    mixed_sum[...] += dot_cols(grad_pre, w_expand[0])

    @pl.when(step == pl.num_programs(0) - 1)
    def _():
        for index in range(slots):
            begin = 2 * QUEUE * index
            part = slice(index * QUEUE, (index + 1) * QUEUE)
            answers[begin : begin + QUEUE] = (out_sum[part] + b_reduce[...]).astype(BF)
            answers[begin + QUEUE : begin + 2 * QUEUE] = mixed_sum[part].astype(BF)


def expert_part(chunk, messages, w_expand, b_expand, w_reduce, b_reduce):
    _, width, hidden = w_expand.shape
    count = messages.shape[0] // 2
    slots = count // QUEUE
    cut = min(512, hidden)
    outs = call(
        functools.partial(expert_kernel, slots),
        f"expert_{chunk}",
        (hidden // cut,),
        [
            whole(2 * count, width),
            pl.BlockSpec((1, width, cut), lambda i: (0, 0, i)),
            pl.BlockSpec((1, cut), lambda i: (0, i)),
            pl.BlockSpec((1, cut, width), lambda i: (0, i, 0)),
            whole(1, width),
        ],
        [
            whole(2 * count, width),
            pl.BlockSpec((count, cut), lambda i: (0, i)),
            pl.BlockSpec((count, cut), lambda i: (0, i)),
        ],
        [shape((2 * count, width), BF)] + [shape((count, hidden), BF)] * 2,
        [pltpu.VMEM((count, width), BF)] * 2 + [pltpu.VMEM((count, width), F32)] * 2,
        (8 * count * width * hidden, 8e6, count * hidden),
    )(messages, w_expand, b_expand, w_reduce, b_reduce)
    return outs


def expert_weights_kernel(chunks, place, *refs):
    messages, activated, grad_pre = refs[:chunks], refs[chunks : 2 * chunks], refs[2 * chunks : 3 * chunks]
    own, other, bias_e, bias_r, full_e, full_r = refs[3 * chunks :]
    join = lambda parts: jnp.concatenate(parts, axis=0)
    pick = lambda offset: join(
        [
            part[begin + offset : begin + offset + QUEUE]
            for part in messages
            for begin in range(0, part.shape[0], 2 * QUEUE)
        ]
    )
    taken, cotangent = pick(0), pick(QUEUE)
    pre = join([part[...] for part in grad_pre])
    full_e[...] = dot_rows(taken, pre).astype(BF)
    full_r[...] = dot_rows(join([part[...] for part in activated]), cotangent).astype(BF)
    bias_e[...] = jnp.sum(pre.astype(F32), axis=0, keepdims=True)
    bias_r[...] = jnp.sum(cotangent.astype(F32), axis=0, keepdims=True)
    begin = 0
    for full in (full_e, full_r):
        cut = full.shape[0] // 2
        for out, side in ((own, place[1] % 2), (other, 1 - place[1] % 2)):
            out[begin : begin + cut] = full[pl.ds(pl.multiple_of(side * cut, cut), cut), :]
        begin += cut


def expert_weights(place, kept):
    chunks = len(kept)
    messages, activated, grad_pre = zip(*kept)
    count, hidden = activated[0].shape
    width = messages[0].shape[1]
    cut = width
    wide = lambda rows: pl.BlockSpec((rows, cut), lambda i: (0, i))
    tall = pl.BlockSpec((cut, width), lambda i: (i, 0))
    return call(
        functools.partial(expert_weights_kernel, chunks),
        "expert_weights",
        (hidden // cut,),
        [scalars()] + [whole(2 * count, width)] * chunks + [wide(count)] * (2 * chunks),
        [tall, tall, wide(1), whole(1, width)],
        [shape((hidden, width), BF)] * 2 + [shape((1, hidden), F32), shape((1, width), F32)],
        [pltpu.VMEM((width, cut), BF), pltpu.VMEM((cut, width), BF)],
        (4 * chunks * count * width * hidden, 9e6, 0),
    )(place, *messages, *activated, *grad_pre)


def place_weights_kernel(place, own, own_across, other, other_across, out_e, out_r):
    begin = 0
    for out in (out_e, out_r):
        cut = out.shape[1] // 2
        part = slice(begin, begin + cut)
        for one, two, side in (
            (own, own_across, place[1] % 2),
            (other, other_across, 1 - place[1] % 2),
        ):
            total = one[part].astype(F32) + two[part].astype(F32)
            out[0, pl.ds(pl.multiple_of(side * cut, cut), cut), :] = total
        begin += cut


def place_weights(place, *parts):
    hidden, width = parts[0].shape
    cut = width
    tall = pl.BlockSpec((cut, width), lambda i: (i, 0))
    return call(
        place_weights_kernel,
        "place_expert_weights",
        (hidden // cut,),
        [scalars()] + [tall] * len(parts),
        [
            pl.BlockSpec((1, width, cut), lambda i: (0, 0, i)),
            pl.BlockSpec((1, cut, width), lambda i: (0, i, 0)),
        ],
        [shape((1, width, hidden), F32), shape((1, hidden, width), F32)],
        cost=(0, 16 * width * hidden, 0),
    )(place, *parts)


def unmix_kernel(slots, control, mixing_ref, members, cotangents, answers, back, merged, control_out):
    rows = members[...]
    grads = cotangents[...].reshape(rows.shape)
    pick = lambda part: jnp.concatenate([answers[index, part] for index in range(slots)], axis=0)
    expert_out, grad_mixed = pick(slice(0, QUEUE)), pick(slice(QUEUE, 2 * QUEUE))
    low = mixing_ref[...]
    mixing = low.astype(F32)
    grad_mixing = dot_cols(grads, expert_out) + dot_cols(rows, grad_mixed)
    weighted = mixing * grad_mixing
    grad_logits = weighted - mixing * jnp.sum(weighted, axis=0, keepdims=True)
    grad_logits = grad_logits.astype(BF)
    back[...] = (dot(low, grad_mixed) + dot_cols(grad_logits, control[...])).astype(BF)
    merged[...] = dot(low, expert_out).astype(BF).reshape(merged.shape)
    grad_control = dot_rows(grad_logits, rows)
    for index in range(slots):
        control_out[index : index + 1, :] = jnp.sum(
            grad_control[index * QUEUE : (index + 1) * QUEUE], axis=0, keepdims=True
        )


def without_previous(kernel, position):
    def inner(*refs):
        return kernel(*refs[:position], *refs[position + 1 :])

    return inner


def unmix_part(chunk, control, mixing, members, cotangents, answers, previous):
    slots, chunks, share, width = cotangents.shape
    columns = control.shape[1]
    kernel = functools.partial(unmix_kernel, slots)
    ins = [control, mixing, members, cotangents, answers]
    specs = [
        whole(width, columns),
        whole(LONG, columns),
        whole(LONG, width),
        chunk_block(slots, share, width, chunk),
        whole(slots, 2 * QUEUE, width),
    ]
    aliases = {}
    if previous is not None:
        aliases = {len(ins): 1}
        kernel = without_previous(kernel, len(ins))
        ins.append(previous)
        specs.append(pl.BlockSpec(memory_space=pl.ANY))
    return call(
        kernel,
        f"unmix_{chunk}",
        (1,),
        specs,
        [whole(LONG, width), chunk_block(slots, share, width, chunk), whole(slots, width)],
        [
            shape((LONG, width), BF),
            shape((slots, chunks, share, width), BF),
            shape((slots, width), F32),
        ],
        (),
        (12 * LONG * columns * width, 6e6, 0),
        aliases,
    )(*ins)


def output_kernel(chunks, *refs):
    merged, out = refs[chunks:]
    for chunk in range(chunks):
        rows = merged[:, chunk].reshape(LONG, out.shape[1]).astype(F32)
        out[chunk * LONG : (chunk + 1) * LONG] = (refs[chunk][...].astype(F32) + rows).astype(BF)


def output_part(resids, merged):
    slots, chunks, share, width = merged.shape
    return call(
        functools.partial(output_kernel, chunks),
        "output",
        (1,),
        [whole(LONG, width)] * chunks + [whole(slots, chunks, share, width)],
        whole(chunks * LONG, width),
        shape((chunks * LONG, width), BF),
        cost=(0, 8e6, 0),
    )(*resids, merged)


def backward_kernel(pairs, begins, later, split, *refs):
    refs = list(refs)
    take = lambda count: [refs.pop(0) for _ in range(count)]
    if begins:
        back, resid, grad_output, gain_second = take(4)
    else:
        (resid_low,) = take(1)
    parts = take(len(pairs))
    normed, qkv, exps, inverse, attended = take(5)
    (weights_before,) = take(1) if later else (None,)
    weights_out = take(len(pairs) if split else 1)
    (grads_out,) = take(1)
    if begins:
        gains_out, low_out = take(2)
    normed_turned, o_now, grad_scores_all, exps_now, arrived = take(5)
    if begins:
        (resid_low,) = take(1)
    step = pl.program_id(0)
    pair_width = attended.shape[2]
    tiles = LONG // TILE

    def fetch(index):
        slot = lax.rem(index, 2)
        return pltpu.make_async_copy(exps.at[pairs[0] - index], exps_now.at[slot], arrived.at[slot])

    @pl.when(step == 0)
    def _():
        fetch(step).start()

    @pl.when(step + 1 < len(pairs))
    def _():
        fetch(step + 1).start()

    @pl.when(step == 0)
    def _():
        normed_turned[...] = normed[...].T
        if begins:
            unit, scaling = normalize(resid[...].astype(F32))
            through, gain_grad = normalize_back(
                back[...].astype(F32), gain_second[...], unit, scaling
            )
            gains_out[...] = gain_grad
            resid_low[...] = (grad_output[...].astype(F32) + through).astype(BF)

    for index, part in enumerate(parts):

        @pl.when(step == index)
        def _(part=part):
            o_now[...] = out_weights(part[...], o_now.shape[1])

    if begins:
        share = low_out.shape[0]
        low_out[...] = resid_low[pl.ds(pl.multiple_of(step * share, share), share), :]
    low = resid_low[...]
    fetch(step).wait()
    exps = exps_now.at[lax.rem(step, 2)]
    grad_attended = dot_cols(low, o_now[...]).astype(BF)
    grad_out_weights = dot_rows(attended[0], low)
    wide = grad_attended.astype(F32)
    inverted = inverse[0].astype(F32)
    scaled = wide * inverted
    products = scaled * attended[0].astype(F32)
    scaled = scaled.astype(BF)
    low_half, high_half = halves(BF)
    low_wide, high_wide = halves(F32)
    queries = qkv[0, :, :pair_width] * BF(HEAD_DIM**-0.5)
    key_rows = qkv[0, :, pair_width : 2 * pair_width]
    value_rows = qkv[0, :, 2 * pair_width :]
    scaled_keys = key_rows * BF(HEAD_DIM**-0.5)
    queries_turned = queries.T
    grads_turned = scaled.T
    ones = (high_half, low_half)
    joined_q, joined_k, joined_v = [], [], []
    for head, (half, half_wide) in enumerate(((low_half, low_wide), (high_half, high_wide))):
        head_grads = scaled * half
        head_keys = scaled_keys * half
        deltas = jnp.sum(products * half_wide, axis=1, keepdims=True)
        part = slice(head * HEAD_DIM, (head + 1) * HEAD_DIM)
        query_rows = []
        for row_tile in range(tiles):
            begin, extent = row_tile * TILE, (row_tile + 1) * TILE
            powers = jnp.concatenate(
                [exps[head, tile_slot(row_tile, col_tile)] for col_tile in range(row_tile + 1)],
                axis=1,
            )
            grad_probs = dot_cols(head_grads[begin:extent], value_rows[:extent])
            grad_scores = (powers.astype(F32) * (grad_probs - deltas[begin:extent])).astype(BF)
            grad_scores_all[begin:extent, :extent] = grad_scores
            query_rows.append(dot(grad_scores, head_keys[:extent]))
        joined_q.append(jnp.concatenate(query_rows, axis=0))
        key_cols, value_cols = [], []
        for col_tile in range(tiles):
            begin, extent = col_tile * TILE, (col_tile + 1) * TILE
            powers = jnp.concatenate(
                [exps[head, tile_slot(row_tile, col_tile)] for row_tile in range(col_tile, tiles)],
                axis=0,
            )
            key_cols.append(dot(queries_turned[part, begin:], grad_scores_all[begin:, begin:extent]))
            value_cols.append(dot(grads_turned[part, begin:], powers))
        joined_k.append(jnp.concatenate(key_cols, axis=1))
        joined_v.append(jnp.concatenate(value_cols, axis=1))
    grads = jnp.concatenate(
        [
            (joined_q[0] + joined_q[1]).astype(BF),
            jnp.concatenate(joined_k, axis=0).T.astype(BF),
            jnp.concatenate(joined_v, axis=0).T.astype(BF),
        ],
        axis=1,
    )
    grads_out[0] = grads
    grad_weights = dot(normed_turned[...], grads)
    width = normed.shape[1]
    blocks = [grad_weights[:, index * pair_width : (index + 1) * pair_width] for index in range(3)]
    blocks += [
        grad_out_weights[:, index * pair_width : (index + 1) * pair_width]
        for index in range(width // pair_width)
    ]
    def store(out):
        begin = 0
        for block in blocks:
            extent = begin + block.shape[0]
            if later:
                block = block + weights_before[0, begin:extent].astype(F32)
            out[begin:extent] = block.astype(BF)
            begin = extent

    if split:
        for index, out in enumerate(weights_out):

            @pl.when(step == index)
            def _(out=out):
                store(out)

    else:
        store(weights_out[0].at[0])


def backward_part(chunk, pairs, start, low, parts, saved, before, split):
    exps = saved[2]
    width = saved[0].shape[1]
    packed, pair_width = parts[0].shape
    triple = 3 * pair_width
    kept = exps.shape[2]
    first = pairs[0]
    per_pair = lambda *dims: pl.BlockSpec((1,) + dims, lambda i: (first - i,) + (0,) * len(dims))
    rows = whole(LONG, width)
    begins, later = start is not None, before is not None
    if begins:
        ins = [*start]
        specs = [rows, rows, pl.BlockSpec((LONG, width), lambda i: (chunk, 0)), whole(1, width)]
    else:
        ins, specs = [low], [rows]
    ins += [parts[pair] for pair in pairs] + list(saved)
    out_part = pl.BlockSpec((width, pair_width), lambda i: (packed // width - 1, 0))
    specs += [out_part] * len(pairs)
    specs += [
        rows,
        per_pair(LONG, triple),
        pl.BlockSpec(memory_space=pl.ANY),
        per_pair(LONG, pair_width),
        per_pair(LONG, pair_width),
    ]
    if later:
        ins.append(before)
        specs.append(per_pair(packed, pair_width))
    count = len(pairs) if split else 1
    if split:
        out_specs = [whole(packed, pair_width)] * count
        outs = [shape((packed, pair_width), BF)] * count
    else:
        out_specs = [per_pair(packed, pair_width)]
        outs = [shape((len(pairs), packed, pair_width), BF)]
    out_specs.append(pl.BlockSpec((1, LONG, triple), lambda i: (i, 0, 0)))
    outs.append(shape((len(pairs), LONG, triple), BF))
    if begins:
        out_specs += [whole(1, width), pl.BlockSpec((LONG // len(pairs), width), lambda i: (i, 0))]
        outs += [shape((1, width), F32), shape((LONG, width), BF)]
    results = call(
        functools.partial(backward_kernel, pairs, begins, later, split),
        f"backward_{chunk}_{first}",
        (len(pairs),),
        specs,
        out_specs,
        outs,
        [
            pltpu.VMEM((width, LONG), BF),
            pltpu.VMEM((pair_width, width), BF),
            pltpu.VMEM((LONG, LONG), BF),
            pltpu.VMEM((2, 2, kept, TILE, TILE), BF),
            pltpu.SemaphoreType.DMA((2,)),
        ]
        + [pltpu.VMEM((LONG, width), BF)] * begins,
        (6e9 * len(pairs), 6e6 * len(pairs), 0),
        limit=LARGE,
    )(*ins)
    weights = dict(zip(pairs, results)) if split else results[0]
    return weights, results[count], results[count + 1 :]


def finish_kernel(groups, *refs):
    chunks = len(groups)
    refs = list(refs)
    take = lambda count: [refs.pop(0) for _ in range(count)]
    tokens, gain_first = take(2)
    parts = take(sum(len(group) for group in groups[0]))
    grads = [take(len(groups[chunk])) for chunk in range(chunks)]
    resids = take(chunks)
    grad_tokens, gain_out, weights = refs
    step = pl.program_id(0)
    width = tokens.shape[1]
    pairs, triple = len(parts), weights.shape[1] // len(parts)

    @pl.when(step == 0)
    def _():
        gain_out[...] = jnp.zeros_like(gain_out)
        for pair, part in enumerate(parts):
            cut = triple // 3
            for block in range(3):
                begin = pair * triple + block * cut
                weights[:, begin : begin + cut] = part[block * width : (block + 1) * width]

    for chunk in range(chunks):

        @pl.when(step == chunk)
        def _(chunk=chunk):
            columns = {}
            for group, ref in zip(groups[chunk], grads[chunk]):
                for index, pair in enumerate(group):
                    columns[pair] = ref[index]
            joined = jnp.concatenate([columns[pair] for pair in range(pairs)], axis=1)
            unit, scaling = normalize(tokens[...].astype(F32))
            through, gain_grad = normalize_back(
                dot_cols(joined, weights[...]), gain_first[...], unit, scaling
            )
            gain_out[...] += gain_grad
            grad_tokens[...] = resids[chunk][...].astype(F32) + through


def finish_part(tokens, gain_first, parts, groups, grads, resids):
    total, width = tokens.shape
    chunks = total // LONG
    packed, pair_width = parts[0].shape
    rows = pl.BlockSpec((LONG, width), lambda i: (i, 0))
    flat = [ref for chunk in grads for ref in chunk]
    return call(
        functools.partial(finish_kernel, groups),
        "finish",
        (chunks,),
        [rows, whole(1, width)]
        + [whole(packed, pair_width)] * len(parts)
        + [whole(*ref.shape) for ref in flat]
        + [whole(LONG, width)] * chunks,
        [rows, whole(1, width)],
        [shape((total, width), F32), shape((1, width), F32)],
        [pltpu.VMEM((width, 3 * pair_width * len(parts)), BF)],
        (2 * total * width * 3 * pair_width * len(parts), 2e7, 0),
        limit=LARGE,
    )(tokens, gain_first, *parts, *flat, *resids)


def tail_pack_kernel(*refs):
    total = refs[0][...].astype(F32)
    for part in refs[1:-1]:
        total = total + part[...].astype(F32)
    refs[-1][...] = total.astype(BF)


def tail_pack(parts):
    rows, cut = parts[0].shape
    return call(
        tail_pack_kernel,
        "tail_pack",
        (1,),
        [whole(rows, cut)] * len(parts),
        whole(rows, cut),
        shape((rows, cut), BF),
        cost=(0, 3e6, 0),
    )(*parts)


def tail_sum_kernel(slots, sent, pieces, *refs):
    *parts, out, bias_e, bias_r = refs
    small = tree_sum([part[...] for part in parts])
    share, cut = pieces.shape[1:]
    total = pieces[0].astype(F32)
    for index in range(1, slots):
        total = total + pieces[index].astype(F32)
    total = total.astype(BF)
    packed = jnp.concatenate(
        [small[:sent, begin : begin + cut] for begin in range(0, small.shape[1], cut)], axis=0
    ).astype(BF)
    for index in range(slots):
        out[index, :share] = total
        out[index, share:] = packed
    width = bias_r.shape[1]
    rows = bias_e.shape[1] // width
    for index in range(rows):
        bias_e[:, index * width : (index + 1) * width] = small[sent + index : sent + index + 1]
    bias_r[...] = small[sent + rows : sent + rows + 1]


def tail_sum(pieces, smalls, sent, hidden):
    slots, share, cut = pieces.shape
    count, width = smalls[0].shape
    rows = share + sent * width // cut
    return call(
        functools.partial(tail_sum_kernel, slots, sent),
        "tail_sum",
        (1,),
        [whole(slots, share, cut)] + [whole(count, width)] * len(smalls),
        [whole(slots, rows, cut), whole(1, hidden), whole(1, width)],
        [shape((slots, rows, cut), BF), shape((1, hidden), F32), shape((1, width), F32)],
        cost=(0, 2e6, 0),
    )(pieces, *smalls)


def gather_kernel(slots, share, pieces, *refs):
    outs, gain_first, gain_second, control, total = refs[:4], refs[4], refs[5], refs[6], refs[7]
    for index in range(slots):
        total[index * share : (index + 1) * share] = pieces[index, :share].astype(F32)
    cut = total.shape[1]
    begin = 0
    for out in outs[:3]:
        out[...] = total[begin : begin + out.shape[0]]
        begin += out.shape[0]
    last = outs[3]
    blocks = last.shape[1] // cut
    for index in range(blocks):
        last[:, index * cut : (index + 1) * cut] = total[begin : begin + last.shape[0]]
        begin += last.shape[0]
    small = pieces[0, share:].astype(F32)
    for index in range(1, slots):
        small = small + pieces[index, share:].astype(F32)
    count = small.shape[0] // blocks
    small = jnp.concatenate(
        [small[index * count : (index + 1) * count] for index in range(blocks)], axis=1
    )
    experts = control.shape[0]
    gain_first[...] = small[experts : experts + 1]
    gain_second[...] = small[experts + 1 : experts + 2]
    control[...] = small[:experts]


def gather_weights(pieces, share, width, experts):
    slots, _, cut = pieces.shape
    outs = [(width, cut)] * 3 + [(cut, width), (1, width), (1, width), (experts, width)]
    return call(
        functools.partial(gather_kernel, slots, share),
        "gather_weights",
        (1,),
        [whole(*pieces.shape)],
        [whole(*dims) for dims in outs],
        [shape(dims, F32) for dims in outs],
        [pltpu.VMEM((share * slots, cut), F32)],
        (0, 3e6, 0),
    )(pieces)


def partner(value, axis, offset):
    count = lax.axis_size(axis)
    return lax.ppermute(value, axis, [(index, index ^ offset) for index in range(count)])


def exchange(value, axis):
    return lax.all_to_all(value, axis, 0, 0, tiled=True)


def tree_sum(parts):
    while len(parts) > 1:
        parts = [parts[index] + parts[index + 1] for index in range(0, len(parts), 2)]
    return parts[0]


def gather_head(part):
    sibling = partner(part, "head", 1)
    across = partner(part, "head", 2)
    return [part, sibling, across, partner(across, "head", 1)]


def add_low(*parts):
    return sum(part.astype(F32) for part in parts).astype(BF)


def after(value, *earlier):
    return lax.optimization_barrier((value, *earlier))[0]


def body(
    tokens,
    gain_first,
    w_query,
    w_key,
    w_value,
    w_out,
    gain_second,
    w_control,
    w_expand,
    b_expand,
    w_reduce,
    b_reduce,
    lengths,
    grad_output,
):
    rows_local, width = tokens.shape
    pair_width = w_query.shape[1]
    slots = lax.axis_size("seq")
    chunks = rows_local // LONG
    place = jnp.stack([lax.axis_index("seq"), lax.axis_index("head")]).astype(jnp.int32)
    gain_first = gain_first[None]
    gain_second = gain_second[None]
    parts = gather_head(pack_weights(w_query, w_key, w_value, w_out))
    experts = w_control.shape[1]
    control = jnp.repeat(w_control, QUEUE, axis=1)
    cotangents = exchange(pack_rows(grad_output, slots), "seq")

    forwards, members = [], []
    for chunk in range(chunks):
        *saved, second = forward_part(
            chunk, place, lengths, tokens, gain_first, parts, gain_second
        )
        forwards.append(saved)
        second = after(second, cotangents)
        members.append(exchange(second, "seq"))
    mixings, answers, kept = [], [], []
    for chunk in range(chunks):
        mixing, messages = mixing_part(chunk, control, members[chunk], cotangents)
        mixings.append(mixing)
        messages = exchange(messages, "seq")
        flat = messages.reshape(-1, width)
        replies, *saved = expert_part(chunk, flat, w_expand, b_expand, w_reduce, b_reduce)
        kept.append((flat, *saved))
        answers.append(exchange(replies.reshape(messages.shape), "seq"))
    backs, merged, controls = [], None, []
    for chunk in range(chunks):
        back, merged, grad_control = unmix_part(
            chunk, control, mixings[chunk], members[chunk], cotangents, answers[chunk], merged
        )
        early_back = back if chunk == 0 else early_back
        backs.append(exchange(back, "seq"))
        controls.append(grad_control)

    own, other, bias_e, bias_r = expert_weights(place, [after(kept[0], early_back), *kept[1:]])
    own = add_low(own, partner(other, "head", 1))
    across = partner(own, "head", 2)
    placed = (own, across, partner(own, "head", 1), partner(across, "head", 1))

    pairs = tuple(reversed(range(len(parts))))
    early, late = pairs[: len(pairs) // 2], pairs[len(pairs) // 2 :]
    before, gains, groups, grads, resids = None, [], [], [], []
    for chunk in range(chunks):
        *saved, resid = forwards[chunk]
        back = backs[chunk]
        if chunk == chunks - 1:
            if gains:
                merged = after(merged, gains[-1])
            merged = exchange(merged, "seq")
            back = after(back, across)
            start = (back, resid, grad_output, gain_second)
            first_weights, first_grads, (gain, low) = backward_part(
                chunk, early, start, None, parts, saved, before, True
            )
            joint = add_low(first_weights[2], partner(first_weights[3], "head", 1))
            pieces = [partner(joint, "head", 2)]
            second_weights, second_grads, _ = backward_part(
                chunk, late, None, after(low, joint), parts, saved, before, True
            )
            groups.append((early, late))
            grads.append((first_grads, second_grads))
        else:
            start = (back, resid, grad_output, gain_second)
            before, chunk_grads, (gain, low) = backward_part(
                chunk, pairs, start, None, parts, saved, before, False
            )
            groups.append((pairs,))
            grads.append((chunk_grads,))
        gains.append(gain)
        resids.append(low)
    resids[-1] = after(resids[-1], *pieces)
    grad_tokens, gain = finish_part(tokens, gain_first, parts, groups, grads, resids)

    pieces.append(partner(after(second_weights[1], *pieces), "head", 1))
    packed = tail_pack([second_weights[0]] + pieces)
    hidden = bias_e.shape[1]
    sent = -(-(experts + 2) // 8) * 8
    spare = jnp.zeros((sent - experts - 2, width), F32)
    small = [sum(controls), gain, sum(gains), spare, bias_e.reshape(-1, width), bias_r]
    small = jnp.concatenate(small, axis=0)
    smalls = [small] + [partner(small, "head", index) for index in range(1, len(parts))]
    packed = after(packed, merged, *smalls, *placed)
    pieces = exchange(packed, "seq").reshape(slots, -1, pair_width)
    pieces, grad_expand_bias, grad_reduce_bias = tail_sum(pieces, smalls, sent, hidden)
    pieces = exchange(pieces, "seq")
    share = parts[0].shape[0] // slots
    *weights, gain_first, gain_second, control = gather_weights(pieces, share, width, experts)
    grad_query, grad_key, grad_value, grad_w_out = weights
    grad_expand, grad_reduce = place_weights(place, *placed)
    output = output_part([saved[5] for saved in forwards], merged)
    return (
        output,
        grad_tokens,
        gain_first[0],
        grad_query,
        grad_key,
        grad_value,
        grad_w_out,
        gain_second[0],
        control.T,
        grad_expand,
        grad_expand_bias,
        grad_reduce,
        grad_reduce_bias,
    )


def solution(mesh):
    in_specs = (
        P(("seq", "head"), None),
        P(),
        P(None, "head"),
        P(None, "head"),
        P(None, "head"),
        P("head", None),
        P(),
        P(),
        P("seq", None, None),
        P("seq", None),
        P("seq", None, None),
        P("seq", None),
        P("seq", None),
        P(("seq", "head"), None),
    )
    out_specs = (
        P(("seq", "head"), None),
        P(("seq", "head"), None),
        P(),
        P(None, "head"),
        P(None, "head"),
        P(None, "head"),
        P("head", None),
        P(),
        P(),
        P("seq", None, None),
        P("seq", None),
        P("seq", None, None),
        P("seq", None),
    )
    return jax.shard_map(body, mesh=mesh, in_specs=in_specs, out_specs=out_specs, check_vma=False)
```

```python
import functools
import jax
import jax.numpy as jnp
from jax import lax
from jax.sharding import PartitionSpec as P
from jax.experimental import pallas as pl
from jax.experimental.pallas import tpu as pltpu

HEAD_DIM = 64
GROUP = 32
LONG = 1024
TILE = 256
QUEUE = 2 * LONG // GROUP
SEQ = ("half", "quarter")
WAITING = 1.5e+10
EPSILON = 1e-05
MASKED = -1000000000.0
BF = jnp.bfloat16
F32 = jnp.float32
ROWS_BY_ROWS = (((0,), (0,)), ((), ()))
COLS_BY_COLS = (((1,), (1,)), ((), ()))
LARGE = 62 * 1024 * 1024
SMALL = 28 * 1024 * 1024


def dot(left, right):
    return jnp.dot(left, right, preferred_element_type=F32)


def dot_rows(left, right):
    return lax.dot_general(left, right, ROWS_BY_ROWS, preferred_element_type=F32)


def dot_cols(left, right):
    return lax.dot_general(left, right, COLS_BY_COLS, preferred_element_type=F32)


def normalize(matrix):
    centre = jnp.mean(matrix, axis=1, keepdims=True)
    shifted = matrix - centre
    scaling = lax.rsqrt(jnp.mean(shifted * shifted, axis=1, keepdims=True) + EPSILON)
    return shifted * scaling, scaling


def normalize_back(grad_norm, gain, unit_rows, scaling):
    inner_grad = grad_norm * gain
    centred = (
        inner_grad
        - jnp.mean(inner_grad, axis=1, keepdims=True)
        - unit_rows * jnp.mean(inner_grad * unit_rows, axis=1, keepdims=True)
    )
    return scaling * centred, jnp.sum(grad_norm * unit_rows, axis=0, keepdims=True)


def whole(*shape):
    return pl.BlockSpec(shape, lambda *_: (0,) * len(shape))


def scalars():
    return pl.BlockSpec(memory_space=pltpu.SMEM)


def call(kernel, name, grid, in_specs, out_specs, out_shape, scratch=(), cost=(0, 0, 0), aliases=None, limit=SMALL):
    return pl.pallas_call(
        kernel,
        grid=grid,
        in_specs=in_specs,
        out_specs=out_specs,
        out_shape=out_shape,
        scratch_shapes=list(scratch),
        input_output_aliases=aliases or {},
        cost_estimate=pl.CostEstimate(
            flops=int(cost[0]), bytes_accessed=int(cost[1]), transcendentals=int(cost[2])
        ),
        compiler_params=pltpu.CompilerParams(vmem_limit_bytes=limit),
        name=name,
    )


def shape(dims, dtype):
    return jax.ShapeDtypeStruct(dims, dtype)


def tile_slot(row_tile, col_tile):
    return row_tile * (row_tile + 1) // 2 + col_tile


def halves(dtype):
    lane = lax.broadcasted_iota(jnp.int32, (1, 2 * HEAD_DIM), 1)
    first = (lane < HEAD_DIM).astype(F32)
    return first.astype(dtype), (1.0 - first).astype(dtype)


def out_weights(part, width):
    cut = part.shape[1]
    base = part.shape[0] - width
    blocks = [part[base + begin : base + begin + cut] for begin in range(0, width, cut)]
    return jnp.concatenate(blocks, axis=1)


def forward_kernel(pairs, chunk, chunks, *refs):
    place, lengths, tokens, gain_first = refs[:4]
    parts = refs[4 : 4 + pairs]
    gain_second = refs[4 + pairs]
    normed_out, qkv_out, exps, inverse, attended, resid, second = refs[5 + pairs : 12 + pairs]
    normed, weights, bias, attended_all, arrived = refs[12 + pairs :]
    step = pl.program_id(0)
    width = tokens.shape[1]
    pair_width = attended.shape[2]
    fetches = [
        pltpu.make_async_copy(part, weights.at[index], arrived.at[index])
        for index, part in enumerate(parts)
    ]
    tiles = LONG // TILE

    @pl.when(step == 0)
    def _():
        for fetch in fetches:
            fetch.start()
        unit, _ = normalize(tokens[...].astype(F32))
        normed[...] = (unit * gain_first[...]).astype(BF)
        base = 4 * (place[1] * chunks + chunk)
        first = lengths[0, base]
        second_bound = first + lengths[0, base + 1]
        third = second_bound + lengths[0, base + 2]
        for row_tile in range(tiles):
            row = lax.broadcasted_iota(jnp.int32, (TILE, 1), 0) + row_tile * TILE
            begin = jnp.where(row >= first, first, 0)
            begin = jnp.where(row >= second_bound, second_bound, begin)
            begin = jnp.where(row >= third, third, begin)
            col = lax.broadcasted_iota(jnp.int32, (TILE, LONG), 1)
            allowed = (col <= row) & (col >= begin)
            bias[pl.ds(row_tile * TILE, TILE), :] = jnp.where(allowed, 0.0, MASKED)

    for index, fetch in enumerate(fetches):

        @pl.when(step == index)
        def _(fetch=fetch):
            fetch.wait()

    share = LONG // pairs
    normed_out[...] = normed[pl.ds(pl.multiple_of(step * share, share), share), :]
    own = weights[step, : 3 * width]
    own = jnp.concatenate([own[begin : begin + width] for begin in range(0, 3 * width, width)], axis=1)
    qkv = dot(normed[...], own).astype(BF)
    qkv_out[0] = qkv
    queries = qkv[:, :pair_width] * BF(HEAD_DIM**-0.5)
    key_rows = qkv[:, pair_width : 2 * pair_width]
    value_rows = qkv[:, 2 * pair_width :]
    low_half, high_half = halves(BF)
    is_low = lax.broadcasted_iota(jnp.int32, (TILE, pair_width), 1) < HEAD_DIM
    masks = ((low_half, high_half), (high_half, low_half))
    head_queries = [queries * own for own, other in masks]
    head_values = [value_rows * own + other for own, other in masks]
    for row_tile in range(tiles):
        begin, extent = row_tile * TILE, (row_tile + 1) * TILE
        raw = []
        for head in range(2):
            scores = dot_cols(head_queries[head][begin:extent], key_rows[:extent])
            scores = scores + bias[begin:extent, :extent]
            highest = jnp.max(scores, axis=1, keepdims=True)
            powers = jnp.exp(scores - highest).astype(BF)
            for col_tile in range(row_tile + 1):
                exps[0, head, tile_slot(row_tile, col_tile)] = powers[
                    :, col_tile * TILE : (col_tile + 1) * TILE
                ]
            raw.append(dot(powers, head_values[head][:extent]))
        totals = jnp.where(
            is_low, pltpu.roll(raw[0], HEAD_DIM, 1), pltpu.roll(raw[1], HEAD_DIM, 1)
        )
        inverted = 1.0 / totals
        inverse[0, begin:extent] = inverted.astype(BF)
        attended_tile = (jnp.where(is_low, raw[0], raw[1]) * inverted).astype(BF)
        attended[0, begin:extent] = attended_tile
        attended_all[step, begin:extent] = attended_tile

    @pl.when(step == pairs - 1)
    def _():
        rows = jnp.concatenate([attended_all[index] for index in range(pairs)], axis=1)
        blocks = width // pair_width
        own = jnp.concatenate([out_weights(weights[index], width) for index in range(pairs)], axis=0)
        total = tokens[...].astype(F32) + dot(rows, own)
        resid[...] = total.astype(BF)
        unit, _ = normalize(total)
        second[...] = (unit * gain_second[...]).astype(BF)


def forward_part(chunk, place, lengths, tokens, gain_first, parts, gain_second):
    rows, width = tokens.shape
    pairs = len(parts)
    packed, pair_width = parts[0].shape
    triple = 3 * pair_width
    kept = LONG // TILE * (LONG // TILE + 1) // 2
    per_pair = lambda *dims: pl.BlockSpec((1,) + dims, lambda i: (i,) + (0,) * len(dims))
    return call(
        functools.partial(forward_kernel, pairs, chunk, rows // LONG),
        f"forward_{chunk}",
        (pairs,),
        [scalars(), scalars(), pl.BlockSpec((LONG, width), lambda i: (chunk, 0)), whole(1, width)]
        + [pl.BlockSpec(memory_space=pl.ANY)] * pairs
        + [whole(1, width)],
        [
            pl.BlockSpec((LONG // pairs, width), lambda i: (i, 0)),
            per_pair(LONG, triple),
            per_pair(2, kept, TILE, TILE),
            per_pair(LONG, pair_width),
            per_pair(LONG, pair_width),
            whole(LONG, width),
            whole(LONG, width),
        ],
        [
            shape((LONG, width), BF),
            shape((pairs, LONG, triple), BF),
            shape((pairs, 2, kept, TILE, TILE), BF),
            shape((pairs, LONG, pair_width), BF),
            shape((pairs, LONG, pair_width), BF),
            shape((LONG, width), BF),
            shape((LONG, width), BF),
        ],
        [
            pltpu.VMEM((LONG, width), BF),
            pltpu.VMEM((pairs, packed, pair_width), BF),
            pltpu.VMEM((LONG, LONG), F32),
            pltpu.VMEM((pairs, LONG, pair_width), BF),
            pltpu.SemaphoreType.DMA((pairs,)),
        ],
        (10e9, 25e6, 5e6),
        limit=LARGE,
    )(place, lengths, tokens, gain_first, *parts, gain_second)


def pack_kernel(rows, out, arrived):
    slots, chunks, share, _ = out.shape
    copies = []
    for chunk in range(chunks):
        for index in range(slots):
            begin = chunk * LONG + index * share
            copies.append(
                pltpu.make_async_copy(
                    rows.at[pl.ds(begin, share)], out.at[index, chunk], arrived.at[len(copies)]
                )
            )
    for copy in copies:
        copy.start()
    for copy in copies:
        copy.wait()


def pack_rows(rows, slots):
    total, width = rows.shape
    chunks, share = total // LONG, LONG // slots
    return call(
        pack_kernel,
        "pack_cotangent",
        (1,),
        [pl.BlockSpec(memory_space=pl.ANY)],
        pl.BlockSpec(memory_space=pl.ANY),
        shape((slots, chunks, share, width), BF),
        [pltpu.SemaphoreType.DMA((slots * chunks,))],
        (0, 4 * total * width, 0),
    )(rows)


def pack_weights_kernel(query, key, value, out, packed):
    width, cut = query.shape
    for index, part in enumerate((query, key, value)):
        packed[index * width : (index + 1) * width] = part[...]
    for index in range(width // cut):
        begin = 3 * width + index * cut
        packed[begin : begin + cut] = out[:, index * cut : (index + 1) * cut]


def pack_weights(query, key, value, out):
    width, cut = query.shape
    return call(
        pack_weights_kernel,
        "pack_weights",
        (1,),
        [whole(width, cut)] * 3 + [whole(cut, width)],
        whole(4 * width, cut),
        shape((4 * width, cut), BF),
        cost=(0, 16 * width * cut, 0),
    )(query, key, value, out)


def group_mask(slots, columns):
    share = LONG // slots
    stride = share // QUEUE
    row = lax.broadcasted_iota(jnp.int32, (LONG, columns), 0)
    col = lax.broadcasted_iota(jnp.int32, (LONG, columns), 1)
    return ((row % share) // stride) == (col % QUEUE)


def chunk_block(slots, rows, width, chunk):
    return pl.BlockSpec((slots, 1, rows, width), lambda i: (0, chunk, 0, 0))


def mixing_kernel(slots, control, members, cotangents, mixing_out, stats, kept, sent):
    width, columns = control.shape
    rows = members[...]
    grads = cotangents[...].reshape(LONG, width)
    logits = jnp.where(group_mask(slots, columns), dot(rows, control[...]), -1e30)
    highest = jnp.max(logits, axis=0, keepdims=True)
    powers = jnp.exp(logits - highest)
    total = jnp.sum(powers, axis=0, keepdims=True)
    stats[0:1] = highest
    stats[1:2] = total
    low = (powers / total).astype(BF)
    mixing_out[...] = low
    mixed = dot_rows(low, rows).astype(BF)
    grad_out = dot_rows(low, grads).astype(BF)
    for index in range(slots):
        for out, begin in ((kept, index * QUEUE), (sent, (index + slots) * QUEUE)):
            out[index, :QUEUE] = mixed[begin : begin + QUEUE]
            out[index, QUEUE:] = grad_out[begin : begin + QUEUE]


def mixing_part(chunk, control, members, cotangents):
    slots, chunks, share, _ = cotangents.shape
    width, columns = control.shape
    return call(
        functools.partial(mixing_kernel, slots),
        f"mixing_{chunk}",
        (1,),
        [whole(width, columns), whole(LONG, width), chunk_block(slots, share, width, chunk)],
        [whole(LONG, columns), whole(2, columns)] + [whole(slots, 2 * QUEUE, width)] * 2,
        [shape((LONG, columns), BF), shape((2, columns), F32)]
        + [shape((slots, 2 * QUEUE, width), BF)] * 2,
        cost=(1e6, 1e4, 0),
        limit=LARGE if columns > 1024 else SMALL,
    )(control, members, cotangents)


def combine_kernel(slots, kept, came, own_stats, came_stats, messages, weights):
    columns = own_stats.shape[1]
    middle = columns // 2
    other = jnp.concatenate([came_stats[:, middle:], came_stats[:, :middle]], axis=1)
    highest = jnp.maximum(own_stats[0:1], other[0:1])
    own_total = own_stats[1:2] * jnp.exp(own_stats[0:1] - highest)
    other_total = other[1:2] * jnp.exp(other[0:1] - highest)
    own_share = own_total / (own_total + other_total)
    weights[...] = own_share
    turned = jnp.broadcast_to(own_share[:, :middle], (8, middle)).T
    for index in range(slots):
        share = turned[index * QUEUE : (index + 1) * QUEUE, 0:1]
        for begin in (0, QUEUE):
            part = slice(begin, begin + QUEUE)
            one = kept[index, part].astype(F32)
            two = came[index, part].astype(F32)
            messages[index, part] = (two + share * (one - two)).astype(BF)


def combine_part(chunk, kept, came, own_stats, came_stats):
    slots, rows, width = kept.shape
    columns = own_stats.shape[1]
    return call(
        functools.partial(combine_kernel, slots),
        f"combine_{chunk}",
        (1,),
        [whole(slots, rows, width)] * 2 + [whole(2, columns)] * 2,
        [whole(slots, rows, width), whole(1, columns)],
        [shape((slots, rows, width), BF), shape((1, columns), F32)],
        cost=(WAITING, 2e6, 0),
    )(kept, came, own_stats, came_stats)


def column_kernel(slots, messages, answers, out, again):
    again[...] = answers[...]
    sums = []
    for index in range(slots):
        mixed = messages[index, :QUEUE].astype(F32)
        grad_out = messages[index, QUEUE:].astype(F32)
        expert_out = answers[index, :QUEUE].astype(F32)
        grad_mixed = answers[index, QUEUE:].astype(F32)
        products = expert_out * grad_out + grad_mixed * mixed
        sums.append(jnp.sum(products, axis=1, keepdims=True))
    sums = jnp.concatenate(sums, axis=0)
    out[...] = jnp.broadcast_to(sums, (sums.shape[0], 8)).T


def column_part(chunk, messages, answers):
    slots, rows, width = messages.shape
    return call(
        functools.partial(column_kernel, slots),
        f"columns_{chunk}",
        (1,),
        [whole(slots, rows, width)] * 2,
        [whole(8, slots * QUEUE), whole(slots, rows, width)],
        [shape((8, slots * QUEUE), F32), shape((slots, rows, width), BF)],
        cost=(1e6, 1e4, 0),
    )(messages, answers)


def expert_kernel(slots, messages, w_expand, b_expand, w_reduce, b_reduce, *refs):
    answers, activated_out, grad_pre_out, taken, grads, out_sum, mixed_sum = refs
    step = pl.program_id(0)

    @pl.when(step == 0)
    def _():
        for index in range(slots):
            begin = 2 * QUEUE * index
            part = slice(index * QUEUE, (index + 1) * QUEUE)
            taken[part] = messages[begin : begin + QUEUE]
            grads[part] = messages[begin + QUEUE : begin + 2 * QUEUE]
        out_sum[...] = jnp.zeros_like(out_sum)
        mixed_sum[...] = jnp.zeros_like(mixed_sum)

    pre = dot(taken[...], w_expand[0]) + b_expand[...]
    slope = 0.7978845608028654
    square = pre * pre
    bend = jnp.tanh(slope * (pre + 0.044715 * (pre * square)))
    half = 0.5 * (1.0 + bend)
    activated = (pre * half).astype(BF)
    activated_out[...] = activated
    out_sum[...] += dot(activated, w_reduce[0])
    derivative = half + (0.5 * slope) * pre * (1.0 - bend * bend) * (1.0 + 0.134145 * square)
    grad_pre = (dot_cols(grads[...], w_reduce[0]) * derivative).astype(BF)
    grad_pre_out[...] = grad_pre
    mixed_sum[...] += dot_cols(grad_pre, w_expand[0])

    @pl.when(step == pl.num_programs(0) - 1)
    def _():
        for index in range(slots):
            begin = 2 * QUEUE * index
            part = slice(index * QUEUE, (index + 1) * QUEUE)
            answers[begin : begin + QUEUE] = (out_sum[part] + b_reduce[...]).astype(BF)
            answers[begin + QUEUE : begin + 2 * QUEUE] = mixed_sum[part].astype(BF)


def expert_part(chunk, messages, w_expand, b_expand, w_reduce, b_reduce):
    _, width, hidden = w_expand.shape
    count = messages.shape[0] // 2
    slots = count // QUEUE
    cut = min(512, hidden)
    outs = call(
        functools.partial(expert_kernel, slots),
        f"expert_{chunk}",
        (hidden // cut,),
        [
            whole(2 * count, width),
            pl.BlockSpec((1, width, cut), lambda i: (0, 0, i)),
            pl.BlockSpec((1, cut), lambda i: (0, i)),
            pl.BlockSpec((1, cut, width), lambda i: (0, i, 0)),
            whole(1, width),
        ],
        [
            whole(2 * count, width),
            pl.BlockSpec((count, cut), lambda i: (0, i)),
            pl.BlockSpec((count, cut), lambda i: (0, i)),
        ],
        [shape((2 * count, width), BF)] + [shape((count, hidden), BF)] * 2,
        [pltpu.VMEM((count, width), BF)] * 2 + [pltpu.VMEM((count, width), F32)] * 2,
        (1e6, 1e4, 0),
    )(messages, w_expand, b_expand, w_reduce, b_reduce)
    return outs


def expert_weights_kernel(chunks, place, *refs):
    messages, activated, grad_pre = refs[:chunks], refs[chunks : 2 * chunks], refs[2 * chunks : 3 * chunks]
    own, other, bias_e, bias_r, full_e, full_r = refs[3 * chunks :]
    join = lambda parts: jnp.concatenate(parts, axis=0)
    pick = lambda offset: join(
        [
            part[begin + offset : begin + offset + QUEUE]
            for part in messages
            for begin in range(0, part.shape[0], 2 * QUEUE)
        ]
    )
    taken, cotangent = pick(0), pick(QUEUE)
    pre = join([part[...] for part in grad_pre])
    full_e[...] = dot_rows(taken, pre).astype(BF)
    full_r[...] = dot_rows(join([part[...] for part in activated]), cotangent).astype(BF)
    bias_e[...] = jnp.sum(pre.astype(F32), axis=0, keepdims=True)
    bias_r[...] = jnp.sum(cotangent.astype(F32), axis=0, keepdims=True)
    begin = 0
    for full in (full_e, full_r):
        cut = full.shape[0] // 2
        for out, side in ((own, place[1] % 2), (other, 1 - place[1] % 2)):
            out[begin : begin + cut] = full[pl.ds(pl.multiple_of(side * cut, cut), cut), :]
        begin += cut


def expert_weights(place, kept):
    chunks = len(kept)
    messages, activated, grad_pre = zip(*kept)
    count, hidden = activated[0].shape
    width = messages[0].shape[1]
    cut = width
    wide = lambda rows: pl.BlockSpec((rows, cut), lambda i: (0, i))
    tall = pl.BlockSpec((cut, width), lambda i: (i, 0))
    return call(
        functools.partial(expert_weights_kernel, chunks),
        "expert_weights",
        (hidden // cut,),
        [scalars()] + [whole(2 * count, width)] * chunks + [wide(count)] * (2 * chunks),
        [tall, tall, wide(1), whole(1, width)],
        [shape((hidden, width), BF)] * 2 + [shape((1, hidden), F32), shape((1, width), F32)],
        [pltpu.VMEM((width, cut), BF), pltpu.VMEM((cut, width), BF)],
        (WAITING, 1e4, 0),
    )(place, *messages, *activated, *grad_pre)


def place_weights_kernel(place, own, own_across, other, other_across, out_e, out_r):
    begin = 0
    for out in (out_e, out_r):
        cut = out.shape[1] // 2
        part = slice(begin, begin + cut)
        for one, two, side in (
            (own, own_across, place[1] % 2),
            (other, other_across, 1 - place[1] % 2),
        ):
            total = one[part].astype(F32) + two[part].astype(F32)
            out[0, pl.ds(pl.multiple_of(side * cut, cut), cut), :] = total
        begin += cut


def place_weights(place, *parts):
    hidden, width = parts[0].shape
    cut = width
    tall = pl.BlockSpec((cut, width), lambda i: (i, 0))
    return call(
        place_weights_kernel,
        "place_expert_weights",
        (hidden // cut,),
        [scalars()] + [tall] * len(parts),
        [
            pl.BlockSpec((1, width, cut), lambda i: (0, 0, i)),
            pl.BlockSpec((1, cut, width), lambda i: (0, i, 0)),
        ],
        [shape((1, width, hidden), F32), shape((1, hidden, width), F32)],
        cost=(0, 16 * width * hidden, 0),
    )(place, *parts)


def unmix_kernel(slots, place, control, mixing_ref, weights, members, cotangents, *refs):
    own_answers, other_answers, own_sums, other_sums, back, merged, control_out = refs
    rows = members[...]
    grads = cotangents[...].reshape(rows.shape)
    pick = lambda part: jnp.concatenate(
        [answers[index, part] for answers in (own_answers, other_answers) for index in range(slots)],
        axis=0,
    )
    expert_out, grad_mixed = pick(slice(0, QUEUE)), pick(slice(QUEUE, 2 * QUEUE))
    mixing = mixing_ref[...].astype(F32) * weights[...]
    low = mixing.astype(BF)
    grad_mixing = dot_cols(grads, expert_out) + dot_cols(rows, grad_mixed)
    sums = jnp.concatenate([own_sums[0:1], other_sums[0:1]], axis=1)
    grad_logits = (mixing * (grad_mixing - sums)).astype(BF)
    back[...] = (dot(low, grad_mixed) + dot_cols(grad_logits, control[...])).astype(BF)
    merged[...] = dot(low, expert_out).astype(BF).reshape(merged.shape)
    grad_control = dot_rows(grad_logits, rows)
    for index in range(2 * slots):
        expert = place[2] * slots + index if index < slots else (1 - place[2]) * slots + index - slots
        control_out[pl.ds(expert, 1), :] = jnp.sum(
            grad_control[index * QUEUE : (index + 1) * QUEUE], axis=0, keepdims=True
        )


def without_previous(kernel, position):
    def inner(*refs):
        return kernel(*refs[:position], *refs[position + 1 :])

    return inner


def unmix_part(
    chunk, place, control, mixing, weights, members, cotangents, answers, sums, previous
):
    slots, chunks, share, width = cotangents.shape
    columns = control.shape[1]
    kernel = functools.partial(unmix_kernel, slots)
    ins = [place, control, mixing, weights, members, cotangents, *answers, *sums]
    specs = [
        scalars(),
        whole(width, columns),
        whole(LONG, columns),
        whole(1, columns),
        whole(LONG, width),
        chunk_block(slots, share, width, chunk),
    ]
    specs += [whole(slots, 2 * QUEUE, width)] * 2 + [whole(8, columns // 2)] * 2
    aliases = {}
    if previous is not None:
        aliases = {len(ins): 1}
        kernel = without_previous(kernel, len(ins))
        ins.append(previous)
        specs.append(pl.BlockSpec(memory_space=pl.ANY))
    return call(
        kernel,
        f"unmix_{chunk}",
        (1,),
        specs,
        [whole(LONG, width), chunk_block(slots, share, width, chunk), whole(2 * slots, width)],
        [
            shape((LONG, width), BF),
            shape((slots, chunks, share, width), BF),
            shape((2 * slots, width), F32),
        ],
        (),
        (WAITING, 6e6, 0),
        aliases,
        limit=LARGE if columns > 1024 else SMALL,
    )(*ins)


def output_kernel(chunks, *refs):
    merged, out = refs[chunks:]
    for chunk in range(chunks):
        rows = merged[:, chunk].reshape(LONG, out.shape[1]).astype(F32)
        out[chunk * LONG : (chunk + 1) * LONG] = (refs[chunk][...].astype(F32) + rows).astype(BF)


def output_part(resids, merged):
    slots, chunks, share, width = merged.shape
    return call(
        functools.partial(output_kernel, chunks),
        "output",
        (1,),
        [whole(LONG, width)] * chunks + [whole(slots, chunks, share, width)],
        whole(chunks * LONG, width),
        shape((chunks * LONG, width), BF),
        cost=(0, 8e6, 0),
    )(*resids, merged)


def backward_kernel(pairs, begins, later, split, *refs):
    refs = list(refs)
    take = lambda count: [refs.pop(0) for _ in range(count)]
    if begins:
        back, resid, grad_output, gain_second = take(4)
    else:
        (resid_low,) = take(1)
    parts = take(len(pairs))
    normed, qkv, exps, inverse, attended = take(5)
    (weights_before,) = take(1) if later else (None,)
    weights_out = take(len(pairs) if split else 1)
    (grads_out,) = take(1)
    if begins:
        gains_out, low_out = take(2)
    normed_turned, o_now, grad_scores_all, exps_now, arrived = take(5)
    if begins:
        (resid_low,) = take(1)
    step = pl.program_id(0)
    pair_width = attended.shape[2]
    tiles = LONG // TILE

    def fetch(index):
        slot = lax.rem(index, 2)
        return pltpu.make_async_copy(exps.at[pairs[0] - index], exps_now.at[slot], arrived.at[slot])

    @pl.when(step == 0)
    def _():
        fetch(step).start()

    @pl.when(step + 1 < len(pairs))
    def _():
        fetch(step + 1).start()

    @pl.when(step == 0)
    def _():
        normed_turned[...] = normed[...].T
        if begins:
            unit, scaling = normalize(resid[...].astype(F32))
            through, gain_grad = normalize_back(
                back[...].astype(F32), gain_second[...], unit, scaling
            )
            gains_out[...] = gain_grad
            resid_low[...] = (grad_output[...].astype(F32) + through).astype(BF)

    for index, part in enumerate(parts):

        @pl.when(step == index)
        def _(part=part):
            o_now[...] = out_weights(part[...], o_now.shape[1])

    if begins:
        share = low_out.shape[0]
        low_out[...] = resid_low[pl.ds(pl.multiple_of(step * share, share), share), :]
    low = resid_low[...]
    fetch(step).wait()
    exps = exps_now.at[lax.rem(step, 2)]
    grad_attended = dot_cols(low, o_now[...]).astype(BF)
    grad_out_weights = dot_rows(attended[0], low)
    wide = grad_attended.astype(F32)
    inverted = inverse[0].astype(F32)
    scaled = wide * inverted
    products = scaled * attended[0].astype(F32)
    scaled = scaled.astype(BF)
    low_half, high_half = halves(BF)
    low_wide, high_wide = halves(F32)
    queries = qkv[0, :, :pair_width] * BF(HEAD_DIM**-0.5)
    key_rows = qkv[0, :, pair_width : 2 * pair_width]
    value_rows = qkv[0, :, 2 * pair_width :]
    scaled_keys = key_rows * BF(HEAD_DIM**-0.5)
    queries_turned = queries.T
    grads_turned = scaled.T
    ones = (high_half, low_half)
    joined_q, joined_k, joined_v = [], [], []
    for head, (half, half_wide) in enumerate(((low_half, low_wide), (high_half, high_wide))):
        head_grads = scaled * half
        head_keys = scaled_keys * half
        deltas = jnp.sum(products * half_wide, axis=1, keepdims=True)
        part = slice(head * HEAD_DIM, (head + 1) * HEAD_DIM)
        query_rows = []
        for row_tile in range(tiles):
            begin, extent = row_tile * TILE, (row_tile + 1) * TILE
            powers = jnp.concatenate(
                [exps[head, tile_slot(row_tile, col_tile)] for col_tile in range(row_tile + 1)],
                axis=1,
            )
            grad_probs = dot_cols(head_grads[begin:extent], value_rows[:extent])
            grad_scores = (powers.astype(F32) * (grad_probs - deltas[begin:extent])).astype(BF)
            grad_scores_all[begin:extent, :extent] = grad_scores
            query_rows.append(dot(grad_scores, head_keys[:extent]))
        joined_q.append(jnp.concatenate(query_rows, axis=0))
        key_cols, value_cols = [], []
        for col_tile in range(tiles):
            begin, extent = col_tile * TILE, (col_tile + 1) * TILE
            powers = jnp.concatenate(
                [exps[head, tile_slot(row_tile, col_tile)] for row_tile in range(col_tile, tiles)],
                axis=0,
            )
            key_cols.append(dot(queries_turned[part, begin:], grad_scores_all[begin:, begin:extent]))
            value_cols.append(dot(grads_turned[part, begin:], powers))
        joined_k.append(jnp.concatenate(key_cols, axis=1))
        joined_v.append(jnp.concatenate(value_cols, axis=1))
    grads = jnp.concatenate(
        [
            (joined_q[0] + joined_q[1]).astype(BF),
            jnp.concatenate(joined_k, axis=0).T.astype(BF),
            jnp.concatenate(joined_v, axis=0).T.astype(BF),
        ],
        axis=1,
    )
    grads_out[0] = grads
    grad_weights = dot(normed_turned[...], grads)
    width = normed.shape[1]
    blocks = [grad_weights[:, index * pair_width : (index + 1) * pair_width] for index in range(3)]
    blocks += [
        grad_out_weights[:, index * pair_width : (index + 1) * pair_width]
        for index in range(width // pair_width)
    ]
    def store(out):
        begin = 0
        for block in blocks:
            extent = begin + block.shape[0]
            if later:
                block = block + weights_before[0, begin:extent].astype(F32)
            out[begin:extent] = block.astype(BF)
            begin = extent

    if split:
        for index, out in enumerate(weights_out):

            @pl.when(step == index)
            def _(out=out):
                store(out)

    else:
        store(weights_out[0].at[0])


def backward_part(chunk, pairs, start, low, parts, saved, before, split):
    exps = saved[2]
    width = saved[0].shape[1]
    packed, pair_width = parts[0].shape
    triple = 3 * pair_width
    kept = exps.shape[2]
    first = pairs[0]
    per_pair = lambda *dims: pl.BlockSpec((1,) + dims, lambda i: (first - i,) + (0,) * len(dims))
    rows = whole(LONG, width)
    begins, later = start is not None, before is not None
    if begins:
        ins = [*start]
        specs = [rows, rows, pl.BlockSpec((LONG, width), lambda i: (chunk, 0)), whole(1, width)]
    else:
        ins, specs = [low], [rows]
    ins += [parts[pair] for pair in pairs] + list(saved)
    out_part = pl.BlockSpec((width, pair_width), lambda i: (packed // width - 1, 0))
    specs += [out_part] * len(pairs)
    specs += [
        rows,
        per_pair(LONG, triple),
        pl.BlockSpec(memory_space=pl.ANY),
        per_pair(LONG, pair_width),
        per_pair(LONG, pair_width),
    ]
    if later:
        ins.append(before)
        specs.append(per_pair(packed, pair_width))
    count = len(pairs) if split else 1
    if split:
        out_specs = [whole(packed, pair_width)] * count
        outs = [shape((packed, pair_width), BF)] * count
    else:
        out_specs = [per_pair(packed, pair_width)]
        outs = [shape((len(pairs), packed, pair_width), BF)]
    out_specs.append(pl.BlockSpec((1, LONG, triple), lambda i: (i, 0, 0)))
    outs.append(shape((len(pairs), LONG, triple), BF))
    if begins:
        out_specs += [whole(1, width), pl.BlockSpec((LONG // len(pairs), width), lambda i: (i, 0))]
        outs += [shape((1, width), F32), shape((LONG, width), BF)]
    results = call(
        functools.partial(backward_kernel, pairs, begins, later, split),
        f"backward_{chunk}_{first}",
        (len(pairs),),
        specs,
        out_specs,
        outs,
        [
            pltpu.VMEM((width, LONG), BF),
            pltpu.VMEM((pair_width, width), BF),
            pltpu.VMEM((LONG, LONG), BF),
            pltpu.VMEM((2, 2, kept, TILE, TILE), BF),
            pltpu.SemaphoreType.DMA((2,)),
        ]
        + [pltpu.VMEM((LONG, width), BF)] * begins,
        (6e9 * len(pairs), 6e6 * len(pairs), 0),
        limit=LARGE,
    )(*ins)
    weights = dict(zip(pairs, results)) if split else results[0]
    return weights, results[count], results[count + 1 :]


def finish_kernel(groups, cuts, sent, *refs):
    chunks = len(groups)
    refs = list(refs)
    take = lambda count: [refs.pop(0) for _ in range(count)]
    tokens, gain_first = take(2)
    controls, gains, (bias_e, bias_r) = take(chunks), take(chunks), take(2)
    parts = take(sum(len(group) for group in groups[0]))
    grads = [take(len(groups[chunk])) for chunk in range(chunks)]
    resids = take(chunks)
    grad_tokens, small, weights = refs
    experts = controls[0].shape[0]
    step = pl.program_id(0)
    width = tokens.shape[1]
    pairs, triple = len(parts), weights.shape[1] // len(parts)

    @pl.when(step == 0)
    def _():
        small[...] = jnp.zeros_like(small)
        small[:experts] = sum(part[...] for part in controls)
        small[experts + 1 : experts + 2] = sum(part[...] for part in gains)
        for block in range(bias_e.shape[1] // width):
            begin = sent + block
            small[begin : begin + 1] = bias_e[:, block * width : (block + 1) * width]
        small[begin + 1 : begin + 2] = bias_r[...]
        for pair, part in enumerate(parts):
            cut = triple // 3
            for block in range(3):
                begin = pair * triple + block * cut
                weights[:, begin : begin + cut] = part[block * width : (block + 1) * width]

    for chunk in range(chunks):

        @pl.when(step // cuts == chunk)
        def _(chunk=chunk):
            columns = {}
            for group, ref in zip(groups[chunk], grads[chunk]):
                for index, pair in enumerate(group):
                    columns[pair] = ref[index]
            joined = jnp.concatenate([columns[pair] for pair in range(pairs)], axis=1)
            unit, scaling = normalize(tokens[...].astype(F32))
            through, gain_grad = normalize_back(
                dot_cols(joined, weights[...]), gain_first[...], unit, scaling
            )
            small[experts : experts + 1] += gain_grad
            grad_tokens[...] = resids[chunk][...].astype(F32) + through


def finish_part(tokens, gain_first, smalls, sent, parts, groups, grads, resids):
    total, width = tokens.shape
    chunks = total // LONG
    packed, pair_width = parts[0].shape
    cuts = 2
    share = LONG // cuts
    hidden = smalls[-2].shape[1]
    count = -(-(sent + hidden // width + 1) // 8) * 8
    rows = pl.BlockSpec((share, width), lambda i: (i, 0))
    flat = [(chunk, ref) for chunk, refs in enumerate(grads) for ref in refs]
    place = lambda chunk: lambda i: jnp.clip(i - chunk * cuts, 0, cuts - 1)
    grad_block = lambda chunk, ref: pl.BlockSpec(
        (ref.shape[0], share, ref.shape[2]), lambda i: (0, place(chunk)(i), 0)
    )
    resid_block = lambda chunk: pl.BlockSpec((share, width), lambda i: (place(chunk)(i), 0))
    return call(
        functools.partial(finish_kernel, groups, cuts, sent),
        "finish",
        (chunks * cuts,),
        [rows, whole(1, width)]
        + [whole(*part.shape) for part in smalls]
        + [whole(packed, pair_width)] * len(parts)
        + [grad_block(chunk, ref) for chunk, ref in flat]
        + [resid_block(chunk) for chunk in range(chunks)],
        [rows, whole(count, width)],
        [shape((total, width), F32), shape((count, width), F32)],
        [pltpu.VMEM((width, 3 * pair_width * len(parts)), BF)],
        (2 * total * width * 3 * pair_width * len(parts), 2e7, 0),
        limit=LARGE,
    )(tokens, gain_first, *smalls, *parts, *[ref for _, ref in flat], *resids)


def tail_pack_kernel(*refs):
    total = refs[0][...].astype(F32)
    for part in refs[1:-1]:
        total = total + part[...].astype(F32)
    refs[-1][...] = total.astype(BF)


def tail_pack(parts):
    rows, cut = parts[0].shape
    return call(
        tail_pack_kernel,
        "tail_pack",
        (1,),
        [whole(rows, cut)] * len(parts),
        whole(rows, cut),
        shape((rows, cut), BF),
        cost=(0, 3e6, 0),
    )(*parts)


def tail_sum_kernel(slots, pieces, out):
    total = pieces[0].astype(F32)
    for index in range(1, slots):
        total = total + pieces[index].astype(F32)
    out[...] = total.astype(BF)


def tail_sum(pieces):
    slots, share, cut = pieces.shape
    return call(
        functools.partial(tail_sum_kernel, slots),
        "tail_sum",
        (1,),
        [whole(slots, share, cut)],
        whole(share, cut),
        shape((share, cut), BF),
        cost=(0, 1e6, 0),
    )(pieces)


def small_sum_kernel(sent, *refs):
    *parts, out, bias_e, bias_r = refs
    small = tree_sum([part[...] for part in parts])
    out[...] = small[:sent]
    width = bias_r.shape[1]
    rows = bias_e.shape[1] // width
    for index in range(rows):
        bias_e[:, index * width : (index + 1) * width] = small[sent + index : sent + index + 1]
    bias_r[...] = small[sent + rows : sent + rows + 1]


def small_sum(smalls, sent, hidden):
    count, width = smalls[0].shape
    return call(
        functools.partial(small_sum_kernel, sent),
        "small_sum",
        (1,),
        [whole(count, width)] * len(smalls),
        [whole(sent, width), whole(1, hidden), whole(1, width)],
        [shape((sent, width), F32), shape((1, hidden), F32), shape((1, width), F32)],
        cost=(0, 1e5, 0),
    )(*smalls)


def tail_join_kernel(slots, own, came, own_small, came_small, out):
    share, cut = own.shape
    total = (own[...].astype(F32) + came[...].astype(F32)).astype(BF)
    small = own_small[...] + came_small[...]
    packed = jnp.concatenate(
        [small[:, begin : begin + cut] for begin in range(0, small.shape[1], cut)], axis=0
    ).astype(BF)
    for index in range(slots):
        out[index, :share] = total
        out[index, share:] = packed


def tail_join(own, came, own_small, came_small, slots):
    share, cut = own.shape
    sent, width = own_small.shape
    rows = share + sent * width // cut
    return call(
        functools.partial(tail_join_kernel, slots),
        "tail_join",
        (1,),
        [whole(share, cut)] * 2 + [whole(sent, width)] * 2,
        whole(slots, rows, cut),
        shape((slots, rows, cut), BF),
        cost=(0, 2e6, 0),
    )(own, came, own_small, came_small)


def gather_kernel(slots, share, pieces, *refs):
    outs, gain_first, gain_second, control, total = refs[:4], refs[4], refs[5], refs[6], refs[7]
    for index in range(slots):
        total[index * share : (index + 1) * share] = pieces[index, :share].astype(F32)
    cut = total.shape[1]
    begin = 0
    for out in outs[:3]:
        out[...] = total[begin : begin + out.shape[0]]
        begin += out.shape[0]
    last = outs[3]
    blocks = last.shape[1] // cut
    for index in range(blocks):
        last[:, index * cut : (index + 1) * cut] = total[begin : begin + last.shape[0]]
        begin += last.shape[0]
    small = pieces[0, share:].astype(F32)
    for index in range(1, slots):
        small = small + pieces[index, share:].astype(F32)
    count = small.shape[0] // blocks
    small = jnp.concatenate(
        [small[index * count : (index + 1) * count] for index in range(blocks)], axis=1
    )
    experts = control.shape[0]
    gain_first[...] = small[experts : experts + 1]
    gain_second[...] = small[experts + 1 : experts + 2]
    control[...] = small[:experts]


def gather_weights(pieces, share, width, experts):
    slots, _, cut = pieces.shape
    outs = [(width, cut)] * 3 + [(cut, width), (1, width), (1, width), (experts, width)]
    return call(
        functools.partial(gather_kernel, slots, share),
        "gather_weights",
        (1,),
        [whole(*pieces.shape)],
        [whole(*dims) for dims in outs],
        [shape(dims, F32) for dims in outs],
        [pltpu.VMEM((share * slots, cut), F32)],
        (0, 3e6, 0),
    )(pieces)


def partner(value, axis, offset):
    count = lax.axis_size(axis)
    return lax.ppermute(value, axis, [(index, index ^ offset) for index in range(count)])


def exchange(value, axis):
    return lax.all_to_all(value, axis, 0, 0, tiled=True)


def tree_sum(parts):
    while len(parts) > 1:
        parts = [parts[index] + parts[index + 1] for index in range(0, len(parts), 2)]
    return parts[0]


def gather_head(part):
    sibling = partner(part, "head", 1)
    across = partner(part, "head", 2)
    return [part, sibling, across, partner(across, "head", 1)]


def add_low(*parts):
    return sum(part.astype(F32) for part in parts).astype(BF)


def after(value, *earlier):
    return lax.optimization_barrier((value, *earlier))[0]


def body(
    tokens,
    gain_first,
    w_query,
    w_key,
    w_value,
    w_out,
    gain_second,
    w_control,
    w_expand,
    b_expand,
    w_reduce,
    b_reduce,
    lengths,
    grad_output,
):
    rows_local, width = tokens.shape
    pair_width = w_query.shape[1]
    slots = lax.axis_size("quarter")
    half = lax.axis_index("half")
    chunks = rows_local // LONG
    place = [lax.axis_index("quarter"), lax.axis_index("head"), half]
    place = jnp.stack(place).astype(jnp.int32)
    gain_first = gain_first[None]
    gain_second = gain_second[None]
    parts = gather_head(pack_weights(w_query, w_key, w_value, w_out))
    experts = w_control.shape[1]
    swapped = jnp.concatenate([w_control[:, slots:], w_control[:, :slots]], axis=1)
    control = jnp.repeat(jnp.where(half == 0, w_control, swapped), QUEUE, axis=1)
    cotangents = exchange(pack_rows(grad_output, slots), "quarter")

    forwards, members = [], []
    for chunk in range(chunks):
        *saved, second = forward_part(
            chunk, place, lengths, tokens, gain_first, parts, gain_second
        )
        gain_first = after(gain_first, second)
        forwards.append(saved)
        second = after(second, cotangents)
        members.append(exchange(second, "quarter"))
    mixings, arrivals, last = [], [], second
    for chunk in range(chunks):
        mixing, stats, kept, sent = mixing_part(
            chunk, control, members[chunk], cotangents
        )
        mixings.append(mixing)
        last = sent
        arrivals.append((kept, partner(sent, "half", 1), stats, partner(stats, "half", 1)))
    weights, combined, answers, sums, saved_experts = [], [], [], [], []
    for chunk in range(chunks):
        kept, *others = arrivals[chunk]
        messages, weight = combine_part(chunk, after(kept, last), *others)
        weights.append(weight)
        combined.append(messages)
        last = messages
        if chunk:
            sums.append(column_part(chunk - 1, combined[-2], answers[-1]))
        messages = exchange(messages, "quarter")
        flat = messages.reshape(-1, width)
        replies, *saved = expert_part(
            chunk, flat, w_expand, b_expand, w_reduce, b_reduce
        )
        last = replies
        saved_experts.append((flat, *saved))
        replies = exchange(replies.reshape(messages.shape), "quarter")
        answers.append(replies)
    own, other, bias_e, bias_r = expert_weights(place, saved_experts)
    backs, merged, controls = [], None, []
    for chunk in range(chunks):
        if chunk == chunks - 1:
            sums.append(column_part(chunk, combined[-1], answers[-1]))
        back, merged, grad_control = unmix_part(
            chunk,
            place,
            control,
            mixings[chunk],
            weights[chunk],
            members[chunk],
            cotangents,
            (answers[chunk], partner(sums[chunk][1], "half", 1)),
            (sums[chunk][0], partner(sums[chunk][0], "half", 1)),
            merged,
        )
        backs.append(exchange(back, "quarter"))
        controls.append(grad_control)
    own = add_low(own, partner(other, "head", 1))
    backs[0] = after(backs[0], back, own)
    across = partner(own, "head", 2)
    placed = (own, across, partner(own, "head", 1), partner(across, "head", 1))

    pairs = tuple(reversed(range(len(parts))))
    early, late = pairs[: len(pairs) // 2], pairs[len(pairs) // 2 :]
    before, gains, groups, grads, resids = None, [], [], [], []
    for chunk in range(chunks):
        *saved, resid = forwards[chunk]
        back = backs[chunk]
        if chunk == chunks - 1:
            if gains:
                merged = after(merged, gains[-1])
            merged = exchange(merged, "quarter")
            start = (back, resid, grad_output, gain_second)
            first_weights, first_grads, (gain, low) = backward_part(
                chunk, early, start, None, parts, saved, before, True
            )
            joint = add_low(first_weights[2], partner(first_weights[3], "head", 1))
            pieces = [partner(joint, "head", 2)]
            second_weights, second_grads, _ = backward_part(
                chunk, late, None, after(low, joint, across), parts, saved, before, True
            )
            groups.append((early, late))
            grads.append((first_grads, second_grads))
        else:
            start = (back, resid, grad_output, gain_second)
            before, chunk_grads, (gain, low) = backward_part(
                chunk, pairs, start, None, parts, saved, before, False
            )
            groups.append((pairs,))
            grads.append((chunk_grads,))
        gains.append(gain)
        resids.append(low)
    resids[-1] = after(resids[-1], *pieces)
    hidden = bias_e.shape[1]
    sent = -(-(experts + 2) // 8) * 8
    smalls = (*controls, *gains, bias_e, bias_r)
    grad_tokens, small = finish_part(
        tokens, gain_first, smalls, sent, parts, groups, grads, resids
    )

    pieces.append(partner(after(second_weights[1], *pieces), "head", 1))
    packed = tail_pack([second_weights[0]] + pieces)
    smalls = [small] + [partner(small, "head", index) for index in range(1, len(parts))]
    packed = after(packed, merged, *placed)
    pieces = exchange(packed, "quarter").reshape(slots, -1, pair_width)
    total = tail_sum(after(pieces, small))
    output = output_part([saved[5] for saved in forwards], after(merged, total))
    small, grad_expand_bias, grad_reduce_bias = small_sum(smalls, sent, hidden)
    pieces = tail_join(after(total, output), partner(total, "half", 1), small, partner(small, "half", 1), slots)
    pieces = exchange(pieces, "quarter")
    share = parts[0].shape[0] // slots
    *weights, gain_first, gain_second, control = gather_weights(pieces, share, width, experts)
    grad_query, grad_key, grad_value, grad_w_out = weights
    grad_expand, grad_reduce = place_weights(place, *placed)
    return (
        output,
        grad_tokens,
        gain_first[0],
        grad_query,
        grad_key,
        grad_value,
        grad_w_out,
        gain_second[0],
        control.T,
        grad_expand,
        grad_expand_bias,
        grad_reduce,
        grad_reduce_bias,
    )


def solution(mesh):
    in_specs = (
        P(SEQ + ("head",), None),
        P(),
        P(None, "head"),
        P(None, "head"),
        P(None, "head"),
        P("head", None),
        P(),
        P(),
        P(SEQ, None, None),
        P(SEQ, None),
        P(SEQ, None, None),
        P(SEQ, None),
        P(SEQ, None),
        P(SEQ + ("head",), None),
    )
    out_specs = (
        P(SEQ + ("head",), None),
        P(SEQ + ("head",), None),
        P(),
        P(None, "head"),
        P(None, "head"),
        P(None, "head"),
        P("head", None),
        P(),
        P(),
        P(SEQ, None, None),
        P(SEQ, None),
        P(SEQ, None, None),
        P(SEQ, None),
    )
    devices = mesh.devices
    count, heads = devices.shape
    mesh = jax.sharding.Mesh(devices.reshape(2, count // 2, heads), SEQ + ("head",))
    return jax.shard_map(body, mesh=mesh, in_specs=in_specs, out_specs=out_specs, check_vma=False)
```

```python
import functools
import jax
import jax.numpy as jnp
from jax import lax
from jax.sharding import PartitionSpec as P
from jax.experimental import pallas as pl
from jax.experimental.pallas import tpu as pltpu

HEAD_DIM = 64
GROUP = 32
LONG = 1024
TILE = 256
QUEUE = 2 * LONG // GROUP
SEQ = ("half", "quarter")
WAITING = 1.5e+10
EPSILON = 1e-05
MASKED = -1000000000.0
SAFE = 50.0
BF = jnp.bfloat16
F32 = jnp.float32
ROWS_BY_ROWS = (((0,), (0,)), ((), ()))
COLS_BY_COLS = (((1,), (1,)), ((), ()))
LARGE = 62 * 1024 * 1024
SMALL = 28 * 1024 * 1024


def dot(left, right):
    return jnp.dot(left, right, preferred_element_type=F32)


def dot_rows(left, right):
    return lax.dot_general(left, right, ROWS_BY_ROWS, preferred_element_type=F32)


def dot_cols(left, right):
    return lax.dot_general(left, right, COLS_BY_COLS, preferred_element_type=F32)


def normalize(matrix):
    centre = jnp.mean(matrix, axis=1, keepdims=True)
    shifted = matrix - centre
    scaling = lax.rsqrt(jnp.mean(shifted * shifted, axis=1, keepdims=True) + EPSILON)
    return shifted * scaling, scaling


def normalize_back(grad_norm, gain, unit_rows, scaling):
    inner_grad = grad_norm * gain
    centred = (
        inner_grad
        - jnp.mean(inner_grad, axis=1, keepdims=True)
        - unit_rows * jnp.mean(inner_grad * unit_rows, axis=1, keepdims=True)
    )
    return scaling * centred, jnp.sum(grad_norm * unit_rows, axis=0, keepdims=True)


def whole(*shape):
    return pl.BlockSpec(shape, lambda *_: (0,) * len(shape))


def scalars():
    return pl.BlockSpec(memory_space=pltpu.SMEM)


def call(kernel, name, grid, in_specs, out_specs, out_shape, scratch=(), cost=(0, 0, 0), aliases=None, limit=SMALL):
    return pl.pallas_call(
        kernel,
        grid=grid,
        in_specs=in_specs,
        out_specs=out_specs,
        out_shape=out_shape,
        scratch_shapes=list(scratch),
        input_output_aliases=aliases or {},
        cost_estimate=pl.CostEstimate(
            flops=int(cost[0]), bytes_accessed=int(cost[1]), transcendentals=int(cost[2])
        ),
        compiler_params=pltpu.CompilerParams(vmem_limit_bytes=limit),
        name=name,
    )


def shape(dims, dtype):
    return jax.ShapeDtypeStruct(dims, dtype)


def tile_slot(row_tile, col_tile):
    return row_tile * (row_tile + 1) // 2 + col_tile


def halves(dtype):
    lane = lax.broadcasted_iota(jnp.int32, (1, 2 * HEAD_DIM), 1)
    first = (lane < HEAD_DIM).astype(F32)
    return first.astype(dtype), (1.0 - first).astype(dtype)


def out_weights(part, width):
    cut = part.shape[1]
    base = part.shape[0] - width
    blocks = [part[base + begin : base + begin + cut] for begin in range(0, width, cut)]
    return jnp.concatenate(blocks, axis=1)


def forward_kernel(pairs, chunk, chunks, *refs):
    place, lengths, tokens, gain_first = refs[:4]
    parts = refs[4 : 4 + pairs]
    gain_second = refs[4 + pairs]
    normed_out, qkv_out, exps, inverse, attended, resid, second = refs[5 + pairs : 12 + pairs]
    normed, weights, bias, attended_all, arrived = refs[12 + pairs :]
    step = pl.program_id(0)
    width = tokens.shape[1]
    pair_width = attended.shape[2]
    fetches = [
        pltpu.make_async_copy(part, weights.at[index], arrived.at[index])
        for index, part in enumerate(parts)
    ]
    tiles = LONG // TILE

    @pl.when(step == 0)
    def _():
        for fetch in fetches:
            fetch.start()
        unit, _ = normalize(tokens[...].astype(F32))
        normed[...] = (unit * gain_first[...]).astype(BF)
        base = 4 * (place[1] * chunks + chunk)
        first = lengths[0, base]
        second_bound = first + lengths[0, base + 1]
        third = second_bound + lengths[0, base + 2]
        for row_tile in range(tiles):
            row = lax.broadcasted_iota(jnp.int32, (TILE, 1), 0) + row_tile * TILE
            begin = jnp.where(row >= first, first, 0)
            begin = jnp.where(row >= second_bound, second_bound, begin)
            begin = jnp.where(row >= third, third, begin)
            col = lax.broadcasted_iota(jnp.int32, (TILE, LONG), 1)
            allowed = (col <= row) & (col >= begin)
            bias[pl.ds(row_tile * TILE, TILE), :] = jnp.where(allowed, 0.0, MASKED)

    for index, fetch in enumerate(fetches):

        @pl.when(step == index)
        def _(fetch=fetch):
            fetch.wait()

    share = LONG // pairs
    normed_out[...] = normed[pl.ds(pl.multiple_of(step * share, share), share), :]
    own = weights[step, : 3 * width]
    own = jnp.concatenate([own[begin : begin + width] for begin in range(0, 3 * width, width)], axis=1)
    qkv = dot(normed[...], own).astype(BF)
    qkv_out[0] = qkv
    queries = qkv[:, :pair_width] * BF(HEAD_DIM**-0.5)
    key_rows = qkv[:, pair_width : 2 * pair_width]
    value_rows = qkv[:, 2 * pair_width :]
    low_half, high_half = halves(BF)
    is_low = lax.broadcasted_iota(jnp.int32, (TILE, pair_width), 1) < HEAD_DIM
    masks = ((low_half, high_half), (high_half, low_half))
    head_queries = [queries * own for own, other in masks]
    head_values = [value_rows * own + other for own, other in masks]
    pair_row = lax.broadcasted_iota(jnp.int32, (pair_width, pair_width), 0) // HEAD_DIM
    pair_col = lax.broadcasted_iota(jnp.int32, (pair_width, pair_width), 1) // HEAD_DIM
    same_half = (pair_row == pair_col).astype(F32).astype(BF)
    sizes = [
        jnp.max(dot(part * part, same_half), axis=0, keepdims=True) for part in (queries, key_rows)
    ]
    tame = jnp.max(sizes[0] * sizes[1]) < SAFE * SAFE

    def attend(shift):
        for row_tile in range(tiles):
            begin, extent = row_tile * TILE, (row_tile + 1) * TILE
            raw = []
            for head in range(2):
                scores = dot_cols(head_queries[head][begin:extent], key_rows[:extent])
                scores = scores + bias[begin:extent, :extent]
                if shift:
                    scores = scores - jnp.max(scores, axis=1, keepdims=True)
                powers = jnp.exp(scores).astype(BF)
                for col_tile in range(row_tile + 1):
                    exps[0, head, tile_slot(row_tile, col_tile)] = powers[
                        :, col_tile * TILE : (col_tile + 1) * TILE
                    ]
                raw.append(dot(powers, head_values[head][:extent]))
            totals = jnp.where(
                is_low, pltpu.roll(raw[0], HEAD_DIM, 1), pltpu.roll(raw[1], HEAD_DIM, 1)
            )
            inverted = 1.0 / totals
            inverse[0, begin:extent] = inverted.astype(BF)
            attended_tile = (jnp.where(is_low, raw[0], raw[1]) * inverted).astype(BF)
            attended[0, begin:extent] = attended_tile
            attended_all[step, begin:extent] = attended_tile

    @pl.when(tame)
    def _():
        attend(False)

    @pl.when(jnp.logical_not(tame))
    def _():
        attend(True)

    @pl.when(step == pairs - 1)
    def _():
        rows = jnp.concatenate([attended_all[index] for index in range(pairs)], axis=1)
        blocks = width // pair_width
        own = jnp.concatenate([out_weights(weights[index], width) for index in range(pairs)], axis=0)
        total = tokens[...].astype(F32) + dot(rows, own)
        resid[...] = total.astype(BF)
        unit, _ = normalize(total)
        second[...] = (unit * gain_second[...]).astype(BF)


def forward_part(chunk, place, lengths, tokens, gain_first, parts, gain_second):
    rows, width = tokens.shape
    pairs = len(parts)
    packed, pair_width = parts[0].shape
    triple = 3 * pair_width
    kept = LONG // TILE * (LONG // TILE + 1) // 2
    per_pair = lambda *dims: pl.BlockSpec((1,) + dims, lambda i: (i,) + (0,) * len(dims))
    return call(
        functools.partial(forward_kernel, pairs, chunk, rows // LONG),
        f"forward_{chunk}",
        (pairs,),
        [scalars(), scalars(), pl.BlockSpec((LONG, width), lambda i: (chunk, 0)), whole(1, width)]
        + [pl.BlockSpec(memory_space=pl.ANY)] * pairs
        + [whole(1, width)],
        [
            pl.BlockSpec((LONG // pairs, width), lambda i: (i, 0)),
            per_pair(LONG, triple),
            per_pair(2, kept, TILE, TILE),
            per_pair(LONG, pair_width),
            per_pair(LONG, pair_width),
            whole(LONG, width),
            whole(LONG, width),
        ],
        [
            shape((LONG, width), BF),
            shape((pairs, LONG, triple), BF),
            shape((pairs, 2, kept, TILE, TILE), BF),
            shape((pairs, LONG, pair_width), BF),
            shape((pairs, LONG, pair_width), BF),
            shape((LONG, width), BF),
            shape((LONG, width), BF),
        ],
        [
            pltpu.VMEM((LONG, width), BF),
            pltpu.VMEM((pairs, packed, pair_width), BF),
            pltpu.VMEM((LONG, LONG), F32),
            pltpu.VMEM((pairs, LONG, pair_width), BF),
            pltpu.SemaphoreType.DMA((pairs,)),
        ],
        (10e9, 25e6, 5e6),
        limit=LARGE,
    )(place, lengths, tokens, gain_first, *parts, gain_second)


def pack_kernel(rows, out, arrived):
    slots, chunks, share, _ = out.shape
    copies = []
    for chunk in range(chunks):
        for index in range(slots):
            begin = chunk * LONG + index * share
            copies.append(
                pltpu.make_async_copy(
                    rows.at[pl.ds(begin, share)], out.at[index, chunk], arrived.at[len(copies)]
                )
            )
    for copy in copies:
        copy.start()
    for copy in copies:
        copy.wait()


def pack_rows(rows, slots):
    total, width = rows.shape
    chunks, share = total // LONG, LONG // slots
    return call(
        pack_kernel,
        "pack_cotangent",
        (1,),
        [pl.BlockSpec(memory_space=pl.ANY)],
        pl.BlockSpec(memory_space=pl.ANY),
        shape((slots, chunks, share, width), BF),
        [pltpu.SemaphoreType.DMA((slots * chunks,))],
        (0, 4 * total * width, 0),
    )(rows)


def pack_weights_kernel(query, key, value, out, packed):
    width, cut = query.shape
    for index, part in enumerate((query, key, value)):
        packed[index * width : (index + 1) * width] = part[...]
    for index in range(width // cut):
        begin = 3 * width + index * cut
        packed[begin : begin + cut] = out[:, index * cut : (index + 1) * cut]


def pack_weights(query, key, value, out):
    width, cut = query.shape
    return call(
        pack_weights_kernel,
        "pack_weights",
        (1,),
        [whole(width, cut)] * 3 + [whole(cut, width)],
        whole(4 * width, cut),
        shape((4 * width, cut), BF),
        cost=(0, 16 * width * cut, 0),
    )(query, key, value, out)


def group_mask(slots, columns):
    share = LONG // slots
    stride = share // QUEUE
    row = lax.broadcasted_iota(jnp.int32, (LONG, columns), 0)
    col = lax.broadcasted_iota(jnp.int32, (LONG, columns), 1)
    return ((row % share) // stride) == (col % QUEUE)


def chunk_block(slots, rows, width, chunk):
    return pl.BlockSpec((slots, 1, rows, width), lambda i: (0, chunk, 0, 0))


def mixing_kernel(slots, control, members, cotangents, mixing_out, stats, kept, sent):
    width, columns = control.shape
    rows = members[...]
    grads = cotangents[...].reshape(LONG, width)
    logits = jnp.where(group_mask(slots, columns), dot(rows, control[...]), -1e30)
    highest = jnp.max(logits, axis=0, keepdims=True)
    powers = jnp.exp(logits - highest)
    total = jnp.sum(powers, axis=0, keepdims=True)
    stats[0:1] = highest
    stats[1:2] = total
    low = (powers / total).astype(BF)
    mixing_out[...] = low
    mixed = dot_rows(low, rows).astype(BF)
    grad_out = dot_rows(low, grads).astype(BF)
    for index in range(slots):
        for out, begin in ((kept, index * QUEUE), (sent, (index + slots) * QUEUE)):
            out[index, :QUEUE] = mixed[begin : begin + QUEUE]
            out[index, QUEUE:] = grad_out[begin : begin + QUEUE]


def mixing_part(chunk, control, members, cotangents):
    slots, chunks, share, _ = cotangents.shape
    width, columns = control.shape
    return call(
        functools.partial(mixing_kernel, slots),
        f"mixing_{chunk}",
        (1,),
        [whole(width, columns), whole(LONG, width), chunk_block(slots, share, width, chunk)],
        [whole(LONG, columns), whole(2, columns)] + [whole(slots, 2 * QUEUE, width)] * 2,
        [shape((LONG, columns), BF), shape((2, columns), F32)]
        + [shape((slots, 2 * QUEUE, width), BF)] * 2,
        cost=(1e6, 1e4, 0),
        limit=LARGE if columns > 1024 else SMALL,
    )(control, members, cotangents)


def combine_kernel(slots, kept, came, own_stats, came_stats, messages, weights):
    columns = own_stats.shape[1]
    middle = columns // 2
    other = jnp.concatenate([came_stats[:, middle:], came_stats[:, :middle]], axis=1)
    highest = jnp.maximum(own_stats[0:1], other[0:1])
    own_total = own_stats[1:2] * jnp.exp(own_stats[0:1] - highest)
    other_total = other[1:2] * jnp.exp(other[0:1] - highest)
    own_share = own_total / (own_total + other_total)
    weights[...] = own_share
    turned = jnp.broadcast_to(own_share[:, :middle], (8, middle)).T
    for index in range(slots):
        share = turned[index * QUEUE : (index + 1) * QUEUE, 0:1]
        for begin in (0, QUEUE):
            part = slice(begin, begin + QUEUE)
            one = kept[index, part].astype(F32)
            two = came[index, part].astype(F32)
            messages[index, part] = (two + share * (one - two)).astype(BF)


def combine_part(chunk, kept, came, own_stats, came_stats):
    slots, rows, width = kept.shape
    columns = own_stats.shape[1]
    return call(
        functools.partial(combine_kernel, slots),
        f"combine_{chunk}",
        (1,),
        [whole(slots, rows, width)] * 2 + [whole(2, columns)] * 2,
        [whole(slots, rows, width), whole(1, columns)],
        [shape((slots, rows, width), BF), shape((1, columns), F32)],
        cost=(WAITING, 2e6, 0),
    )(kept, came, own_stats, came_stats)


def column_kernel(slots, messages, answers, out, again):
    again[...] = answers[...]
    sums = []
    for index in range(slots):
        mixed = messages[index, :QUEUE].astype(F32)
        grad_out = messages[index, QUEUE:].astype(F32)
        expert_out = answers[index, :QUEUE].astype(F32)
        grad_mixed = answers[index, QUEUE:].astype(F32)
        products = expert_out * grad_out + grad_mixed * mixed
        sums.append(jnp.sum(products, axis=1, keepdims=True))
    sums = jnp.concatenate(sums, axis=0)
    out[...] = jnp.broadcast_to(sums, (sums.shape[0], 8)).T


def column_part(chunk, messages, answers):
    slots, rows, width = messages.shape
    return call(
        functools.partial(column_kernel, slots),
        f"columns_{chunk}",
        (1,),
        [whole(slots, rows, width)] * 2,
        [whole(8, slots * QUEUE), whole(slots, rows, width)],
        [shape((8, slots * QUEUE), F32), shape((slots, rows, width), BF)],
        cost=(1e6, 1e4, 0),
    )(messages, answers)


def expert_kernel(slots, messages, w_expand, b_expand, w_reduce, b_reduce, *refs):
    answers, activated_out, grad_pre_out, taken, grads, out_sum, mixed_sum = refs
    step = pl.program_id(0)

    @pl.when(step == 0)
    def _():
        for index in range(slots):
            begin = 2 * QUEUE * index
            part = slice(index * QUEUE, (index + 1) * QUEUE)
            taken[part] = messages[begin : begin + QUEUE]
            grads[part] = messages[begin + QUEUE : begin + 2 * QUEUE]
        out_sum[...] = jnp.zeros_like(out_sum)
        mixed_sum[...] = jnp.zeros_like(mixed_sum)

    pre = dot(taken[...], w_expand[0]) + b_expand[...]
    slope = 0.7978845608028654
    square = pre * pre
    bend = jnp.tanh(slope * (pre + 0.044715 * (pre * square)))
    half = 0.5 * (1.0 + bend)
    activated = (pre * half).astype(BF)
    activated_out[...] = activated
    out_sum[...] += dot(activated, w_reduce[0])
    derivative = half + (0.5 * slope) * pre * (1.0 - bend * bend) * (1.0 + 0.134145 * square)
    grad_pre = (dot_cols(grads[...], w_reduce[0]) * derivative).astype(BF)
    grad_pre_out[...] = grad_pre
    mixed_sum[...] += dot_cols(grad_pre, w_expand[0])

    @pl.when(step == pl.num_programs(0) - 1)
    def _():
        for index in range(slots):
            begin = 2 * QUEUE * index
            part = slice(index * QUEUE, (index + 1) * QUEUE)
            answers[begin : begin + QUEUE] = (out_sum[part] + b_reduce[...]).astype(BF)
            answers[begin + QUEUE : begin + 2 * QUEUE] = mixed_sum[part].astype(BF)


def expert_part(chunk, messages, w_expand, b_expand, w_reduce, b_reduce):
    _, width, hidden = w_expand.shape
    count = messages.shape[0] // 2
    slots = count // QUEUE
    cut = min(512, hidden)
    outs = call(
        functools.partial(expert_kernel, slots),
        f"expert_{chunk}",
        (hidden // cut,),
        [
            whole(2 * count, width),
            pl.BlockSpec((1, width, cut), lambda i: (0, 0, i)),
            pl.BlockSpec((1, cut), lambda i: (0, i)),
            pl.BlockSpec((1, cut, width), lambda i: (0, i, 0)),
            whole(1, width),
        ],
        [
            whole(2 * count, width),
            pl.BlockSpec((count, cut), lambda i: (0, i)),
            pl.BlockSpec((count, cut), lambda i: (0, i)),
        ],
        [shape((2 * count, width), BF)] + [shape((count, hidden), BF)] * 2,
        [pltpu.VMEM((count, width), BF)] * 2 + [pltpu.VMEM((count, width), F32)] * 2,
        (1e6, 1e4, 0),
        limit=LARGE,
    )(messages, w_expand, b_expand, w_reduce, b_reduce)
    return outs


def expert_weights_kernel(chunks, place, *refs):
    messages, activated, grad_pre = refs[:chunks], refs[chunks : 2 * chunks], refs[2 * chunks : 3 * chunks]
    own, other, bias_e, bias_r, full_e, full_r = refs[3 * chunks :]
    join = lambda parts: jnp.concatenate(parts, axis=0)
    pick = lambda offset: join(
        [
            part[begin + offset : begin + offset + QUEUE]
            for part in messages
            for begin in range(0, part.shape[0], 2 * QUEUE)
        ]
    )
    taken, cotangent = pick(0), pick(QUEUE)
    pre = join([part[...] for part in grad_pre])
    full_e[...] = dot_rows(taken, pre).astype(BF)
    full_r[...] = dot_rows(join([part[...] for part in activated]), cotangent).astype(BF)
    bias_e[...] = jnp.sum(pre.astype(F32), axis=0, keepdims=True)
    bias_r[...] = jnp.sum(cotangent.astype(F32), axis=0, keepdims=True)
    begin = 0
    for full in (full_e, full_r):
        cut = full.shape[0] // 2
        for out, side in ((own, place[1] % 2), (other, 1 - place[1] % 2)):
            out[begin : begin + cut] = full[pl.ds(pl.multiple_of(side * cut, cut), cut), :]
        begin += cut


def expert_weights(place, kept):
    chunks = len(kept)
    messages, activated, grad_pre = zip(*kept)
    count, hidden = activated[0].shape
    width = messages[0].shape[1]
    cut = width
    wide = lambda rows: pl.BlockSpec((rows, cut), lambda i: (0, i))
    tall = pl.BlockSpec((cut, width), lambda i: (i, 0))
    return call(
        functools.partial(expert_weights_kernel, chunks),
        "expert_weights",
        (hidden // cut,),
        [scalars()] + [whole(2 * count, width)] * chunks + [wide(count)] * (2 * chunks),
        [tall, tall, wide(1), whole(1, width)],
        [shape((hidden, width), BF)] * 2 + [shape((1, hidden), F32), shape((1, width), F32)],
        [pltpu.VMEM((width, cut), BF), pltpu.VMEM((cut, width), BF)],
        (WAITING, 1e4, 0),
        limit=LARGE,
    )(place, *messages, *activated, *grad_pre)


def place_weights_kernel(place, own, own_across, other, other_across, out_e, out_r):
    begin = 0
    for out in (out_e, out_r):
        cut = out.shape[1] // 2
        part = slice(begin, begin + cut)
        for one, two, side in (
            (own, own_across, place[1] % 2),
            (other, other_across, 1 - place[1] % 2),
        ):
            total = one[part].astype(F32) + two[part].astype(F32)
            out[0, pl.ds(pl.multiple_of(side * cut, cut), cut), :] = total
        begin += cut


def place_weights(place, *parts):
    hidden, width = parts[0].shape
    cut = width
    tall = pl.BlockSpec((cut, width), lambda i: (i, 0))
    return call(
        place_weights_kernel,
        "place_expert_weights",
        (hidden // cut,),
        [scalars()] + [tall] * len(parts),
        [
            pl.BlockSpec((1, width, cut), lambda i: (0, 0, i)),
            pl.BlockSpec((1, cut, width), lambda i: (0, i, 0)),
        ],
        [shape((1, width, hidden), F32), shape((1, hidden, width), F32)],
        cost=(0, 16 * width * hidden, 0),
    )(place, *parts)


def unmix_kernel(slots, place, control, mixing_ref, weights, members, cotangents, *refs):
    own_answers, other_answers, own_sums, other_sums, back, merged, control_out = refs
    rows = members[...]
    grads = cotangents[...].reshape(rows.shape)
    pick = lambda part: jnp.concatenate(
        [answers[index, part] for answers in (own_answers, other_answers) for index in range(slots)],
        axis=0,
    )
    expert_out, grad_mixed = pick(slice(0, QUEUE)), pick(slice(QUEUE, 2 * QUEUE))
    mixing = mixing_ref[...].astype(F32) * weights[...]
    low = mixing.astype(BF)
    grad_mixing = dot_cols(grads, expert_out) + dot_cols(rows, grad_mixed)
    sums = jnp.concatenate([own_sums[0:1], other_sums[0:1]], axis=1)
    grad_logits = (mixing * (grad_mixing - sums)).astype(BF)
    back[...] = (dot(low, grad_mixed) + dot_cols(grad_logits, control[...])).astype(BF)
    merged[...] = dot(low, expert_out).astype(BF).reshape(merged.shape)
    grad_control = dot_rows(grad_logits, rows)
    for index in range(2 * slots):
        expert = place[2] * slots + index if index < slots else (1 - place[2]) * slots + index - slots
        control_out[pl.ds(expert, 1), :] = jnp.sum(
            grad_control[index * QUEUE : (index + 1) * QUEUE], axis=0, keepdims=True
        )


def without_previous(kernel, position):
    def inner(*refs):
        return kernel(*refs[:position], *refs[position + 1 :])

    return inner


def unmix_part(
    chunk, place, control, mixing, weights, members, cotangents, answers, sums, previous
):
    slots, chunks, share, width = cotangents.shape
    columns = control.shape[1]
    kernel = functools.partial(unmix_kernel, slots)
    ins = [place, control, mixing, weights, members, cotangents, *answers, *sums]
    specs = [
        scalars(),
        whole(width, columns),
        whole(LONG, columns),
        whole(1, columns),
        whole(LONG, width),
        chunk_block(slots, share, width, chunk),
    ]
    specs += [whole(slots, 2 * QUEUE, width)] * 2 + [whole(8, columns // 2)] * 2
    aliases = {}
    if previous is not None:
        aliases = {len(ins): 1}
        kernel = without_previous(kernel, len(ins))
        ins.append(previous)
        specs.append(pl.BlockSpec(memory_space=pl.ANY))
    return call(
        kernel,
        f"unmix_{chunk}",
        (1,),
        specs,
        [whole(LONG, width), chunk_block(slots, share, width, chunk), whole(2 * slots, width)],
        [
            shape((LONG, width), BF),
            shape((slots, chunks, share, width), BF),
            shape((2 * slots, width), F32),
        ],
        (),
        (WAITING, 6e6, 0),
        aliases,
        limit=LARGE,
    )(*ins)


def output_kernel(chunks, *refs):
    merged, out = refs[chunks:]
    for chunk in range(chunks):
        rows = merged[:, chunk].reshape(LONG, out.shape[1]).astype(F32)
        out[chunk * LONG : (chunk + 1) * LONG] = (refs[chunk][...].astype(F32) + rows).astype(BF)


def output_part(resids, merged):
    slots, chunks, share, width = merged.shape
    return call(
        functools.partial(output_kernel, chunks),
        "output",
        (1,),
        [whole(LONG, width)] * chunks + [whole(slots, chunks, share, width)],
        whole(chunks * LONG, width),
        shape((chunks * LONG, width), BF),
        cost=(0, 8e6, 0),
    )(*resids, merged)


def backward_kernel(pairs, begins, later, split, *refs):
    refs = list(refs)
    take = lambda count: [refs.pop(0) for _ in range(count)]
    if begins:
        back, resid, grad_output, gain_second = take(4)
    else:
        (resid_low,) = take(1)
    parts = take(len(pairs))
    normed, qkv, exps, inverse, attended = take(5)
    (weights_before,) = take(1) if later else (None,)
    weights_out = take(len(pairs) if split else 1)
    (grads_out,) = take(1)
    if begins:
        gains_out, low_out = take(2)
    normed_turned, o_now, grad_scores_all, exps_now, arrived = take(5)
    if begins:
        (resid_low,) = take(1)
    step = pl.program_id(0)
    pair_width = attended.shape[2]
    tiles = LONG // TILE

    def fetch(index):
        slot = lax.rem(index, 2)
        return pltpu.make_async_copy(exps.at[pairs[0] - index], exps_now.at[slot], arrived.at[slot])

    @pl.when(step == 0)
    def _():
        fetch(step).start()

    @pl.when(step + 1 < len(pairs))
    def _():
        fetch(step + 1).start()

    @pl.when(step == 0)
    def _():
        normed_turned[...] = normed[...].T
        if begins:
            unit, scaling = normalize(resid[...].astype(F32))
            through, gain_grad = normalize_back(
                back[...].astype(F32), gain_second[...], unit, scaling
            )
            gains_out[...] = gain_grad
            resid_low[...] = (grad_output[...].astype(F32) + through).astype(BF)

    for index, part in enumerate(parts):

        @pl.when(step == index)
        def _(part=part):
            o_now[...] = out_weights(part[...], o_now.shape[1])

    if begins:
        share = low_out.shape[0]
        low_out[...] = resid_low[pl.ds(pl.multiple_of(step * share, share), share), :]
    low = resid_low[...]
    fetch(step).wait()
    exps = exps_now.at[lax.rem(step, 2)]
    grad_attended = dot_cols(low, o_now[...]).astype(BF)
    grad_out_weights = dot_rows(attended[0], low)
    wide = grad_attended.astype(F32)
    inverted = inverse[0].astype(F32)
    scaled = wide * inverted
    products = scaled * attended[0].astype(F32)
    scaled = scaled.astype(BF)
    low_half, high_half = halves(BF)
    low_wide, high_wide = halves(F32)
    queries = qkv[0, :, :pair_width] * BF(HEAD_DIM**-0.5)
    key_rows = qkv[0, :, pair_width : 2 * pair_width]
    value_rows = qkv[0, :, 2 * pair_width :]
    scaled_keys = key_rows * BF(HEAD_DIM**-0.5)
    queries_turned = queries.T
    grads_turned = scaled.T
    ones = (high_half, low_half)
    joined_q, joined_k, joined_v = [], [], []
    both = []
    for head, (half, half_wide) in enumerate(((low_half, low_wide), (high_half, high_wide))):
        deltas = jnp.sum(products * half_wide, axis=1, keepdims=True)
        both.append((scaled * half, scaled_keys * half, deltas))
    query_rows = []
    for row_tile in range(tiles):
        begin, extent = row_tile * TILE, (row_tile + 1) * TILE
        total = None
        for head, (head_grads, head_keys, deltas) in enumerate(both):
            powers = jnp.concatenate(
                [exps[head, tile_slot(row_tile, col_tile)] for col_tile in range(row_tile + 1)],
                axis=1,
            )
            grad_probs = dot_cols(head_grads[begin:extent], value_rows[:extent])
            grad_scores = (powers.astype(F32) * (grad_probs - deltas[begin:extent])).astype(BF)
            grad_scores_all[head, begin:extent, :extent] = grad_scores
            product = dot(grad_scores, head_keys[:extent])
            total = product if total is None else total + product
        query_rows.append(total)
    joined_q = [jnp.concatenate(query_rows, axis=0)]
    for head in range(2):
        part = slice(head * HEAD_DIM, (head + 1) * HEAD_DIM)
        key_cols, value_cols = [], []
        for col_tile in range(tiles):
            begin, extent = col_tile * TILE, (col_tile + 1) * TILE
            powers = jnp.concatenate(
                [exps[head, tile_slot(row_tile, col_tile)] for row_tile in range(col_tile, tiles)],
                axis=0,
            )
            key_cols.append(
                dot(queries_turned[part, begin:], grad_scores_all[head, begin:, begin:extent])
            )
            value_cols.append(dot(grads_turned[part, begin:], powers))
        joined_k.append(jnp.concatenate(key_cols, axis=1))
        joined_v.append(jnp.concatenate(value_cols, axis=1))
    grads = jnp.concatenate(
        [
            joined_q[0].astype(BF),
            jnp.concatenate(joined_k, axis=0).T.astype(BF),
            jnp.concatenate(joined_v, axis=0).T.astype(BF),
        ],
        axis=1,
    )
    grads_out[0] = grads
    grad_weights = dot(normed_turned[...], grads)
    width = normed.shape[1]
    blocks = [grad_weights[:, index * pair_width : (index + 1) * pair_width] for index in range(3)]
    blocks += [
        grad_out_weights[:, index * pair_width : (index + 1) * pair_width]
        for index in range(width // pair_width)
    ]
    def store(out):
        begin = 0
        for block in blocks:
            extent = begin + block.shape[0]
            if later:
                block = block + weights_before[0, begin:extent].astype(F32)
            out[begin:extent] = block.astype(BF)
            begin = extent

    if split:
        for index, out in enumerate(weights_out):

            @pl.when(step == index)
            def _(out=out):
                store(out)

    else:
        store(weights_out[0].at[0])


def backward_part(chunk, pairs, start, low, parts, saved, before, split):
    exps = saved[2]
    width = saved[0].shape[1]
    packed, pair_width = parts[0].shape
    triple = 3 * pair_width
    kept = exps.shape[2]
    first = pairs[0]
    per_pair = lambda *dims: pl.BlockSpec((1,) + dims, lambda i: (first - i,) + (0,) * len(dims))
    rows = whole(LONG, width)
    begins, later = start is not None, before is not None
    if begins:
        ins = [*start]
        specs = [rows, rows, pl.BlockSpec((LONG, width), lambda i: (chunk, 0)), whole(1, width)]
    else:
        ins, specs = [low], [rows]
    ins += [parts[pair] for pair in pairs] + list(saved)
    out_part = pl.BlockSpec((width, pair_width), lambda i: (packed // width - 1, 0))
    specs += [out_part] * len(pairs)
    specs += [
        rows,
        per_pair(LONG, triple),
        pl.BlockSpec(memory_space=pl.ANY),
        per_pair(LONG, pair_width),
        per_pair(LONG, pair_width),
    ]
    if later:
        ins.append(before)
        specs.append(per_pair(packed, pair_width))
    count = len(pairs) if split else 1
    if split:
        out_specs = [whole(packed, pair_width)] * count
        outs = [shape((packed, pair_width), BF)] * count
    else:
        out_specs = [per_pair(packed, pair_width)]
        outs = [shape((len(pairs), packed, pair_width), BF)]
    out_specs.append(pl.BlockSpec((1, LONG, triple), lambda i: (i, 0, 0)))
    outs.append(shape((len(pairs), LONG, triple), BF))
    if begins:
        out_specs += [whole(1, width), pl.BlockSpec((LONG // len(pairs), width), lambda i: (i, 0))]
        outs += [shape((1, width), F32), shape((LONG, width), BF)]
    results = call(
        functools.partial(backward_kernel, pairs, begins, later, split),
        f"backward_{chunk}_{first}",
        (len(pairs),),
        specs,
        out_specs,
        outs,
        [
            pltpu.VMEM((width, LONG), BF),
            pltpu.VMEM((pair_width, width), BF),
            pltpu.VMEM((2, LONG, LONG), BF),
            pltpu.VMEM((2, 2, kept, TILE, TILE), BF),
            pltpu.SemaphoreType.DMA((2,)),
        ]
        + [pltpu.VMEM((LONG, width), BF)] * begins,
        (6e9 * len(pairs), 6e6 * len(pairs), 0),
        limit=LARGE,
    )(*ins)
    weights = dict(zip(pairs, results)) if split else results[0]
    return weights, results[count], results[count + 1 :]


def finish_kernel(groups, cuts, sent, *refs):
    chunks = len(groups)
    refs = list(refs)
    take = lambda count: [refs.pop(0) for _ in range(count)]
    tokens, gain_first = take(2)
    controls, gains, (bias_e, bias_r) = take(chunks), take(chunks), take(2)
    parts = take(sum(len(group) for group in groups[0]))
    grads = [take(len(groups[chunk])) for chunk in range(chunks)]
    resids = take(chunks)
    grad_tokens, small, weights = refs
    experts = controls[0].shape[0]
    step = pl.program_id(0)
    width = tokens.shape[1]
    pairs, triple = len(parts), weights.shape[1] // len(parts)

    @pl.when(step == 0)
    def _():
        small[...] = jnp.zeros_like(small)
        small[:experts] = sum(part[...] for part in controls)
        small[experts + 1 : experts + 2] = sum(part[...] for part in gains)
        for block in range(bias_e.shape[1] // width):
            begin = sent + block
            small[begin : begin + 1] = bias_e[:, block * width : (block + 1) * width]
        small[begin + 1 : begin + 2] = bias_r[...]
        for pair, part in enumerate(parts):
            cut = triple // 3
            for block in range(3):
                begin = pair * triple + block * cut
                weights[:, begin : begin + cut] = part[block * width : (block + 1) * width]

    for chunk in range(chunks):

        @pl.when(step // cuts == chunk)
        def _(chunk=chunk):
            columns = {}
            for group, ref in zip(groups[chunk], grads[chunk]):
                for index, pair in enumerate(group):
                    columns[pair] = ref[index]
            joined = jnp.concatenate([columns[pair] for pair in range(pairs)], axis=1)
            unit, scaling = normalize(tokens[...].astype(F32))
            through, gain_grad = normalize_back(
                dot_cols(joined, weights[...]), gain_first[...], unit, scaling
            )
            small[experts : experts + 1] += gain_grad
            grad_tokens[...] = resids[chunk][...].astype(F32) + through


def finish_part(tokens, gain_first, smalls, sent, parts, groups, grads, resids):
    total, width = tokens.shape
    chunks = total // LONG
    packed, pair_width = parts[0].shape
    cuts = 2
    share = LONG // cuts
    hidden = smalls[-2].shape[1]
    count = -(-(sent + hidden // width + 1) // 8) * 8
    rows = pl.BlockSpec((share, width), lambda i: (i, 0))
    flat = [(chunk, ref) for chunk, refs in enumerate(grads) for ref in refs]
    place = lambda chunk: lambda i: jnp.clip(i - chunk * cuts, 0, cuts - 1)
    grad_block = lambda chunk, ref: pl.BlockSpec(
        (ref.shape[0], share, ref.shape[2]), lambda i: (0, place(chunk)(i), 0)
    )
    resid_block = lambda chunk: pl.BlockSpec((share, width), lambda i: (place(chunk)(i), 0))
    return call(
        functools.partial(finish_kernel, groups, cuts, sent),
        "finish",
        (chunks * cuts,),
        [rows, whole(1, width)]
        + [whole(*part.shape) for part in smalls]
        + [whole(3 * width, pair_width)] * len(parts)
        + [grad_block(chunk, ref) for chunk, ref in flat]
        + [resid_block(chunk) for chunk in range(chunks)],
        [rows, whole(count, width)],
        [shape((total, width), F32), shape((count, width), F32)],
        [pltpu.VMEM((width, 3 * pair_width * len(parts)), BF)],
        (2 * total * width * 3 * pair_width * len(parts), 2e7, 0),
        limit=LARGE,
    )(tokens, gain_first, *smalls, *parts, *[ref for _, ref in flat], *resids)


def tail_pack_kernel(*refs):
    total = refs[0][...].astype(F32)
    for part in refs[1:-1]:
        total = total + part[...].astype(F32)
    refs[-1][...] = total.astype(BF)


def tail_pack(parts):
    rows, cut = parts[0].shape
    return call(
        tail_pack_kernel,
        "tail_pack",
        (1,),
        [whole(rows, cut)] * len(parts),
        whole(rows, cut),
        shape((rows, cut), BF),
        cost=(0, 3e6, 0),
    )(*parts)


def tail_sum_kernel(slots, pieces, out):
    total = pieces[0].astype(F32)
    for index in range(1, slots):
        total = total + pieces[index].astype(F32)
    out[...] = total.astype(BF)


def tail_sum(pieces):
    slots, share, cut = pieces.shape
    return call(
        functools.partial(tail_sum_kernel, slots),
        "tail_sum",
        (1,),
        [whole(slots, share, cut)],
        whole(share, cut),
        shape((share, cut), BF),
        cost=(0, 1e6, 0),
    )(pieces)


def small_sum_kernel(sent, *refs):
    *parts, out, bias_e, bias_r = refs
    small = tree_sum([part[...] for part in parts])
    out[...] = small[:sent]
    width = bias_r.shape[1]
    rows = bias_e.shape[1] // width
    for index in range(rows):
        bias_e[:, index * width : (index + 1) * width] = small[sent + index : sent + index + 1]
    bias_r[...] = small[sent + rows : sent + rows + 1]


def small_sum(smalls, sent, hidden):
    count, width = smalls[0].shape
    return call(
        functools.partial(small_sum_kernel, sent),
        "small_sum",
        (1,),
        [whole(count, width)] * len(smalls),
        [whole(sent, width), whole(1, hidden), whole(1, width)],
        [shape((sent, width), F32), shape((1, hidden), F32), shape((1, width), F32)],
        cost=(0, 1e5, 0),
    )(*smalls)


def tail_join_kernel(slots, own, came, own_small, came_small, out):
    share, cut = own.shape
    total = (own[...].astype(F32) + came[...].astype(F32)).astype(BF)
    small = own_small[...] + came_small[...]
    packed = jnp.concatenate(
        [small[:, begin : begin + cut] for begin in range(0, small.shape[1], cut)], axis=0
    ).astype(BF)
    for index in range(slots):
        out[index, :share] = total
        out[index, share:] = packed


def tail_join(own, came, own_small, came_small, slots):
    share, cut = own.shape
    sent, width = own_small.shape
    rows = share + sent * width // cut
    return call(
        functools.partial(tail_join_kernel, slots),
        "tail_join",
        (1,),
        [whole(share, cut)] * 2 + [whole(sent, width)] * 2,
        whole(slots, rows, cut),
        shape((slots, rows, cut), BF),
        cost=(0, 2e6, 0),
    )(own, came, own_small, came_small)


def gather_kernel(slots, share, pieces, *refs):
    outs, gain_first, gain_second, control, total = refs[:4], refs[4], refs[5], refs[6], refs[7]
    for index in range(slots):
        total[index * share : (index + 1) * share] = pieces[index, :share].astype(F32)
    cut = total.shape[1]
    begin = 0
    for out in outs[:3]:
        out[...] = total[begin : begin + out.shape[0]]
        begin += out.shape[0]
    last = outs[3]
    blocks = last.shape[1] // cut
    for index in range(blocks):
        last[:, index * cut : (index + 1) * cut] = total[begin : begin + last.shape[0]]
        begin += last.shape[0]
    small = pieces[0, share:].astype(F32)
    for index in range(1, slots):
        small = small + pieces[index, share:].astype(F32)
    count = small.shape[0] // blocks
    small = jnp.concatenate(
        [small[index * count : (index + 1) * count] for index in range(blocks)], axis=1
    )
    experts = control.shape[0]
    gain_first[...] = small[experts : experts + 1]
    gain_second[...] = small[experts + 1 : experts + 2]
    control[...] = small[:experts]


def gather_weights(pieces, share, width, experts):
    slots, _, cut = pieces.shape
    outs = [(width, cut)] * 3 + [(cut, width), (1, width), (1, width), (experts, width)]
    return call(
        functools.partial(gather_kernel, slots, share),
        "gather_weights",
        (1,),
        [whole(*pieces.shape)],
        [whole(*dims) for dims in outs],
        [shape(dims, F32) for dims in outs],
        [pltpu.VMEM((share * slots, cut), F32)],
        (0, 3e6, 0),
    )(pieces)


def partner(value, axis, offset):
    count = lax.axis_size(axis)
    return lax.ppermute(value, axis, [(index, index ^ offset) for index in range(count)])


def exchange(value, axis):
    return lax.all_to_all(value, axis, 0, 0, tiled=True)


def tree_sum(parts):
    while len(parts) > 1:
        parts = [parts[index] + parts[index + 1] for index in range(0, len(parts), 2)]
    return parts[0]


def gather_head(part):
    sibling = partner(part, "head", 1)
    across = partner(part, "head", 2)
    return [part, sibling, across, partner(across, "head", 1)]


def add_low(*parts):
    return sum(part.astype(F32) for part in parts).astype(BF)


def after(value, *earlier):
    return lax.optimization_barrier((value, *earlier))[0]


def body(
    tokens,
    gain_first,
    w_query,
    w_key,
    w_value,
    w_out,
    gain_second,
    w_control,
    w_expand,
    b_expand,
    w_reduce,
    b_reduce,
    lengths,
    grad_output,
):
    rows_local, width = tokens.shape
    pair_width = w_query.shape[1]
    slots = lax.axis_size("quarter")
    half = lax.axis_index("half")
    chunks = rows_local // LONG
    place = [lax.axis_index("quarter"), lax.axis_index("head"), half]
    place = jnp.stack(place).astype(jnp.int32)
    gain_first = gain_first[None]
    gain_second = gain_second[None]
    parts = gather_head(pack_weights(w_query, w_key, w_value, w_out))
    experts = w_control.shape[1]
    swapped = jnp.concatenate([w_control[:, slots:], w_control[:, :slots]], axis=1)
    control = jnp.repeat(jnp.where(half == 0, w_control, swapped), QUEUE, axis=1)
    cotangents = exchange(pack_rows(grad_output, slots), "quarter")

    forwards, members = [], []
    for chunk in range(chunks):
        *saved, second = forward_part(
            chunk, place, lengths, tokens, gain_first, parts, gain_second
        )
        gain_first = after(gain_first, second)
        forwards.append(saved)
        second = after(second, cotangents)
        members.append(exchange(second, "quarter"))
    mixings, arrivals, last = [], [], second
    for chunk in range(chunks):
        mixing, stats, kept, sent = mixing_part(
            chunk, control, members[chunk], cotangents
        )
        mixings.append(mixing)
        last = sent
        arrivals.append((kept, partner(sent, "half", 1), stats, partner(stats, "half", 1)))
    weights, combined, answers, sums, saved_experts = [], [], [], [], []
    for chunk in range(chunks):
        kept, *others = arrivals[chunk]
        messages, weight = combine_part(chunk, after(kept, last), *others)
        weights.append(weight)
        combined.append(messages)
        last = messages
        if chunk:
            sums.append(column_part(chunk - 1, combined[-2], answers[-1]))
        messages = exchange(messages, "quarter")
        flat = messages.reshape(-1, width)
        replies, *saved = expert_part(
            chunk, flat, w_expand, b_expand, w_reduce, b_reduce
        )
        last = replies
        saved_experts.append((flat, *saved))
        replies = exchange(replies.reshape(messages.shape), "quarter")
        answers.append(replies)
    own, other, bias_e, bias_r = expert_weights(place, saved_experts)
    backs, merged, controls = [], None, []
    for chunk in range(chunks):
        if chunk == chunks - 1:
            sums.append(column_part(chunk, combined[-1], answers[-1]))
        back, merged, grad_control = unmix_part(
            chunk,
            place,
            control,
            mixings[chunk],
            weights[chunk],
            members[chunk],
            cotangents,
            (answers[chunk], partner(sums[chunk][1], "half", 1)),
            (sums[chunk][0], partner(sums[chunk][0], "half", 1)),
            merged,
        )
        backs.append(exchange(back, "quarter"))
        controls.append(grad_control)
    own = add_low(own, partner(other, "head", 1))
    backs[0] = after(backs[0], back, own)
    across = partner(own, "head", 2)
    placed = (own, across, partner(own, "head", 1), partner(across, "head", 1))

    pairs = tuple(reversed(range(len(parts))))
    early, late = pairs[: len(pairs) // 2], pairs[len(pairs) // 2 :]
    before, gains, groups, grads, resids = None, [], [], [], []
    for chunk in range(chunks):
        *saved, resid = forwards[chunk]
        back = backs[chunk]
        if chunk == chunks - 1:
            if gains:
                merged = after(merged, gains[-1])
            merged = exchange(merged, "quarter")
            start = (back, resid, grad_output, gain_second)
            first_weights, first_grads, (gain, low) = backward_part(
                chunk, early, start, None, parts, saved, before, True
            )
            joint = add_low(first_weights[2], partner(first_weights[3], "head", 1))
            pieces = [partner(joint, "head", 2)]
            second_weights, second_grads, _ = backward_part(
                chunk, late, None, after(low, joint, across), parts, saved, before, True
            )
            groups.append((early, late))
            grads.append((first_grads, second_grads))
        else:
            start = (back, resid, grad_output, gain_second)
            before, chunk_grads, (gain, low) = backward_part(
                chunk, pairs, start, None, parts, saved, before, False
            )
            groups.append((pairs,))
            grads.append((chunk_grads,))
        gains.append(gain)
        resids.append(low)
    resids[-1] = after(resids[-1], *pieces)
    hidden = bias_e.shape[1]
    sent = -(-(experts + 2) // 8) * 8
    smalls = (*controls, *gains, bias_e, bias_r)
    grad_tokens, small = finish_part(
        tokens, gain_first, smalls, sent, parts, groups, grads, resids
    )

    pieces.append(partner(after(second_weights[1], *pieces), "head", 1))
    packed = tail_pack([second_weights[0]] + pieces)
    smalls = [small] + [partner(small, "head", index) for index in range(1, len(parts))]
    packed = after(packed, merged, *placed)
    pieces = exchange(packed, "quarter").reshape(slots, -1, pair_width)
    total = tail_sum(after(pieces, small))
    output = output_part([saved[5] for saved in forwards], after(merged, total))
    small, grad_expand_bias, grad_reduce_bias = small_sum(smalls, sent, hidden)
    pieces = tail_join(after(total, output), partner(total, "half", 1), small, partner(small, "half", 1), slots)
    pieces = exchange(pieces, "quarter")
    share = parts[0].shape[0] // slots
    *weights, gain_first, gain_second, control = gather_weights(pieces, share, width, experts)
    grad_query, grad_key, grad_value, grad_w_out = weights
    grad_expand, grad_reduce = place_weights(place, *placed)
    return (
        output,
        grad_tokens,
        gain_first[0],
        grad_query,
        grad_key,
        grad_value,
        grad_w_out,
        gain_second[0],
        control.T,
        grad_expand,
        grad_expand_bias,
        grad_reduce,
        grad_reduce_bias,
    )


def solution(mesh):
    in_specs = (
        P(SEQ + ("head",), None),
        P(),
        P(None, "head"),
        P(None, "head"),
        P(None, "head"),
        P("head", None),
        P(),
        P(),
        P(SEQ, None, None),
        P(SEQ, None),
        P(SEQ, None, None),
        P(SEQ, None),
        P(SEQ, None),
        P(SEQ + ("head",), None),
    )
    out_specs = (
        P(SEQ + ("head",), None),
        P(SEQ + ("head",), None),
        P(),
        P(None, "head"),
        P(None, "head"),
        P(None, "head"),
        P("head", None),
        P(),
        P(),
        P(SEQ, None, None),
        P(SEQ, None),
        P(SEQ, None, None),
        P(SEQ, None),
    )
    devices = mesh.devices
    count, heads = devices.shape
    mesh = jax.sharding.Mesh(devices.reshape(2, count // 2, heads), SEQ + ("head",))
    return jax.shard_map(body, mesh=mesh, in_specs=in_specs, out_specs=out_specs, check_vma=False)
```

```python
import functools
import jax
import jax.numpy as jnp
from jax import lax
from jax.sharding import PartitionSpec as P
from jax.experimental import pallas as pl
from jax.experimental.pallas import tpu as pltpu

HEAD_DIM = 64
GROUP = 32
LONG = 1024
TILE = 256
QUEUE = 2 * LONG // GROUP
SEQ = ("half", "quarter")
WAITING = 1e+10
EPSILON = 1e-05
MASKED = -1000000000.0
SAFE = 50.0
BF = jnp.bfloat16
F32 = jnp.float32
ROWS_BY_ROWS = (((0,), (0,)), ((), ()))
COLS_BY_COLS = (((1,), (1,)), ((), ()))
LARGE = 62 * 1024 * 1024
SMALL = 28 * 1024 * 1024


def dot(left, right):
    return jnp.dot(left, right, preferred_element_type=F32)


def dot_rows(left, right):
    return lax.dot_general(left, right, ROWS_BY_ROWS, preferred_element_type=F32)


def dot_cols(left, right):
    return lax.dot_general(left, right, COLS_BY_COLS, preferred_element_type=F32)


def normalize(matrix):
    centre = jnp.mean(matrix, axis=1, keepdims=True)
    shifted = matrix - centre
    scaling = lax.rsqrt(jnp.mean(shifted * shifted, axis=1, keepdims=True) + EPSILON)
    return shifted * scaling, scaling


def normalize_back(grad_norm, gain, unit_rows, scaling):
    inner_grad = grad_norm * gain
    centred = (
        inner_grad
        - jnp.mean(inner_grad, axis=1, keepdims=True)
        - unit_rows * jnp.mean(inner_grad * unit_rows, axis=1, keepdims=True)
    )
    return scaling * centred, jnp.sum(grad_norm * unit_rows, axis=0, keepdims=True)


def whole(*shape):
    return pl.BlockSpec(shape, lambda *_: (0,) * len(shape))


def scalars():
    return pl.BlockSpec(memory_space=pltpu.SMEM)


def call(kernel, name, grid, in_specs, out_specs, out_shape, scratch=(), cost=(0, 0, 0), aliases=None, limit=SMALL):
    return pl.pallas_call(
        kernel,
        grid=grid,
        in_specs=in_specs,
        out_specs=out_specs,
        out_shape=out_shape,
        scratch_shapes=list(scratch),
        input_output_aliases=aliases or {},
        cost_estimate=pl.CostEstimate(
            flops=int(cost[0]), bytes_accessed=int(cost[1]), transcendentals=int(cost[2])
        ),
        compiler_params=pltpu.CompilerParams(vmem_limit_bytes=limit),
        name=name,
    )


def shape(dims, dtype):
    return jax.ShapeDtypeStruct(dims, dtype)


def tile_slot(row_tile, col_tile):
    return row_tile * (row_tile + 1) // 2 + col_tile


def halves(dtype):
    lane = lax.broadcasted_iota(jnp.int32, (1, 2 * HEAD_DIM), 1)
    first = (lane < HEAD_DIM).astype(F32)
    return first.astype(dtype), (1.0 - first).astype(dtype)


def out_weights(part, width):
    cut = part.shape[1]
    base = part.shape[0] - width
    blocks = [part[base + begin : base + begin + cut] for begin in range(0, width, cut)]
    return jnp.concatenate(blocks, axis=1)


def forward_kernel(pairs, chunk, chunks, *refs):
    place, lengths, tokens, gain_first = refs[:4]
    parts = refs[4 : 4 + pairs]
    gain_second = refs[4 + pairs]
    normed_out, qkv_out, exps, inverse, attended, resid, second = refs[5 + pairs : 12 + pairs]
    normed, weights, bias, attended_all, arrived = refs[12 + pairs :]
    step = pl.program_id(0)
    width = tokens.shape[1]
    pair_width = attended.shape[2]
    fetches = [
        pltpu.make_async_copy(part, weights.at[index], arrived.at[index])
        for index, part in enumerate(parts)
    ]
    tiles = LONG // TILE

    @pl.when(step == 0)
    def _():
        for fetch in fetches:
            fetch.start()
        unit, _ = normalize(tokens[...].astype(F32))
        normed[...] = (unit * gain_first[...]).astype(BF)
        base = 4 * (place[1] * chunks + chunk)
        first = lengths[0, base]
        second_bound = first + lengths[0, base + 1]
        third = second_bound + lengths[0, base + 2]
        for row_tile in range(tiles):
            row = lax.broadcasted_iota(jnp.int32, (TILE, 1), 0) + row_tile * TILE
            begin = jnp.where(row >= first, first, 0)
            begin = jnp.where(row >= second_bound, second_bound, begin)
            begin = jnp.where(row >= third, third, begin)
            col = lax.broadcasted_iota(jnp.int32, (TILE, LONG), 1)
            allowed = (col <= row) & (col >= begin)
            bias[pl.ds(row_tile * TILE, TILE), :] = jnp.where(allowed, 0.0, MASKED)

    for index, fetch in enumerate(fetches):

        @pl.when(step == index)
        def _(fetch=fetch):
            fetch.wait()

    share = LONG // pairs
    normed_out[...] = normed[pl.ds(pl.multiple_of(step * share, share), share), :]
    own = weights[step, : 3 * width]
    own = jnp.concatenate([own[begin : begin + width] for begin in range(0, 3 * width, width)], axis=1)
    qkv = dot(normed[...], own).astype(BF)
    qkv_out[0] = qkv
    queries = qkv[:, :pair_width] * BF(HEAD_DIM**-0.5)
    key_rows = qkv[:, pair_width : 2 * pair_width]
    value_rows = qkv[:, 2 * pair_width :]
    low_half, high_half = halves(BF)
    is_low = lax.broadcasted_iota(jnp.int32, (TILE, pair_width), 1) < HEAD_DIM
    masks = ((low_half, high_half), (high_half, low_half))
    head_queries = [queries * own for own, other in masks]
    head_values = [value_rows * own + other for own, other in masks]
    pair_row = lax.broadcasted_iota(jnp.int32, (pair_width, pair_width), 0) // HEAD_DIM
    pair_col = lax.broadcasted_iota(jnp.int32, (pair_width, pair_width), 1) // HEAD_DIM
    same_half = (pair_row == pair_col).astype(F32).astype(BF)
    sizes = [
        jnp.max(dot(part * part, same_half), axis=0, keepdims=True) for part in (queries, key_rows)
    ]
    tame = jnp.max(sizes[0] * sizes[1]) < SAFE * SAFE

    def attend(shift):
        for row_tile in range(tiles):
            begin, extent = row_tile * TILE, (row_tile + 1) * TILE
            raw = []
            for head in range(2):
                scores = dot_cols(head_queries[head][begin:extent], key_rows[:extent])
                scores = scores + bias[begin:extent, :extent]
                if shift:
                    scores = scores - jnp.max(scores, axis=1, keepdims=True)
                powers = jnp.exp(scores).astype(BF)
                for col_tile in range(row_tile + 1):
                    exps[0, head, tile_slot(row_tile, col_tile)] = powers[
                        :, col_tile * TILE : (col_tile + 1) * TILE
                    ]
                raw.append(dot(powers, head_values[head][:extent]))
            totals = jnp.where(
                is_low, pltpu.roll(raw[0], HEAD_DIM, 1), pltpu.roll(raw[1], HEAD_DIM, 1)
            )
            inverted = 1.0 / totals
            inverse[0, begin:extent] = inverted.astype(BF)
            attended_tile = (jnp.where(is_low, raw[0], raw[1]) * inverted).astype(BF)
            attended[0, begin:extent] = attended_tile
            attended_all[step, begin:extent] = attended_tile

    @pl.when(tame)
    def _():
        attend(False)

    @pl.when(jnp.logical_not(tame))
    def _():
        attend(True)

    @pl.when(step == pairs - 1)
    def _():
        rows = jnp.concatenate([attended_all[index] for index in range(pairs)], axis=1)
        blocks = width // pair_width
        own = jnp.concatenate([out_weights(weights[index], width) for index in range(pairs)], axis=0)
        total = tokens[...].astype(F32) + dot(rows, own)
        resid[...] = total.astype(BF)
        unit, _ = normalize(total)
        second[...] = (unit * gain_second[...]).astype(BF)


def forward_part(chunk, place, lengths, tokens, gain_first, parts, gain_second):
    rows, width = tokens.shape
    pairs = len(parts)
    packed, pair_width = parts[0].shape
    triple = 3 * pair_width
    kept = LONG // TILE * (LONG // TILE + 1) // 2
    per_pair = lambda *dims: pl.BlockSpec((1,) + dims, lambda i: (i,) + (0,) * len(dims))
    return call(
        functools.partial(forward_kernel, pairs, chunk, rows // LONG),
        f"forward_{chunk}",
        (pairs,),
        [scalars(), scalars(), pl.BlockSpec((LONG, width), lambda i: (chunk, 0)), whole(1, width)]
        + [pl.BlockSpec(memory_space=pl.ANY)] * pairs
        + [whole(1, width)],
        [
            pl.BlockSpec((LONG // pairs, width), lambda i: (i, 0)),
            per_pair(LONG, triple),
            per_pair(2, kept, TILE, TILE),
            per_pair(LONG, pair_width),
            per_pair(LONG, pair_width),
            whole(LONG, width),
            whole(LONG, width),
        ],
        [
            shape((LONG, width), BF),
            shape((pairs, LONG, triple), BF),
            shape((pairs, 2, kept, TILE, TILE), BF),
            shape((pairs, LONG, pair_width), BF),
            shape((pairs, LONG, pair_width), BF),
            shape((LONG, width), BF),
            shape((LONG, width), BF),
        ],
        [
            pltpu.VMEM((LONG, width), BF),
            pltpu.VMEM((pairs, packed, pair_width), BF),
            pltpu.VMEM((LONG, LONG), F32),
            pltpu.VMEM((pairs, LONG, pair_width), BF),
            pltpu.SemaphoreType.DMA((pairs,)),
        ],
        (10e9, 25e6, 5e6),
        limit=LARGE,
    )(place, lengths, tokens, gain_first, *parts, gain_second)


def pack_kernel(rows, out, arrived):
    slots, chunks, share, _ = out.shape
    copies = []
    for chunk in range(chunks):
        for index in range(slots):
            begin = chunk * LONG + index * share
            copies.append(
                pltpu.make_async_copy(
                    rows.at[pl.ds(begin, share)], out.at[index, chunk], arrived.at[len(copies)]
                )
            )
    for copy in copies:
        copy.start()
    for copy in copies:
        copy.wait()


def pack_rows(rows, slots):
    total, width = rows.shape
    chunks, share = total // LONG, LONG // slots
    return call(
        pack_kernel,
        "pack_cotangent",
        (1,),
        [pl.BlockSpec(memory_space=pl.ANY)],
        pl.BlockSpec(memory_space=pl.ANY),
        shape((slots, chunks, share, width), BF),
        [pltpu.SemaphoreType.DMA((slots * chunks,))],
        (0, 4 * total * width, 0),
    )(rows)


def pack_weights_kernel(query, key, value, out, packed):
    width, cut = query.shape
    for index, part in enumerate((query, key, value)):
        packed[index * width : (index + 1) * width] = part[...]
    for index in range(width // cut):
        begin = 3 * width + index * cut
        packed[begin : begin + cut] = out[:, index * cut : (index + 1) * cut]


def pack_weights(query, key, value, out):
    width, cut = query.shape
    return call(
        pack_weights_kernel,
        "pack_weights",
        (1,),
        [whole(width, cut)] * 3 + [whole(cut, width)],
        whole(4 * width, cut),
        shape((4 * width, cut), BF),
        cost=(0, 16 * width * cut, 0),
    )(query, key, value, out)


def group_mask(slots, columns):
    share = LONG // slots
    stride = share // QUEUE
    row = lax.broadcasted_iota(jnp.int32, (LONG, columns), 0)
    col = lax.broadcasted_iota(jnp.int32, (LONG, columns), 1)
    return ((row % share) // stride) == (col % QUEUE)


def chunk_block(slots, rows, width, chunk):
    return pl.BlockSpec((slots, 1, rows, width), lambda i: (0, chunk, 0, 0))


def mixing_kernel(slots, control, members, cotangents, mixing_out, stats, kept, sent):
    width, columns = control.shape
    rows = members[...]
    grads = cotangents[...].reshape(LONG, width)
    logits = jnp.where(group_mask(slots, columns), dot(rows, control[...]), -1e30)
    highest = jnp.max(logits, axis=0, keepdims=True)
    powers = jnp.exp(logits - highest)
    total = jnp.sum(powers, axis=0, keepdims=True)
    stats[0:1] = highest
    stats[1:2] = total
    low = (powers / total).astype(BF)
    mixing_out[...] = low
    mixed = dot_rows(low, rows).astype(BF)
    grad_out = dot_rows(low, grads).astype(BF)
    for index in range(slots):
        for out, begin in ((kept, index * QUEUE), (sent, (index + slots) * QUEUE)):
            out[index, :QUEUE] = mixed[begin : begin + QUEUE]
            out[index, QUEUE:] = grad_out[begin : begin + QUEUE]


def mixing_part(chunk, control, members, cotangents):
    slots, chunks, share, _ = cotangents.shape
    width, columns = control.shape
    return call(
        functools.partial(mixing_kernel, slots),
        f"mixing_{chunk}",
        (1,),
        [whole(width, columns), whole(LONG, width), chunk_block(slots, share, width, chunk)],
        [whole(LONG, columns), whole(2, columns)] + [whole(slots, 2 * QUEUE, width)] * 2,
        [shape((LONG, columns), BF), shape((2, columns), F32)]
        + [shape((slots, 2 * QUEUE, width), BF)] * 2,
        cost=(1e6, 1e4, 0),
        limit=LARGE if columns > 1024 else SMALL,
    )(control, members, cotangents)


def combine_kernel(slots, kept, came, own_stats, came_stats, messages, weights):
    columns = own_stats.shape[1]
    middle = columns // 2
    other = jnp.concatenate([came_stats[:, middle:], came_stats[:, :middle]], axis=1)
    highest = jnp.maximum(own_stats[0:1], other[0:1])
    own_total = own_stats[1:2] * jnp.exp(own_stats[0:1] - highest)
    other_total = other[1:2] * jnp.exp(other[0:1] - highest)
    own_share = own_total / (own_total + other_total)
    weights[...] = own_share
    turned = jnp.broadcast_to(own_share[:, :middle], (8, middle)).T
    for index in range(slots):
        share = turned[index * QUEUE : (index + 1) * QUEUE, 0:1]
        for begin in (0, QUEUE):
            part = slice(begin, begin + QUEUE)
            one = kept[index, part].astype(F32)
            two = came[index, part].astype(F32)
            messages[index, part] = (two + share * (one - two)).astype(BF)


def combine_part(chunk, kept, came, own_stats, came_stats):
    slots, rows, width = kept.shape
    columns = own_stats.shape[1]
    return call(
        functools.partial(combine_kernel, slots),
        f"combine_{chunk}",
        (1,),
        [whole(slots, rows, width)] * 2 + [whole(2, columns)] * 2,
        [whole(slots, rows, width), whole(1, columns)],
        [shape((slots, rows, width), BF), shape((1, columns), F32)],
        cost=(WAITING, 2e6, 0),
    )(kept, came, own_stats, came_stats)


def column_kernel(slots, messages, answers, out, again):
    again[...] = answers[...]
    sums = []
    for index in range(slots):
        mixed = messages[index, :QUEUE].astype(F32)
        grad_out = messages[index, QUEUE:].astype(F32)
        expert_out = answers[index, :QUEUE].astype(F32)
        grad_mixed = answers[index, QUEUE:].astype(F32)
        products = expert_out * grad_out + grad_mixed * mixed
        sums.append(jnp.sum(products, axis=1, keepdims=True))
    sums = jnp.concatenate(sums, axis=0)
    out[...] = jnp.broadcast_to(sums, (sums.shape[0], 8)).T


def column_part(chunk, messages, answers):
    slots, rows, width = messages.shape
    return call(
        functools.partial(column_kernel, slots),
        f"columns_{chunk}",
        (1,),
        [whole(slots, rows, width)] * 2,
        [whole(8, slots * QUEUE), whole(slots, rows, width)],
        [shape((8, slots * QUEUE), F32), shape((slots, rows, width), BF)],
        cost=(1e6, 1e4, 0),
    )(messages, answers)


def expert_kernel(slots, messages, w_expand, b_expand, w_reduce, b_reduce, *refs):
    answers, activated_out, grad_pre_out, taken, grads, out_sum, mixed_sum = refs
    step = pl.program_id(0)

    @pl.when(step == 0)
    def _():
        for index in range(slots):
            begin = 2 * QUEUE * index
            part = slice(index * QUEUE, (index + 1) * QUEUE)
            taken[part] = messages[begin : begin + QUEUE]
            grads[part] = messages[begin + QUEUE : begin + 2 * QUEUE]
        out_sum[...] = jnp.zeros_like(out_sum)
        mixed_sum[...] = jnp.zeros_like(mixed_sum)

    pre = dot(taken[...], w_expand[0]) + b_expand[...]
    slope = 0.7978845608028654
    square = pre * pre
    bend = jnp.tanh(slope * (pre + 0.044715 * (pre * square)))
    half = 0.5 * (1.0 + bend)
    activated = (pre * half).astype(BF)
    activated_out[...] = activated
    out_sum[...] += dot(activated, w_reduce[0])
    derivative = half + (0.5 * slope) * pre * (1.0 - bend * bend) * (1.0 + 0.134145 * square)
    grad_pre = (dot_cols(grads[...], w_reduce[0]) * derivative).astype(BF)
    grad_pre_out[...] = grad_pre
    mixed_sum[...] += dot_cols(grad_pre, w_expand[0])

    @pl.when(step == pl.num_programs(0) - 1)
    def _():
        for index in range(slots):
            begin = 2 * QUEUE * index
            part = slice(index * QUEUE, (index + 1) * QUEUE)
            answers[begin : begin + QUEUE] = (out_sum[part] + b_reduce[...]).astype(BF)
            answers[begin + QUEUE : begin + 2 * QUEUE] = mixed_sum[part].astype(BF)


def expert_part(chunk, messages, w_expand, b_expand, w_reduce, b_reduce):
    _, width, hidden = w_expand.shape
    count = messages.shape[0] // 2
    slots = count // QUEUE
    cut = min(1024, hidden)
    outs = call(
        functools.partial(expert_kernel, slots),
        f"expert_{chunk}",
        (hidden // cut,),
        [
            whole(2 * count, width),
            pl.BlockSpec((1, width, cut), lambda i: (0, 0, i)),
            pl.BlockSpec((1, cut), lambda i: (0, i)),
            pl.BlockSpec((1, cut, width), lambda i: (0, i, 0)),
            whole(1, width),
        ],
        [
            whole(2 * count, width),
            pl.BlockSpec((count, cut), lambda i: (0, i)),
            pl.BlockSpec((count, cut), lambda i: (0, i)),
        ],
        [shape((2 * count, width), BF)] + [shape((count, hidden), BF)] * 2,
        [pltpu.VMEM((count, width), BF)] * 2 + [pltpu.VMEM((count, width), F32)] * 2,
        (1e6, 1e4, 0),
        limit=LARGE,
    )(messages, w_expand, b_expand, w_reduce, b_reduce)
    return outs


def expert_weights_kernel(chunks, place, *refs):
    messages, activated, grad_pre = refs[:chunks], refs[chunks : 2 * chunks], refs[2 * chunks : 3 * chunks]
    own, other, bias_e, bias_r, full_e, full_r = refs[3 * chunks :]
    join = lambda parts: jnp.concatenate(parts, axis=0)
    pick = lambda offset: join(
        [
            part[begin + offset : begin + offset + QUEUE]
            for part in messages
            for begin in range(0, part.shape[0], 2 * QUEUE)
        ]
    )
    taken, cotangent = pick(0), pick(QUEUE)
    pre = join([part[...] for part in grad_pre])
    full_e[...] = dot_rows(taken, pre).astype(BF)
    full_r[...] = dot_rows(join([part[...] for part in activated]), cotangent).astype(BF)
    bias_e[...] = jnp.sum(pre.astype(F32), axis=0, keepdims=True)
    bias_r[...] = jnp.sum(cotangent.astype(F32), axis=0, keepdims=True)
    begin = 0
    for full in (full_e, full_r):
        cut = full.shape[0] // 2
        for out, side in ((own, place[1] % 2), (other, 1 - place[1] % 2)):
            out[begin : begin + cut] = full[pl.ds(pl.multiple_of(side * cut, cut), cut), :]
        begin += cut


def expert_weights(place, kept):
    chunks = len(kept)
    messages, activated, grad_pre = zip(*kept)
    count, hidden = activated[0].shape
    width = messages[0].shape[1]
    cut = width
    wide = lambda rows: pl.BlockSpec((rows, cut), lambda i: (0, i))
    tall = pl.BlockSpec((cut, width), lambda i: (i, 0))
    return call(
        functools.partial(expert_weights_kernel, chunks),
        "expert_weights",
        (hidden // cut,),
        [scalars()] + [whole(2 * count, width)] * chunks + [wide(count)] * (2 * chunks),
        [tall, tall, wide(1), whole(1, width)],
        [shape((hidden, width), BF)] * 2 + [shape((1, hidden), F32), shape((1, width), F32)],
        [pltpu.VMEM((width, cut), BF), pltpu.VMEM((cut, width), BF)],
        (WAITING, 1e4, 0),
        limit=LARGE,
    )(place, *messages, *activated, *grad_pre)


def place_weights_kernel(place, own, own_across, other, other_across, out_e, out_r):
    begin = 0
    for out in (out_e, out_r):
        cut = out.shape[1] // 2
        part = slice(begin, begin + cut)
        for one, two, side in (
            (own, own_across, place[1] % 2),
            (other, other_across, 1 - place[1] % 2),
        ):
            total = one[part].astype(F32) + two[part].astype(F32)
            out[0, pl.ds(pl.multiple_of(side * cut, cut), cut), :] = total
        begin += cut


def place_weights(place, *parts):
    hidden, width = parts[0].shape
    cut = width
    tall = pl.BlockSpec((cut, width), lambda i: (i, 0))
    return call(
        place_weights_kernel,
        "place_expert_weights",
        (hidden // cut,),
        [scalars()] + [tall] * len(parts),
        [
            pl.BlockSpec((1, width, cut), lambda i: (0, 0, i)),
            pl.BlockSpec((1, cut, width), lambda i: (0, i, 0)),
        ],
        [shape((1, width, hidden), F32), shape((1, hidden, width), F32)],
        cost=(0, 16 * width * hidden, 0),
    )(place, *parts)


def unmix_kernel(slots, place, control, mixing_ref, weights, members, cotangents, *refs):
    own_answers, other_answers, own_sums, other_sums, back, merged, control_out = refs
    rows = members[...]
    grads = cotangents[...].reshape(rows.shape)
    pick = lambda part: jnp.concatenate(
        [answers[index, part] for answers in (own_answers, other_answers) for index in range(slots)],
        axis=0,
    )
    expert_out, grad_mixed = pick(slice(0, QUEUE)), pick(slice(QUEUE, 2 * QUEUE))
    mixing = mixing_ref[...].astype(F32) * weights[...]
    low = mixing.astype(BF)
    grad_mixing = dot_cols(grads, expert_out) + dot_cols(rows, grad_mixed)
    sums = jnp.concatenate([own_sums[0:1], other_sums[0:1]], axis=1)
    grad_logits = (mixing * (grad_mixing - sums)).astype(BF)
    back[...] = (dot(low, grad_mixed) + dot_cols(grad_logits, control[...])).astype(BF)
    merged[...] = dot(low, expert_out).astype(BF).reshape(merged.shape)
    grad_control = dot_rows(grad_logits, rows)
    for index in range(2 * slots):
        expert = place[2] * slots + index if index < slots else (1 - place[2]) * slots + index - slots
        control_out[pl.ds(expert, 1), :] = jnp.sum(
            grad_control[index * QUEUE : (index + 1) * QUEUE], axis=0, keepdims=True
        )


def without_previous(kernel, position):
    def inner(*refs):
        return kernel(*refs[:position], *refs[position + 1 :])

    return inner


def unmix_part(
    chunk, place, control, mixing, weights, members, cotangents, answers, sums, previous
):
    slots, chunks, share, width = cotangents.shape
    columns = control.shape[1]
    kernel = functools.partial(unmix_kernel, slots)
    ins = [place, control, mixing, weights, members, cotangents, *answers, *sums]
    specs = [
        scalars(),
        whole(width, columns),
        whole(LONG, columns),
        whole(1, columns),
        whole(LONG, width),
        chunk_block(slots, share, width, chunk),
    ]
    specs += [whole(slots, 2 * QUEUE, width)] * 2 + [whole(8, columns // 2)] * 2
    aliases = {}
    if previous is not None:
        aliases = {len(ins): 1}
        kernel = without_previous(kernel, len(ins))
        ins.append(previous)
        specs.append(pl.BlockSpec(memory_space=pl.ANY))
    return call(
        kernel,
        f"unmix_{chunk}",
        (1,),
        specs,
        [whole(LONG, width), chunk_block(slots, share, width, chunk), whole(2 * slots, width)],
        [
            shape((LONG, width), BF),
            shape((slots, chunks, share, width), BF),
            shape((2 * slots, width), F32),
        ],
        (),
        (WAITING, 6e6, 0),
        aliases,
        limit=LARGE,
    )(*ins)


def output_kernel(chunks, *refs):
    merged, out = refs[chunks:]
    for chunk in range(chunks):
        rows = merged[:, chunk].reshape(LONG, out.shape[1]).astype(F32)
        out[chunk * LONG : (chunk + 1) * LONG] = (refs[chunk][...].astype(F32) + rows).astype(BF)


def output_part(resids, merged):
    slots, chunks, share, width = merged.shape
    return call(
        functools.partial(output_kernel, chunks),
        "output",
        (1,),
        [whole(LONG, width)] * chunks + [whole(slots, chunks, share, width)],
        whole(chunks * LONG, width),
        shape((chunks * LONG, width), BF),
        cost=(0, 8e6, 0),
    )(*resids, merged)


def backward_kernel(pairs, begins, later, split, *refs):
    refs = list(refs)
    take = lambda count: [refs.pop(0) for _ in range(count)]
    if begins:
        back, resid, grad_output, gain_second = take(4)
    else:
        (resid_low,) = take(1)
    parts = take(len(pairs))
    normed, qkv, exps, inverse, attended = take(5)
    (weights_before,) = take(1) if later else (None,)
    weights_out = take(len(pairs) if split else 1)
    (grads_out,) = take(1)
    if begins:
        gains_out, low_out = take(2)
    normed_turned, o_now, grad_scores_all, exps_now, arrived = take(5)
    if begins:
        (resid_low,) = take(1)
    step = pl.program_id(0)
    pair_width = attended.shape[2]
    tiles = LONG // TILE

    def fetch(index):
        slot = lax.rem(index, 2)
        return pltpu.make_async_copy(exps.at[pairs[0] - index], exps_now.at[slot], arrived.at[slot])

    @pl.when(step == 0)
    def _():
        fetch(step).start()

    @pl.when(step + 1 < len(pairs))
    def _():
        fetch(step + 1).start()

    @pl.when(step == 0)
    def _():
        normed_turned[...] = normed[...].T
        if begins:
            unit, scaling = normalize(resid[...].astype(F32))
            through, gain_grad = normalize_back(
                back[...].astype(F32), gain_second[...], unit, scaling
            )
            gains_out[...] = gain_grad
            resid_low[...] = (grad_output[...].astype(F32) + through).astype(BF)

    for index, part in enumerate(parts):

        @pl.when(step == index)
        def _(part=part):
            o_now[...] = out_weights(part[...], o_now.shape[1])

    if begins:
        share = low_out.shape[0]
        low_out[...] = resid_low[pl.ds(pl.multiple_of(step * share, share), share), :]
    low = resid_low[...]
    fetch(step).wait()
    exps = exps_now.at[lax.rem(step, 2)]
    grad_attended = dot_cols(low, o_now[...]).astype(BF)
    grad_out_weights = dot_rows(attended[0], low)
    wide = grad_attended.astype(F32)
    inverted = inverse[0].astype(F32)
    scaled = wide * inverted
    products = scaled * attended[0].astype(F32)
    scaled = scaled.astype(BF)
    low_half, high_half = halves(BF)
    low_wide, high_wide = halves(F32)
    queries = qkv[0, :, :pair_width] * BF(HEAD_DIM**-0.5)
    key_rows = qkv[0, :, pair_width : 2 * pair_width]
    value_rows = qkv[0, :, 2 * pair_width :]
    scaled_keys = key_rows * BF(HEAD_DIM**-0.5)
    queries_turned = queries.T
    grads_turned = scaled.T
    ones = (high_half, low_half)
    joined_q, joined_k, joined_v = [], [], []
    both = []
    for head, (half, half_wide) in enumerate(((low_half, low_wide), (high_half, high_wide))):
        deltas = jnp.sum(products * half_wide, axis=1, keepdims=True)
        both.append((scaled * half, scaled_keys * half, deltas))
    query_rows = []
    for row_tile in range(tiles):
        begin, extent = row_tile * TILE, (row_tile + 1) * TILE
        total = None
        for head, (head_grads, head_keys, deltas) in enumerate(both):
            powers = jnp.concatenate(
                [exps[head, tile_slot(row_tile, col_tile)] for col_tile in range(row_tile + 1)],
                axis=1,
            )
            grad_probs = dot_cols(head_grads[begin:extent], value_rows[:extent])
            grad_scores = (powers.astype(F32) * (grad_probs - deltas[begin:extent])).astype(BF)
            grad_scores_all[head, begin:extent, :extent] = grad_scores
            product = dot(grad_scores, head_keys[:extent])
            total = product if total is None else total + product
        query_rows.append(total)
    joined_q = [jnp.concatenate(query_rows, axis=0)]
    for head in range(2):
        part = slice(head * HEAD_DIM, (head + 1) * HEAD_DIM)
        key_cols, value_cols = [], []
        for col_tile in range(tiles):
            begin, extent = col_tile * TILE, (col_tile + 1) * TILE
            powers = jnp.concatenate(
                [exps[head, tile_slot(row_tile, col_tile)] for row_tile in range(col_tile, tiles)],
                axis=0,
            )
            key_cols.append(
                dot(queries_turned[part, begin:], grad_scores_all[head, begin:, begin:extent])
            )
            value_cols.append(dot(grads_turned[part, begin:], powers))
        joined_k.append(jnp.concatenate(key_cols, axis=1))
        joined_v.append(jnp.concatenate(value_cols, axis=1))
    grads = jnp.concatenate(
        [
            joined_q[0].astype(BF),
            jnp.concatenate(joined_k, axis=0).T.astype(BF),
            jnp.concatenate(joined_v, axis=0).T.astype(BF),
        ],
        axis=1,
    )
    grads_out[0] = grads
    grad_weights = dot(normed_turned[...], grads)
    width = normed.shape[1]
    blocks = [grad_weights[:, index * pair_width : (index + 1) * pair_width] for index in range(3)]
    blocks += [
        grad_out_weights[:, index * pair_width : (index + 1) * pair_width]
        for index in range(width // pair_width)
    ]
    def store(out):
        begin = 0
        for block in blocks:
            extent = begin + block.shape[0]
            if later:
                block = block + weights_before[0, begin:extent].astype(F32)
            out[begin:extent] = block.astype(BF)
            begin = extent

    if split:
        for index, out in enumerate(weights_out):

            @pl.when(step == index)
            def _(out=out):
                store(out)

    else:
        store(weights_out[0].at[0])


def backward_part(chunk, pairs, start, low, parts, saved, before, split):
    exps = saved[2]
    width = saved[0].shape[1]
    packed, pair_width = parts[0].shape
    triple = 3 * pair_width
    kept = exps.shape[2]
    first = pairs[0]
    per_pair = lambda *dims: pl.BlockSpec((1,) + dims, lambda i: (first - i,) + (0,) * len(dims))
    rows = whole(LONG, width)
    begins, later = start is not None, before is not None
    if begins:
        ins = [*start]
        specs = [rows, rows, pl.BlockSpec((LONG, width), lambda i: (chunk, 0)), whole(1, width)]
    else:
        ins, specs = [low], [rows]
    ins += [parts[pair] for pair in pairs] + list(saved)
    out_part = pl.BlockSpec((width, pair_width), lambda i: (packed // width - 1, 0))
    specs += [out_part] * len(pairs)
    specs += [
        rows,
        per_pair(LONG, triple),
        pl.BlockSpec(memory_space=pl.ANY),
        per_pair(LONG, pair_width),
        per_pair(LONG, pair_width),
    ]
    if later:
        ins.append(before)
        specs.append(per_pair(packed, pair_width))
    count = len(pairs) if split else 1
    if split:
        out_specs = [whole(packed, pair_width)] * count
        outs = [shape((packed, pair_width), BF)] * count
    else:
        out_specs = [per_pair(packed, pair_width)]
        outs = [shape((len(pairs), packed, pair_width), BF)]
    out_specs.append(pl.BlockSpec((1, LONG, triple), lambda i: (i, 0, 0)))
    outs.append(shape((len(pairs), LONG, triple), BF))
    if begins:
        out_specs += [whole(1, width), pl.BlockSpec((LONG // len(pairs), width), lambda i: (i, 0))]
        outs += [shape((1, width), F32), shape((LONG, width), BF)]
    results = call(
        functools.partial(backward_kernel, pairs, begins, later, split),
        f"backward_{chunk}_{first}",
        (len(pairs),),
        specs,
        out_specs,
        outs,
        [
            pltpu.VMEM((width, LONG), BF),
            pltpu.VMEM((pair_width, width), BF),
            pltpu.VMEM((2, LONG, LONG), BF),
            pltpu.VMEM((2, 2, kept, TILE, TILE), BF),
            pltpu.SemaphoreType.DMA((2,)),
        ]
        + [pltpu.VMEM((LONG, width), BF)] * begins,
        (6e9 * len(pairs), 6e6 * len(pairs), 0),
        limit=LARGE,
    )(*ins)
    weights = dict(zip(pairs, results)) if split else results[0]
    return weights, results[count], results[count + 1 :]


def finish_kernel(groups, cuts, sent, *refs):
    chunks = len(groups)
    refs = list(refs)
    take = lambda count: [refs.pop(0) for _ in range(count)]
    tokens, gain_first = take(2)
    controls, gains, (bias_e, bias_r) = take(chunks), take(chunks), take(2)
    parts = take(sum(len(group) for group in groups[0]))
    grads = [take(len(groups[chunk])) for chunk in range(chunks)]
    resids = take(chunks)
    grad_tokens, small, weights = refs
    experts = controls[0].shape[0]
    step = pl.program_id(0)
    width = tokens.shape[1]
    pairs, triple = len(parts), weights.shape[1] // len(parts)

    @pl.when(step == 0)
    def _():
        small[...] = jnp.zeros_like(small)
        small[:experts] = sum(part[...] for part in controls)
        small[experts + 1 : experts + 2] = sum(part[...] for part in gains)
        for block in range(bias_e.shape[1] // width):
            begin = sent + block
            small[begin : begin + 1] = bias_e[:, block * width : (block + 1) * width]
        small[begin + 1 : begin + 2] = bias_r[...]
        for pair, part in enumerate(parts):
            cut = triple // 3
            for block in range(3):
                begin = pair * triple + block * cut
                weights[:, begin : begin + cut] = part[block * width : (block + 1) * width]

    for chunk in range(chunks):

        @pl.when(step // cuts == chunk)
        def _(chunk=chunk):
            columns = {}
            for group, ref in zip(groups[chunk], grads[chunk]):
                for index, pair in enumerate(group):
                    columns[pair] = ref[index]
            joined = jnp.concatenate([columns[pair] for pair in range(pairs)], axis=1)
            unit, scaling = normalize(tokens[...].astype(F32))
            through, gain_grad = normalize_back(
                dot_cols(joined, weights[...]), gain_first[...], unit, scaling
            )
            small[experts : experts + 1] += gain_grad
            grad_tokens[...] = resids[chunk][...].astype(F32) + through


def finish_part(tokens, gain_first, smalls, sent, parts, groups, grads, resids):
    total, width = tokens.shape
    chunks = total // LONG
    packed, pair_width = parts[0].shape
    cuts = 2
    share = LONG // cuts
    hidden = smalls[-2].shape[1]
    count = -(-(sent + hidden // width + 1) // 8) * 8
    rows = pl.BlockSpec((share, width), lambda i: (i, 0))
    flat = [(chunk, ref) for chunk, refs in enumerate(grads) for ref in refs]
    place = lambda chunk: lambda i: jnp.clip(i - chunk * cuts, 0, cuts - 1)
    grad_block = lambda chunk, ref: pl.BlockSpec(
        (ref.shape[0], share, ref.shape[2]), lambda i: (0, place(chunk)(i), 0)
    )
    resid_block = lambda chunk: pl.BlockSpec((share, width), lambda i: (place(chunk)(i), 0))
    return call(
        functools.partial(finish_kernel, groups, cuts, sent),
        "finish",
        (chunks * cuts,),
        [rows, whole(1, width)]
        + [whole(*part.shape) for part in smalls]
        + [whole(3 * width, pair_width)] * len(parts)
        + [grad_block(chunk, ref) for chunk, ref in flat]
        + [resid_block(chunk) for chunk in range(chunks)],
        [rows, whole(count, width)],
        [shape((total, width), F32), shape((count, width), F32)],
        [pltpu.VMEM((width, 3 * pair_width * len(parts)), BF)],
        (2 * total * width * 3 * pair_width * len(parts), 2e7, 0),
        limit=LARGE,
    )(tokens, gain_first, *smalls, *parts, *[ref for _, ref in flat], *resids)


def tail_pack_kernel(*refs):
    total = refs[0][...].astype(F32)
    for part in refs[1:-1]:
        total = total + part[...].astype(F32)
    refs[-1][...] = total.astype(BF)


def tail_pack(parts):
    rows, cut = parts[0].shape
    return call(
        tail_pack_kernel,
        "tail_pack",
        (1,),
        [whole(rows, cut)] * len(parts),
        whole(rows, cut),
        shape((rows, cut), BF),
        cost=(0, 3e6, 0),
    )(*parts)


def tail_sum_kernel(slots, pieces, out):
    total = pieces[0].astype(F32)
    for index in range(1, slots):
        total = total + pieces[index].astype(F32)
    out[...] = total.astype(BF)


def tail_sum(pieces):
    slots, share, cut = pieces.shape
    return call(
        functools.partial(tail_sum_kernel, slots),
        "tail_sum",
        (1,),
        [whole(slots, share, cut)],
        whole(share, cut),
        shape((share, cut), BF),
        cost=(0, 1e6, 0),
    )(pieces)


def small_sum_kernel(sent, *refs):
    *parts, out, bias_e, bias_r = refs
    small = tree_sum([part[...] for part in parts])
    out[...] = small[:sent]
    width = bias_r.shape[1]
    rows = bias_e.shape[1] // width
    for index in range(rows):
        bias_e[:, index * width : (index + 1) * width] = small[sent + index : sent + index + 1]
    bias_r[...] = small[sent + rows : sent + rows + 1]


def small_sum(smalls, sent, hidden):
    count, width = smalls[0].shape
    return call(
        functools.partial(small_sum_kernel, sent),
        "small_sum",
        (1,),
        [whole(count, width)] * len(smalls),
        [whole(sent, width), whole(1, hidden), whole(1, width)],
        [shape((sent, width), F32), shape((1, hidden), F32), shape((1, width), F32)],
        cost=(0, 1e5, 0),
    )(*smalls)


def tail_join_kernel(slots, own, came, own_small, came_small, out):
    share, cut = own.shape
    total = (own[...].astype(F32) + came[...].astype(F32)).astype(BF)
    small = own_small[...] + came_small[...]
    packed = jnp.concatenate(
        [small[:, begin : begin + cut] for begin in range(0, small.shape[1], cut)], axis=0
    ).astype(BF)
    for index in range(slots):
        out[index, :share] = total
        out[index, share:] = packed


def tail_join(own, came, own_small, came_small, slots):
    share, cut = own.shape
    sent, width = own_small.shape
    rows = share + sent * width // cut
    return call(
        functools.partial(tail_join_kernel, slots),
        "tail_join",
        (1,),
        [whole(share, cut)] * 2 + [whole(sent, width)] * 2,
        whole(slots, rows, cut),
        shape((slots, rows, cut), BF),
        cost=(0, 2e6, 0),
    )(own, came, own_small, came_small)


def gather_kernel(slots, share, pieces, *refs):
    outs, gain_first, gain_second, control, total = refs[:4], refs[4], refs[5], refs[6], refs[7]
    for index in range(slots):
        total[index * share : (index + 1) * share] = pieces[index, :share].astype(F32)
    cut = total.shape[1]
    begin = 0
    for out in outs[:3]:
        out[...] = total[begin : begin + out.shape[0]]
        begin += out.shape[0]
    last = outs[3]
    blocks = last.shape[1] // cut
    for index in range(blocks):
        last[:, index * cut : (index + 1) * cut] = total[begin : begin + last.shape[0]]
        begin += last.shape[0]
    small = pieces[0, share:].astype(F32)
    for index in range(1, slots):
        small = small + pieces[index, share:].astype(F32)
    count = small.shape[0] // blocks
    small = jnp.concatenate(
        [small[index * count : (index + 1) * count] for index in range(blocks)], axis=1
    )
    experts = control.shape[0]
    gain_first[...] = small[experts : experts + 1]
    gain_second[...] = small[experts + 1 : experts + 2]
    control[...] = small[:experts]


def gather_weights(pieces, share, width, experts):
    slots, _, cut = pieces.shape
    outs = [(width, cut)] * 3 + [(cut, width), (1, width), (1, width), (experts, width)]
    return call(
        functools.partial(gather_kernel, slots, share),
        "gather_weights",
        (1,),
        [whole(*pieces.shape)],
        [whole(*dims) for dims in outs],
        [shape(dims, F32) for dims in outs],
        [pltpu.VMEM((share * slots, cut), F32)],
        (0, 3e6, 0),
    )(pieces)


def partner(value, axis, offset):
    count = lax.axis_size(axis)
    return lax.ppermute(value, axis, [(index, index ^ offset) for index in range(count)])


def exchange(value, axis):
    return lax.all_to_all(value, axis, 0, 0, tiled=True)


def tree_sum(parts):
    while len(parts) > 1:
        parts = [parts[index] + parts[index + 1] for index in range(0, len(parts), 2)]
    return parts[0]


def gather_head(part):
    sibling = partner(part, "head", 1)
    across = partner(part, "head", 2)
    return [part, sibling, across, partner(across, "head", 1)]


def add_low(*parts):
    return sum(part.astype(F32) for part in parts).astype(BF)


def after(value, *earlier):
    return lax.optimization_barrier((value, *earlier))[0]


def body(
    tokens,
    gain_first,
    w_query,
    w_key,
    w_value,
    w_out,
    gain_second,
    w_control,
    w_expand,
    b_expand,
    w_reduce,
    b_reduce,
    lengths,
    grad_output,
):
    rows_local, width = tokens.shape
    pair_width = w_query.shape[1]
    slots = lax.axis_size("quarter")
    half = lax.axis_index("half")
    chunks = rows_local // LONG
    place = [lax.axis_index("quarter"), lax.axis_index("head"), half]
    place = jnp.stack(place).astype(jnp.int32)
    gain_first = gain_first[None]
    gain_second = gain_second[None]
    parts = gather_head(pack_weights(w_query, w_key, w_value, w_out))
    experts = w_control.shape[1]
    swapped = jnp.concatenate([w_control[:, slots:], w_control[:, :slots]], axis=1)
    control = jnp.repeat(jnp.where(half == 0, w_control, swapped), QUEUE, axis=1)
    cotangents = exchange(pack_rows(grad_output, slots), "quarter")

    forwards, members = [], []
    for chunk in range(chunks):
        *saved, second = forward_part(
            chunk, place, lengths, tokens, gain_first, parts, gain_second
        )
        gain_first = after(gain_first, second)
        forwards.append(saved)
        second = after(second, cotangents)
        members.append(exchange(second, "quarter"))
    mixings, arrivals, last = [], [], second
    for chunk in range(chunks):
        mixing, stats, kept, sent = mixing_part(
            chunk, control, members[chunk], cotangents
        )
        mixings.append(mixing)
        last = sent
        arrivals.append((kept, partner(sent, "half", 1), stats, partner(stats, "half", 1)))
    weights, combined, answers, sums, saved_experts = [], [], [], [], []
    for chunk in range(chunks):
        kept, *others = arrivals[chunk]
        messages, weight = combine_part(chunk, after(kept, last), *others)
        weights.append(weight)
        combined.append(messages)
        last = messages
        if chunk:
            sums.append(column_part(chunk - 1, combined[-2], answers[-1]))
        messages = exchange(messages, "quarter")
        flat = messages.reshape(-1, width)
        replies, *saved = expert_part(
            chunk, flat, w_expand, b_expand, w_reduce, b_reduce
        )
        last = replies
        saved_experts.append((flat, *saved))
        replies = exchange(replies.reshape(messages.shape), "quarter")
        answers.append(replies)
    own, other, bias_e, bias_r = expert_weights(place, saved_experts)
    backs, merged, controls = [], None, []
    for chunk in range(chunks):
        if chunk == chunks - 1:
            sums.append(column_part(chunk, combined[-1], answers[-1]))
        back, merged, grad_control = unmix_part(
            chunk,
            place,
            control,
            mixings[chunk],
            weights[chunk],
            members[chunk],
            cotangents,
            (answers[chunk], partner(sums[chunk][1], "half", 1)),
            (sums[chunk][0], partner(sums[chunk][0], "half", 1)),
            merged,
        )
        backs.append(exchange(back, "quarter"))
        controls.append(grad_control)
    own = add_low(own, partner(other, "head", 1))
    backs[0] = after(backs[0], back, own)
    across = partner(own, "head", 2)
    placed = (own, across, partner(own, "head", 1), partner(across, "head", 1))

    pairs = tuple(reversed(range(len(parts))))
    early, late = pairs[: len(pairs) // 2], pairs[len(pairs) // 2 :]
    before, gains, groups, grads, resids = None, [], [], [], []
    for chunk in range(chunks):
        *saved, resid = forwards[chunk]
        back = backs[chunk]
        if chunk == chunks - 1:
            if gains:
                merged = after(merged, gains[-1])
            merged = exchange(merged, "quarter")
            start = (back, resid, grad_output, gain_second)
            first_weights, first_grads, (gain, low) = backward_part(
                chunk, early, start, None, parts, saved, before, True
            )
            joint = add_low(first_weights[2], partner(first_weights[3], "head", 1))
            pieces = [partner(joint, "head", 2)]
            second_weights, second_grads, _ = backward_part(
                chunk, late, None, after(low, joint, across), parts, saved, before, True
            )
            groups.append((early, late))
            grads.append((first_grads, second_grads))
        else:
            start = (back, resid, grad_output, gain_second)
            before, chunk_grads, (gain, low) = backward_part(
                chunk, pairs, start, None, parts, saved, before, False
            )
            groups.append((pairs,))
            grads.append((chunk_grads,))
        gains.append(gain)
        resids.append(low)
    resids[-1] = after(resids[-1], *pieces)
    hidden = bias_e.shape[1]
    sent = -(-(experts + 2) // 8) * 8
    smalls = (*controls, *gains, bias_e, bias_r)
    grad_tokens, small = finish_part(
        tokens, gain_first, smalls, sent, parts, groups, grads, resids
    )

    pieces.append(partner(after(second_weights[1], *pieces), "head", 1))
    packed = tail_pack([second_weights[0]] + pieces)
    smalls = [small] + [partner(small, "head", index) for index in range(1, len(parts))]
    packed = after(packed, merged, *placed)
    pieces = exchange(packed, "quarter").reshape(slots, -1, pair_width)
    total = tail_sum(after(pieces, small))
    output = output_part([saved[5] for saved in forwards], after(merged, total))
    small, grad_expand_bias, grad_reduce_bias = small_sum(smalls, sent, hidden)
    pieces = tail_join(after(total, output), partner(total, "half", 1), small, partner(small, "half", 1), slots)
    pieces = exchange(pieces, "quarter")
    share = parts[0].shape[0] // slots
    *weights, gain_first, gain_second, control = gather_weights(pieces, share, width, experts)
    grad_query, grad_key, grad_value, grad_w_out = weights
    grad_expand, grad_reduce = place_weights(place, *placed)
    return (
        output,
        grad_tokens,
        gain_first[0],
        grad_query,
        grad_key,
        grad_value,
        grad_w_out,
        gain_second[0],
        control.T,
        grad_expand,
        grad_expand_bias,
        grad_reduce,
        grad_reduce_bias,
    )


def solution(mesh):
    in_specs = (
        P(SEQ + ("head",), None),
        P(),
        P(None, "head"),
        P(None, "head"),
        P(None, "head"),
        P("head", None),
        P(),
        P(),
        P(SEQ, None, None),
        P(SEQ, None),
        P(SEQ, None, None),
        P(SEQ, None),
        P(SEQ, None),
        P(SEQ + ("head",), None),
    )
    out_specs = (
        P(SEQ + ("head",), None),
        P(SEQ + ("head",), None),
        P(),
        P(None, "head"),
        P(None, "head"),
        P(None, "head"),
        P("head", None),
        P(),
        P(),
        P(SEQ, None, None),
        P(SEQ, None),
        P(SEQ, None, None),
        P(SEQ, None),
    )
    devices = mesh.devices
    count, heads = devices.shape
    mesh = jax.sharding.Mesh(devices.reshape(2, count // 2, heads), SEQ + ("head",))
    return jax.shard_map(body, mesh=mesh, in_specs=in_specs, out_specs=out_specs, check_vma=False)
```

```python
import functools
import jax
import jax.numpy as jnp
from jax import lax
from jax.sharding import PartitionSpec as P
from jax.experimental import pallas as pl
from jax.experimental.pallas import tpu as pltpu

HEAD_DIM = 64
GROUP = 32
LONG = 1024
TILE = 256
QUEUE = 2 * LONG // GROUP
SEQ = ("half", "quarter")
WAITING = 1e+10
EPSILON = 1e-05
MASKED = -1000000000.0
SAFE = 50.0
BF = jnp.bfloat16
F32 = jnp.float32
ROWS_BY_ROWS = (((0,), (0,)), ((), ()))
COLS_BY_COLS = (((1,), (1,)), ((), ()))
LARGE = 62 * 1024 * 1024
SMALL = 28 * 1024 * 1024


def dot(left, right):
    return jnp.dot(left, right, preferred_element_type=F32)


def dot_rows(left, right):
    return lax.dot_general(left, right, ROWS_BY_ROWS, preferred_element_type=F32)


def dot_cols(left, right):
    return lax.dot_general(left, right, COLS_BY_COLS, preferred_element_type=F32)


def normalize(matrix):
    centre = jnp.mean(matrix, axis=1, keepdims=True)
    shifted = matrix - centre
    scaling = lax.rsqrt(jnp.mean(shifted * shifted, axis=1, keepdims=True) + EPSILON)
    return shifted * scaling, scaling


def normalize_back(grad_norm, gain, unit_rows, scaling):
    inner_grad = grad_norm * gain
    centred = (
        inner_grad
        - jnp.mean(inner_grad, axis=1, keepdims=True)
        - unit_rows * jnp.mean(inner_grad * unit_rows, axis=1, keepdims=True)
    )
    return scaling * centred, jnp.sum(grad_norm * unit_rows, axis=0, keepdims=True)


def whole(*shape):
    return pl.BlockSpec(shape, lambda *_: (0,) * len(shape))


def scalars():
    return pl.BlockSpec(memory_space=pltpu.SMEM)


def call(kernel, name, grid, in_specs, out_specs, out_shape, scratch=(), cost=(0, 0, 0), aliases=None, limit=SMALL):
    return pl.pallas_call(
        kernel,
        grid=grid,
        in_specs=in_specs,
        out_specs=out_specs,
        out_shape=out_shape,
        scratch_shapes=list(scratch),
        input_output_aliases=aliases or {},
        cost_estimate=pl.CostEstimate(
            flops=int(cost[0]), bytes_accessed=int(cost[1]), transcendentals=int(cost[2])
        ),
        compiler_params=pltpu.CompilerParams(vmem_limit_bytes=limit),
        name=name,
    )


def shape(dims, dtype):
    return jax.ShapeDtypeStruct(dims, dtype)


def tile_slot(row_tile, col_tile):
    return row_tile * (row_tile + 1) // 2 + col_tile


def halves(dtype):
    lane = lax.broadcasted_iota(jnp.int32, (1, 2 * HEAD_DIM), 1)
    first = (lane < HEAD_DIM).astype(F32)
    return first.astype(dtype), (1.0 - first).astype(dtype)


def out_weights(part, width):
    cut = part.shape[1]
    base = part.shape[0] - width
    blocks = [part[base + begin : base + begin + cut] for begin in range(0, width, cut)]
    return jnp.concatenate(blocks, axis=1)


def forward_kernel(pairs, chunk, chunks, *refs):
    place, lengths, tokens, gain_first = refs[:4]
    parts = refs[4 : 4 + pairs]
    gain_second = refs[4 + pairs]
    normed_out, qkv_out, exps, inverse, attended, resid, second = refs[5 + pairs : 12 + pairs]
    normed, weights, bias, attended_all, arrived = refs[12 + pairs :]
    step = pl.program_id(0)
    width = tokens.shape[1]
    pair_width = attended.shape[2]
    fetches = [
        pltpu.make_async_copy(part, weights.at[index], arrived.at[index])
        for index, part in enumerate(parts)
    ]
    tiles = LONG // TILE

    @pl.when(step == 0)
    def _():
        for fetch in fetches:
            fetch.start()
        unit, _ = normalize(tokens[...].astype(F32))
        normed[...] = (unit * gain_first[...]).astype(BF)
        base = 4 * (place[1] * chunks + chunk)
        first = lengths[0, base]
        second_bound = first + lengths[0, base + 1]
        third = second_bound + lengths[0, base + 2]
        for row_tile in range(tiles):
            row = lax.broadcasted_iota(jnp.int32, (TILE, 1), 0) + row_tile * TILE
            begin = jnp.where(row >= first, first, 0)
            begin = jnp.where(row >= second_bound, second_bound, begin)
            begin = jnp.where(row >= third, third, begin)
            col = lax.broadcasted_iota(jnp.int32, (TILE, LONG), 1)
            allowed = (col <= row) & (col >= begin)
            bias[pl.ds(row_tile * TILE, TILE), :] = jnp.where(allowed, 0.0, MASKED)

    for index, fetch in enumerate(fetches):

        @pl.when(step == index)
        def _(fetch=fetch):
            fetch.wait()

    share = LONG // pairs
    normed_out[...] = normed[pl.ds(pl.multiple_of(step * share, share), share), :]
    own = weights[step, : 3 * width]
    own = jnp.concatenate([own[begin : begin + width] for begin in range(0, 3 * width, width)], axis=1)
    qkv = dot(normed[...], own).astype(BF)
    qkv_out[0] = qkv
    queries = qkv[:, :pair_width] * BF(HEAD_DIM**-0.5)
    key_rows = qkv[:, pair_width : 2 * pair_width]
    value_rows = qkv[:, 2 * pair_width :]
    low_half, high_half = halves(BF)
    is_low = lax.broadcasted_iota(jnp.int32, (TILE, pair_width), 1) < HEAD_DIM
    masks = ((low_half, high_half), (high_half, low_half))
    head_queries = [queries * own for own, other in masks]
    head_values = [value_rows * own + other for own, other in masks]
    pair_row = lax.broadcasted_iota(jnp.int32, (pair_width, pair_width), 0) // HEAD_DIM
    pair_col = lax.broadcasted_iota(jnp.int32, (pair_width, pair_width), 1) // HEAD_DIM
    same_half = (pair_row == pair_col).astype(F32).astype(BF)
    sizes = [
        jnp.max(dot(part * part, same_half), axis=0, keepdims=True) for part in (queries, key_rows)
    ]
    tame = jnp.max(sizes[0] * sizes[1]) < SAFE * SAFE

    def attend(shift):
        for row_tile in range(tiles):
            begin, extent = row_tile * TILE, (row_tile + 1) * TILE
            raw = []
            for head in range(2):
                scores = dot_cols(head_queries[head][begin:extent], key_rows[:extent])
                scores = scores + bias[begin:extent, :extent]
                if shift:
                    scores = scores - jnp.max(scores, axis=1, keepdims=True)
                powers = jnp.exp(scores).astype(BF)
                for col_tile in range(row_tile + 1):
                    exps[0, head, tile_slot(row_tile, col_tile)] = powers[
                        :, col_tile * TILE : (col_tile + 1) * TILE
                    ]
                raw.append(dot(powers, head_values[head][:extent]))
            totals = jnp.where(
                is_low, pltpu.roll(raw[0], HEAD_DIM, 1), pltpu.roll(raw[1], HEAD_DIM, 1)
            )
            inverted = 1.0 / totals
            inverse[0, begin:extent] = inverted.astype(BF)
            attended_tile = (jnp.where(is_low, raw[0], raw[1]) * inverted).astype(BF)
            attended[0, begin:extent] = attended_tile
            attended_all[step, begin:extent] = attended_tile

    @pl.when(tame)
    def _():
        attend(False)

    @pl.when(jnp.logical_not(tame))
    def _():
        attend(True)

    @pl.when(step == pairs - 1)
    def _():
        rows = jnp.concatenate([attended_all[index] for index in range(pairs)], axis=1)
        blocks = width // pair_width
        own = jnp.concatenate([out_weights(weights[index], width) for index in range(pairs)], axis=0)
        total = tokens[...].astype(F32) + dot(rows, own)
        resid[...] = total.astype(BF)
        unit, _ = normalize(total)
        second[...] = (unit * gain_second[...]).astype(BF)


def forward_part(chunk, place, lengths, tokens, gain_first, parts, gain_second):
    rows, width = tokens.shape
    pairs = len(parts)
    packed, pair_width = parts[0].shape
    triple = 3 * pair_width
    kept = LONG // TILE * (LONG // TILE + 1) // 2
    per_pair = lambda *dims: pl.BlockSpec((1,) + dims, lambda i: (i,) + (0,) * len(dims))
    return call(
        functools.partial(forward_kernel, pairs, chunk, rows // LONG),
        f"forward_{chunk}",
        (pairs,),
        [scalars(), scalars(), pl.BlockSpec((LONG, width), lambda i: (chunk, 0)), whole(1, width)]
        + [pl.BlockSpec(memory_space=pl.ANY)] * pairs
        + [whole(1, width)],
        [
            pl.BlockSpec((LONG // pairs, width), lambda i: (i, 0)),
            per_pair(LONG, triple),
            per_pair(2, kept, TILE, TILE),
            per_pair(LONG, pair_width),
            per_pair(LONG, pair_width),
            whole(LONG, width),
            whole(LONG, width),
        ],
        [
            shape((LONG, width), BF),
            shape((pairs, LONG, triple), BF),
            shape((pairs, 2, kept, TILE, TILE), BF),
            shape((pairs, LONG, pair_width), BF),
            shape((pairs, LONG, pair_width), BF),
            shape((LONG, width), BF),
            shape((LONG, width), BF),
        ],
        [
            pltpu.VMEM((LONG, width), BF),
            pltpu.VMEM((pairs, packed, pair_width), BF),
            pltpu.VMEM((LONG, LONG), F32),
            pltpu.VMEM((pairs, LONG, pair_width), BF),
            pltpu.SemaphoreType.DMA((pairs,)),
        ],
        (10e9, 25e6, 5e6),
        limit=LARGE,
    )(place, lengths, tokens, gain_first, *parts, gain_second)


def pack_kernel(rows, out, buffer, arrived, left):
    slots, chunks, share, _ = out.shape
    places = [(index, chunk) for index in range(slots) for chunk in range(chunks)]
    loads, stores = [], []
    for slot, (index, chunk) in enumerate(places):
        begin = chunk * LONG + index * share
        loads.append(
            pltpu.make_async_copy(rows.at[pl.ds(begin, share)], buffer.at[slot], arrived.at[slot])
        )
        stores.append(pltpu.make_async_copy(buffer.at[slot], out.at[index, chunk], left.at[slot]))
    for load in loads:
        load.start()
    for load, store in zip(loads, stores):
        load.wait()
        store.start()
    for store in stores:
        store.wait()


def pack_rows(rows, slots):
    total, width = rows.shape
    chunks, share = total // LONG, LONG // slots
    count = slots * chunks
    return call(
        pack_kernel,
        "pack_cotangent",
        (1,),
        [pl.BlockSpec(memory_space=pl.ANY)],
        pl.BlockSpec(memory_space=pl.ANY),
        shape((slots, chunks, share, width), BF),
        [
            pltpu.VMEM((count, share, width), BF),
            pltpu.SemaphoreType.DMA((count,)),
            pltpu.SemaphoreType.DMA((count,)),
        ],
        (0, 4 * total * width, 0),
        limit=LARGE,
    )(rows)


def pack_weights_kernel(query, key, value, out, packed):
    width, cut = query.shape
    for index, part in enumerate((query, key, value)):
        packed[index * width : (index + 1) * width] = part[...]
    for index in range(width // cut):
        begin = 3 * width + index * cut
        packed[begin : begin + cut] = out[:, index * cut : (index + 1) * cut]


def pack_weights(query, key, value, out):
    width, cut = query.shape
    return call(
        pack_weights_kernel,
        "pack_weights",
        (1,),
        [whole(width, cut)] * 3 + [whole(cut, width)],
        whole(4 * width, cut),
        shape((4 * width, cut), BF),
        cost=(0, 16 * width * cut, 0),
    )(query, key, value, out)


def group_mask(slots, columns):
    share = LONG // slots
    stride = share // QUEUE
    row = lax.broadcasted_iota(jnp.int32, (LONG, columns), 0)
    col = lax.broadcasted_iota(jnp.int32, (LONG, columns), 1)
    return ((row % share) // stride) == (col % QUEUE)


def chunk_block(slots, rows, width, chunk):
    return pl.BlockSpec((slots, 1, rows, width), lambda i: (0, chunk, 0, 0))


def mixing_kernel(slots, control, members, cotangents, mixing_out, stats, kept, sent):
    width, columns = control.shape
    rows = members[...]
    grads = cotangents[...].reshape(LONG, width)
    logits = jnp.where(group_mask(slots, columns), dot(rows, control[...]), -1e30)
    highest = jnp.max(logits, axis=0, keepdims=True)
    powers = jnp.exp(logits - highest)
    total = jnp.sum(powers, axis=0, keepdims=True)
    stats[0:1] = highest
    stats[1:2] = total
    low = (powers / total).astype(BF)
    mixing_out[...] = low
    mixed = dot_rows(low, rows).astype(BF)
    grad_out = dot_rows(low, grads).astype(BF)
    for index in range(slots):
        for out, begin in ((kept, index * QUEUE), (sent, (index + slots) * QUEUE)):
            out[index, :QUEUE] = mixed[begin : begin + QUEUE]
            out[index, QUEUE:] = grad_out[begin : begin + QUEUE]


def mixing_part(chunk, control, members, cotangents):
    slots, chunks, share, _ = cotangents.shape
    width, columns = control.shape
    return call(
        functools.partial(mixing_kernel, slots),
        f"mixing_{chunk}",
        (1,),
        [whole(width, columns), whole(LONG, width), chunk_block(slots, share, width, chunk)],
        [whole(LONG, columns), whole(2, columns)] + [whole(slots, 2 * QUEUE, width)] * 2,
        [shape((LONG, columns), BF), shape((2, columns), F32)]
        + [shape((slots, 2 * QUEUE, width), BF)] * 2,
        cost=(1e6, 1e4, 0),
        limit=LARGE,
    )(control, members, cotangents)


def combine_kernel(slots, kept, came, own_stats, came_stats, messages, weights):
    columns = own_stats.shape[1]
    middle = columns // 2
    other = jnp.concatenate([came_stats[:, middle:], came_stats[:, :middle]], axis=1)
    highest = jnp.maximum(own_stats[0:1], other[0:1])
    own_total = own_stats[1:2] * jnp.exp(own_stats[0:1] - highest)
    other_total = other[1:2] * jnp.exp(other[0:1] - highest)
    own_share = own_total / (own_total + other_total)
    weights[...] = own_share
    turned = jnp.broadcast_to(own_share[:, :middle], (8, middle)).T
    for index in range(slots):
        share = turned[index * QUEUE : (index + 1) * QUEUE, 0:1]
        for begin in (0, QUEUE):
            part = slice(begin, begin + QUEUE)
            one = kept[index, part].astype(F32)
            two = came[index, part].astype(F32)
            messages[index, part] = (two + share * (one - two)).astype(BF)


def combine_part(chunk, kept, came, own_stats, came_stats):
    slots, rows, width = kept.shape
    columns = own_stats.shape[1]
    return call(
        functools.partial(combine_kernel, slots),
        f"combine_{chunk}",
        (1,),
        [whole(slots, rows, width)] * 2 + [whole(2, columns)] * 2,
        [whole(slots, rows, width), whole(1, columns)],
        [shape((slots, rows, width), BF), shape((1, columns), F32)],
        cost=(WAITING, 2e6, 0),
    )(kept, came, own_stats, came_stats)


def column_kernel(slots, messages, answers, out, again):
    again[...] = answers[...]
    sums = []
    for index in range(slots):
        mixed = messages[index, :QUEUE].astype(F32)
        grad_out = messages[index, QUEUE:].astype(F32)
        expert_out = answers[index, :QUEUE].astype(F32)
        grad_mixed = answers[index, QUEUE:].astype(F32)
        products = expert_out * grad_out + grad_mixed * mixed
        sums.append(jnp.sum(products, axis=1, keepdims=True))
    sums = jnp.concatenate(sums, axis=0)
    out[...] = jnp.broadcast_to(sums, (sums.shape[0], 8)).T


def column_part(chunk, messages, answers):
    slots, rows, width = messages.shape
    return call(
        functools.partial(column_kernel, slots),
        f"columns_{chunk}",
        (1,),
        [whole(slots, rows, width)] * 2,
        [whole(8, slots * QUEUE), whole(slots, rows, width)],
        [shape((8, slots * QUEUE), F32), shape((slots, rows, width), BF)],
        cost=(1e6, 1e4, 0),
    )(messages, answers)


def expert_kernel(slots, messages, w_expand, b_expand, w_reduce, b_reduce, *refs):
    answers, activated_out, grad_pre_out, taken, grads, out_sum, mixed_sum = refs
    step = pl.program_id(0)

    @pl.when(step == 0)
    def _():
        for index in range(slots):
            begin = 2 * QUEUE * index
            part = slice(index * QUEUE, (index + 1) * QUEUE)
            taken[part] = messages[begin : begin + QUEUE]
            grads[part] = messages[begin + QUEUE : begin + 2 * QUEUE]
        out_sum[...] = jnp.zeros_like(out_sum)
        mixed_sum[...] = jnp.zeros_like(mixed_sum)

    pre = dot(taken[...], w_expand[0]) + b_expand[...]
    slope = 0.7978845608028654
    square = pre * pre
    bend = jnp.tanh(slope * (pre + 0.044715 * (pre * square)))
    half = 0.5 * (1.0 + bend)
    activated = (pre * half).astype(BF)
    activated_out[...] = activated
    out_sum[...] += dot(activated, w_reduce[0])
    derivative = half + (0.5 * slope) * pre * (1.0 - bend * bend) * (1.0 + 0.134145 * square)
    grad_pre = (dot_cols(grads[...], w_reduce[0]) * derivative).astype(BF)
    grad_pre_out[...] = grad_pre
    mixed_sum[...] += dot_cols(grad_pre, w_expand[0])

    @pl.when(step == pl.num_programs(0) - 1)
    def _():
        for index in range(slots):
            begin = 2 * QUEUE * index
            part = slice(index * QUEUE, (index + 1) * QUEUE)
            answers[begin : begin + QUEUE] = (out_sum[part] + b_reduce[...]).astype(BF)
            answers[begin + QUEUE : begin + 2 * QUEUE] = mixed_sum[part].astype(BF)


def expert_part(chunk, messages, w_expand, b_expand, w_reduce, b_reduce):
    _, width, hidden = w_expand.shape
    count = messages.shape[0] // 2
    slots = count // QUEUE
    cut = min(1024, hidden)
    outs = call(
        functools.partial(expert_kernel, slots),
        f"expert_{chunk}",
        (hidden // cut,),
        [
            whole(2 * count, width),
            pl.BlockSpec((1, width, cut), lambda i: (0, 0, i)),
            pl.BlockSpec((1, cut), lambda i: (0, i)),
            pl.BlockSpec((1, cut, width), lambda i: (0, i, 0)),
            whole(1, width),
        ],
        [
            whole(2 * count, width),
            pl.BlockSpec((count, cut), lambda i: (0, i)),
            pl.BlockSpec((count, cut), lambda i: (0, i)),
        ],
        [shape((2 * count, width), BF)] + [shape((count, hidden), BF)] * 2,
        [pltpu.VMEM((count, width), BF)] * 2 + [pltpu.VMEM((count, width), F32)] * 2,
        (1e6, 1e4, 0),
        limit=LARGE,
    )(messages, w_expand, b_expand, w_reduce, b_reduce)
    return outs


def expert_weights_kernel(chunks, place, *refs):
    messages, activated, grad_pre = refs[:chunks], refs[chunks : 2 * chunks], refs[2 * chunks : 3 * chunks]
    own, other, bias_e, bias_r, full_e, full_r = refs[3 * chunks :]
    join = lambda parts: jnp.concatenate(parts, axis=0)
    pick = lambda offset: join(
        [
            part[begin + offset : begin + offset + QUEUE]
            for part in messages
            for begin in range(0, part.shape[0], 2 * QUEUE)
        ]
    )
    taken, cotangent = pick(0), pick(QUEUE)
    pre = join([part[...] for part in grad_pre])
    full_e[...] = dot_rows(taken, pre).astype(BF)
    full_r[...] = dot_rows(join([part[...] for part in activated]), cotangent).astype(BF)
    bias_e[...] = jnp.sum(pre.astype(F32), axis=0, keepdims=True)
    bias_r[...] = jnp.sum(cotangent.astype(F32), axis=0, keepdims=True)
    begin = 0
    for full in (full_e, full_r):
        cut = full.shape[0] // 2
        for out, side in ((own, place[1] % 2), (other, 1 - place[1] % 2)):
            out[begin : begin + cut] = full[pl.ds(pl.multiple_of(side * cut, cut), cut), :]
        begin += cut


def expert_weights(place, kept):
    chunks = len(kept)
    messages, activated, grad_pre = zip(*kept)
    count, hidden = activated[0].shape
    width = messages[0].shape[1]
    cut = width
    wide = lambda rows: pl.BlockSpec((rows, cut), lambda i: (0, i))
    tall = pl.BlockSpec((cut, width), lambda i: (i, 0))
    return call(
        functools.partial(expert_weights_kernel, chunks),
        "expert_weights",
        (hidden // cut,),
        [scalars()] + [whole(2 * count, width)] * chunks + [wide(count)] * (2 * chunks),
        [tall, tall, wide(1), whole(1, width)],
        [shape((hidden, width), BF)] * 2 + [shape((1, hidden), F32), shape((1, width), F32)],
        [pltpu.VMEM((width, cut), BF), pltpu.VMEM((cut, width), BF)],
        (WAITING, 1e4, 0),
        limit=LARGE,
    )(place, *messages, *activated, *grad_pre)


def place_weights_kernel(place, own, own_across, other, other_across, out_e, out_r):
    begin = 0
    for out in (out_e, out_r):
        cut = out.shape[1] // 2
        part = slice(begin, begin + cut)
        for one, two, side in (
            (own, own_across, place[1] % 2),
            (other, other_across, 1 - place[1] % 2),
        ):
            total = one[part].astype(F32) + two[part].astype(F32)
            out[0, pl.ds(pl.multiple_of(side * cut, cut), cut), :] = total
        begin += cut


def place_weights(place, *parts):
    hidden, width = parts[0].shape
    cut = width
    tall = pl.BlockSpec((cut, width), lambda i: (i, 0))
    return call(
        place_weights_kernel,
        "place_expert_weights",
        (hidden // cut,),
        [scalars()] + [tall] * len(parts),
        [
            pl.BlockSpec((1, width, cut), lambda i: (0, 0, i)),
            pl.BlockSpec((1, cut, width), lambda i: (0, i, 0)),
        ],
        [shape((1, width, hidden), F32), shape((1, hidden, width), F32)],
        cost=(0, 16 * width * hidden, 0),
        limit=LARGE,
    )(place, *parts)


def unmix_kernel(slots, place, control, mixing_ref, weights, members, cotangents, *refs):
    own_answers, other_answers, own_sums, other_sums, back, merged, control_out = refs
    rows = members[...]
    grads = cotangents[...].reshape(rows.shape)
    pick = lambda part: jnp.concatenate(
        [answers[index, part] for answers in (own_answers, other_answers) for index in range(slots)],
        axis=0,
    )
    expert_out, grad_mixed = pick(slice(0, QUEUE)), pick(slice(QUEUE, 2 * QUEUE))
    mixing = mixing_ref[...].astype(F32) * weights[...]
    low = mixing.astype(BF)
    grad_mixing = dot_cols(grads, expert_out) + dot_cols(rows, grad_mixed)
    sums = jnp.concatenate([own_sums[0:1], other_sums[0:1]], axis=1)
    grad_logits = (mixing * (grad_mixing - sums)).astype(BF)
    back[...] = (dot(low, grad_mixed) + dot_cols(grad_logits, control[...])).astype(BF)
    merged[...] = dot(low, expert_out).astype(BF).reshape(merged.shape)
    grad_control = dot_rows(grad_logits, rows)
    for index in range(2 * slots):
        expert = place[2] * slots + index if index < slots else (1 - place[2]) * slots + index - slots
        control_out[pl.ds(expert, 1), :] = jnp.sum(
            grad_control[index * QUEUE : (index + 1) * QUEUE], axis=0, keepdims=True
        )


def without_previous(kernel, position):
    def inner(*refs):
        return kernel(*refs[:position], *refs[position + 1 :])

    return inner


def unmix_part(
    chunk, place, control, mixing, weights, members, cotangents, answers, sums, previous
):
    slots, chunks, share, width = cotangents.shape
    columns = control.shape[1]
    kernel = functools.partial(unmix_kernel, slots)
    ins = [place, control, mixing, weights, members, cotangents, *answers, *sums]
    specs = [
        scalars(),
        whole(width, columns),
        whole(LONG, columns),
        whole(1, columns),
        whole(LONG, width),
        chunk_block(slots, share, width, chunk),
    ]
    specs += [whole(slots, 2 * QUEUE, width)] * 2 + [whole(8, columns // 2)] * 2
    aliases = {}
    if previous is not None:
        aliases = {len(ins): 1}
        kernel = without_previous(kernel, len(ins))
        ins.append(previous)
        specs.append(pl.BlockSpec(memory_space=pl.ANY))
    return call(
        kernel,
        f"unmix_{chunk}",
        (1,),
        specs,
        [whole(LONG, width), chunk_block(slots, share, width, chunk), whole(2 * slots, width)],
        [
            shape((LONG, width), BF),
            shape((slots, chunks, share, width), BF),
            shape((2 * slots, width), F32),
        ],
        (),
        (WAITING, 6e6, 0),
        aliases,
        limit=LARGE,
    )(*ins)


def output_kernel(chunks, *refs):
    merged, out = refs[chunks:]
    for chunk in range(chunks):
        rows = merged[:, chunk].reshape(LONG, out.shape[1]).astype(F32)
        out[chunk * LONG : (chunk + 1) * LONG] = (refs[chunk][...].astype(F32) + rows).astype(BF)


def output_part(resids, merged):
    slots, chunks, share, width = merged.shape
    return call(
        functools.partial(output_kernel, chunks),
        "output",
        (1,),
        [whole(LONG, width)] * chunks + [whole(slots, chunks, share, width)],
        whole(chunks * LONG, width),
        shape((chunks * LONG, width), BF),
        cost=(0, 8e6, 0),
    )(*resids, merged)


def backward_kernel(pairs, begins, later, split, *refs):
    refs = list(refs)
    take = lambda count: [refs.pop(0) for _ in range(count)]
    if begins:
        back, resid, grad_output, gain_second = take(4)
    else:
        (resid_low,) = take(1)
    parts = take(len(pairs))
    normed, qkv, exps, inverse, attended = take(5)
    (weights_before,) = take(1) if later else (None,)
    weights_out = take(len(pairs) if split else 1)
    (grads_out,) = take(1)
    if begins:
        gains_out, low_out = take(2)
    normed_turned, o_now, grad_scores_all, exps_now, arrived = take(5)
    if begins:
        (resid_low,) = take(1)
    step = pl.program_id(0)
    pair_width = attended.shape[2]
    tiles = LONG // TILE

    def fetch(index):
        slot = lax.rem(index, 2)
        return pltpu.make_async_copy(exps.at[pairs[0] - index], exps_now.at[slot], arrived.at[slot])

    @pl.when(step == 0)
    def _():
        fetch(step).start()

    @pl.when(step + 1 < len(pairs))
    def _():
        fetch(step + 1).start()

    @pl.when(step == 0)
    def _():
        normed_turned[...] = normed[...].T
        if begins:
            unit, scaling = normalize(resid[...].astype(F32))
            through, gain_grad = normalize_back(
                back[...].astype(F32), gain_second[...], unit, scaling
            )
            gains_out[...] = gain_grad
            resid_low[...] = (grad_output[...].astype(F32) + through).astype(BF)

    for index, part in enumerate(parts):

        @pl.when(step == index)
        def _(part=part):
            o_now[...] = out_weights(part[...], o_now.shape[1])

    if begins:
        share = low_out.shape[0]
        low_out[...] = resid_low[pl.ds(pl.multiple_of(step * share, share), share), :]
    low = resid_low[...]
    fetch(step).wait()
    exps = exps_now.at[lax.rem(step, 2)]
    grad_attended = dot_cols(low, o_now[...]).astype(BF)
    grad_out_weights = dot_rows(attended[0], low)
    wide = grad_attended.astype(F32)
    inverted = inverse[0].astype(F32)
    scaled = wide * inverted
    products = scaled * attended[0].astype(F32)
    scaled = scaled.astype(BF)
    low_half, high_half = halves(BF)
    low_wide, high_wide = halves(F32)
    queries = qkv[0, :, :pair_width] * BF(HEAD_DIM**-0.5)
    key_rows = qkv[0, :, pair_width : 2 * pair_width]
    value_rows = qkv[0, :, 2 * pair_width :]
    scaled_keys = key_rows * BF(HEAD_DIM**-0.5)
    queries_turned = queries.T
    grads_turned = scaled.T
    ones = (high_half, low_half)
    joined_q, joined_k, joined_v = [], [], []
    both = []
    for head, (half, half_wide) in enumerate(((low_half, low_wide), (high_half, high_wide))):
        deltas = jnp.sum(products * half_wide, axis=1, keepdims=True)
        both.append((scaled * half, scaled_keys * half, deltas))
    query_rows = []
    for row_tile in range(tiles):
        begin, extent = row_tile * TILE, (row_tile + 1) * TILE
        total = None
        for head, (head_grads, head_keys, deltas) in enumerate(both):
            powers = jnp.concatenate(
                [exps[head, tile_slot(row_tile, col_tile)] for col_tile in range(row_tile + 1)],
                axis=1,
            )
            grad_probs = dot_cols(head_grads[begin:extent], value_rows[:extent])
            grad_scores = (powers.astype(F32) * (grad_probs - deltas[begin:extent])).astype(BF)
            grad_scores_all[head, begin:extent, :extent] = grad_scores
            product = dot(grad_scores, head_keys[:extent])
            total = product if total is None else total + product
        query_rows.append(total)
    joined_q = [jnp.concatenate(query_rows, axis=0)]
    for head in range(2):
        part = slice(head * HEAD_DIM, (head + 1) * HEAD_DIM)
        key_cols, value_cols = [], []
        for col_tile in range(tiles):
            begin, extent = col_tile * TILE, (col_tile + 1) * TILE
            powers = jnp.concatenate(
                [exps[head, tile_slot(row_tile, col_tile)] for row_tile in range(col_tile, tiles)],
                axis=0,
            )
            key_cols.append(
                dot(queries_turned[part, begin:], grad_scores_all[head, begin:, begin:extent])
            )
            value_cols.append(dot(grads_turned[part, begin:], powers))
        joined_k.append(jnp.concatenate(key_cols, axis=1))
        joined_v.append(jnp.concatenate(value_cols, axis=1))
    grads = jnp.concatenate(
        [
            joined_q[0].astype(BF),
            jnp.concatenate(joined_k, axis=0).T.astype(BF),
            jnp.concatenate(joined_v, axis=0).T.astype(BF),
        ],
        axis=1,
    )
    grads_out[0] = grads
    grad_weights = dot(normed_turned[...], grads)
    width = normed.shape[1]
    blocks = [grad_weights[:, index * pair_width : (index + 1) * pair_width] for index in range(3)]
    blocks += [
        grad_out_weights[:, index * pair_width : (index + 1) * pair_width]
        for index in range(width // pair_width)
    ]
    def store(out):
        begin = 0
        for block in blocks:
            extent = begin + block.shape[0]
            if later:
                block = block + weights_before[0, begin:extent].astype(F32)
            out[begin:extent] = block.astype(BF)
            begin = extent

    if split:
        for index, out in enumerate(weights_out):

            @pl.when(step == index)
            def _(out=out):
                store(out)

    else:
        store(weights_out[0].at[0])


def backward_part(chunk, pairs, start, low, parts, saved, before, split):
    exps = saved[2]
    width = saved[0].shape[1]
    packed, pair_width = parts[0].shape
    triple = 3 * pair_width
    kept = exps.shape[2]
    first = pairs[0]
    per_pair = lambda *dims: pl.BlockSpec((1,) + dims, lambda i: (first - i,) + (0,) * len(dims))
    rows = whole(LONG, width)
    begins, later = start is not None, before is not None
    if begins:
        ins = [*start]
        specs = [rows, rows, pl.BlockSpec((LONG, width), lambda i: (chunk, 0)), whole(1, width)]
    else:
        ins, specs = [low], [rows]
    ins += [parts[pair] for pair in pairs] + list(saved)
    out_part = pl.BlockSpec((width, pair_width), lambda i: (packed // width - 1, 0))
    specs += [out_part] * len(pairs)
    specs += [
        rows,
        per_pair(LONG, triple),
        pl.BlockSpec(memory_space=pl.ANY),
        per_pair(LONG, pair_width),
        per_pair(LONG, pair_width),
    ]
    if later:
        ins.append(before)
        specs.append(per_pair(packed, pair_width))
    count = len(pairs) if split else 1
    if split:
        out_specs = [whole(packed, pair_width)] * count
        outs = [shape((packed, pair_width), BF)] * count
    else:
        out_specs = [per_pair(packed, pair_width)]
        outs = [shape((len(pairs), packed, pair_width), BF)]
    out_specs.append(pl.BlockSpec((1, LONG, triple), lambda i: (i, 0, 0)))
    outs.append(shape((len(pairs), LONG, triple), BF))
    if begins:
        out_specs += [whole(1, width), pl.BlockSpec((LONG // len(pairs), width), lambda i: (i, 0))]
        outs += [shape((1, width), F32), shape((LONG, width), BF)]
    results = call(
        functools.partial(backward_kernel, pairs, begins, later, split),
        f"backward_{chunk}_{first}",
        (len(pairs),),
        specs,
        out_specs,
        outs,
        [
            pltpu.VMEM((width, LONG), BF),
            pltpu.VMEM((pair_width, width), BF),
            pltpu.VMEM((2, LONG, LONG), BF),
            pltpu.VMEM((2, 2, kept, TILE, TILE), BF),
            pltpu.SemaphoreType.DMA((2,)),
        ]
        + [pltpu.VMEM((LONG, width), BF)] * begins,
        (6e9 * len(pairs), 6e6 * len(pairs), 0),
        limit=LARGE,
    )(*ins)
    weights = dict(zip(pairs, results)) if split else results[0]
    return weights, results[count], results[count + 1 :]


def finish_kernel(groups, cuts, sent, *refs):
    chunks = len(groups)
    refs = list(refs)
    take = lambda count: [refs.pop(0) for _ in range(count)]
    tokens, gain_first = take(2)
    controls, gains, (bias_e, bias_r) = take(chunks), take(chunks), take(2)
    parts = take(sum(len(group) for group in groups[0]))
    grads = [take(len(groups[chunk])) for chunk in range(chunks)]
    resids = take(chunks)
    grad_tokens, small, weights = refs
    experts = controls[0].shape[0]
    step = pl.program_id(0)
    width = tokens.shape[1]
    pairs, triple = len(parts), weights.shape[1] // len(parts)

    @pl.when(step == 0)
    def _():
        small[...] = jnp.zeros_like(small)
        small[:experts] = sum(part[...] for part in controls)
        small[experts + 1 : experts + 2] = sum(part[...] for part in gains)
        for block in range(bias_e.shape[1] // width):
            begin = sent + block
            small[begin : begin + 1] = bias_e[:, block * width : (block + 1) * width]
        small[begin + 1 : begin + 2] = bias_r[...]
        for pair, part in enumerate(parts):
            cut = triple // 3
            for block in range(3):
                begin = pair * triple + block * cut
                weights[:, begin : begin + cut] = part[block * width : (block + 1) * width]

    for chunk in range(chunks):

        @pl.when(step // cuts == chunk)
        def _(chunk=chunk):
            columns = {}
            for group, ref in zip(groups[chunk], grads[chunk]):
                for index, pair in enumerate(group):
                    columns[pair] = ref[index]
            joined = jnp.concatenate([columns[pair] for pair in range(pairs)], axis=1)
            unit, scaling = normalize(tokens[...].astype(F32))
            through, gain_grad = normalize_back(
                dot_cols(joined, weights[...]), gain_first[...], unit, scaling
            )
            small[experts : experts + 1] += gain_grad
            grad_tokens[...] = resids[chunk][...].astype(F32) + through


def finish_part(tokens, gain_first, smalls, sent, parts, groups, grads, resids):
    total, width = tokens.shape
    chunks = total // LONG
    packed, pair_width = parts[0].shape
    cuts = 2
    share = LONG // cuts
    hidden = smalls[-2].shape[1]
    count = -(-(sent + hidden // width + 1) // 8) * 8
    rows = pl.BlockSpec((share, width), lambda i: (i, 0))
    flat = [(chunk, ref) for chunk, refs in enumerate(grads) for ref in refs]
    place = lambda chunk: lambda i: jnp.clip(i - chunk * cuts, 0, cuts - 1)
    grad_block = lambda chunk, ref: pl.BlockSpec(
        (ref.shape[0], share, ref.shape[2]), lambda i: (0, place(chunk)(i), 0)
    )
    resid_block = lambda chunk: pl.BlockSpec((share, width), lambda i: (place(chunk)(i), 0))
    return call(
        functools.partial(finish_kernel, groups, cuts, sent),
        "finish",
        (chunks * cuts,),
        [rows, whole(1, width)]
        + [whole(*part.shape) for part in smalls]
        + [whole(3 * width, pair_width)] * len(parts)
        + [grad_block(chunk, ref) for chunk, ref in flat]
        + [resid_block(chunk) for chunk in range(chunks)],
        [rows, whole(count, width)],
        [shape((total, width), F32), shape((count, width), F32)],
        [pltpu.VMEM((width, 3 * pair_width * len(parts)), BF)],
        (2 * total * width * 3 * pair_width * len(parts), 2e7, 0),
        limit=LARGE,
    )(tokens, gain_first, *smalls, *parts, *[ref for _, ref in flat], *resids)


def tail_pack_kernel(*refs):
    total = refs[0][...].astype(F32)
    for part in refs[1:-1]:
        total = total + part[...].astype(F32)
    refs[-1][...] = total.astype(BF)


def tail_pack(parts):
    rows, cut = parts[0].shape
    return call(
        tail_pack_kernel,
        "tail_pack",
        (1,),
        [whole(rows, cut)] * len(parts),
        whole(rows, cut),
        shape((rows, cut), BF),
        cost=(0, 3e6, 0),
    )(*parts)


def tail_sum_kernel(slots, pieces, out):
    total = pieces[0].astype(F32)
    for index in range(1, slots):
        total = total + pieces[index].astype(F32)
    out[...] = total.astype(BF)


def tail_sum(pieces):
    slots, share, cut = pieces.shape
    return call(
        functools.partial(tail_sum_kernel, slots),
        "tail_sum",
        (1,),
        [whole(slots, share, cut)],
        whole(share, cut),
        shape((share, cut), BF),
        cost=(0, 1e6, 0),
    )(pieces)


def small_sum_kernel(sent, *refs):
    *parts, out, bias_e, bias_r = refs
    small = tree_sum([part[...] for part in parts])
    out[...] = small[:sent]
    width = bias_r.shape[1]
    rows = bias_e.shape[1] // width
    for index in range(rows):
        bias_e[:, index * width : (index + 1) * width] = small[sent + index : sent + index + 1]
    bias_r[...] = small[sent + rows : sent + rows + 1]


def small_sum(smalls, sent, hidden):
    count, width = smalls[0].shape
    return call(
        functools.partial(small_sum_kernel, sent),
        "small_sum",
        (1,),
        [whole(count, width)] * len(smalls),
        [whole(sent, width), whole(1, hidden), whole(1, width)],
        [shape((sent, width), F32), shape((1, hidden), F32), shape((1, width), F32)],
        cost=(0, 1e5, 0),
    )(*smalls)


def tail_join_kernel(slots, own, came, own_small, came_small, out):
    share, cut = own.shape
    total = (own[...].astype(F32) + came[...].astype(F32)).astype(BF)
    small = own_small[...] + came_small[...]
    packed = jnp.concatenate(
        [small[:, begin : begin + cut] for begin in range(0, small.shape[1], cut)], axis=0
    ).astype(BF)
    for index in range(slots):
        out[index, :share] = total
        out[index, share:] = packed


def tail_join(own, came, own_small, came_small, slots):
    share, cut = own.shape
    sent, width = own_small.shape
    rows = share + sent * width // cut
    return call(
        functools.partial(tail_join_kernel, slots),
        "tail_join",
        (1,),
        [whole(share, cut)] * 2 + [whole(sent, width)] * 2,
        whole(slots, rows, cut),
        shape((slots, rows, cut), BF),
        cost=(0, 2e6, 0),
    )(own, came, own_small, came_small)


def gather_kernel(slots, share, pieces, *refs):
    outs, gain_first, gain_second, control, total = refs[:4], refs[4], refs[5], refs[6], refs[7]
    for index in range(slots):
        total[index * share : (index + 1) * share] = pieces[index, :share].astype(F32)
    cut = total.shape[1]
    begin = 0
    for out in outs[:3]:
        out[...] = total[begin : begin + out.shape[0]]
        begin += out.shape[0]
    last = outs[3]
    blocks = last.shape[1] // cut
    for index in range(blocks):
        last[:, index * cut : (index + 1) * cut] = total[begin : begin + last.shape[0]]
        begin += last.shape[0]
    small = pieces[0, share:].astype(F32)
    for index in range(1, slots):
        small = small + pieces[index, share:].astype(F32)
    count = small.shape[0] // blocks
    small = jnp.concatenate(
        [small[index * count : (index + 1) * count] for index in range(blocks)], axis=1
    )
    experts = control.shape[0]
    gain_first[...] = small[experts : experts + 1]
    gain_second[...] = small[experts + 1 : experts + 2]
    control[...] = small[:experts]


def gather_weights(pieces, share, width, experts):
    slots, _, cut = pieces.shape
    outs = [(width, cut)] * 3 + [(cut, width), (1, width), (1, width), (experts, width)]
    return call(
        functools.partial(gather_kernel, slots, share),
        "gather_weights",
        (1,),
        [whole(*pieces.shape)],
        [whole(*dims) for dims in outs],
        [shape(dims, F32) for dims in outs],
        [pltpu.VMEM((share * slots, cut), F32)],
        (0, 3e6, 0),
    )(pieces)


def partner(value, axis, offset):
    count = lax.axis_size(axis)
    return lax.ppermute(value, axis, [(index, index ^ offset) for index in range(count)])


def exchange(value, axis):
    return lax.all_to_all(value, axis, 0, 0, tiled=True)


def tree_sum(parts):
    while len(parts) > 1:
        parts = [parts[index] + parts[index + 1] for index in range(0, len(parts), 2)]
    return parts[0]


def gather_head(part):
    sibling = partner(part, "head", 1)
    across = partner(part, "head", 2)
    return [part, sibling, across, partner(across, "head", 1)]


def add_low(*parts):
    return sum(part.astype(F32) for part in parts).astype(BF)


def after(value, *earlier):
    return lax.optimization_barrier((value, *earlier))[0]


def body(
    tokens,
    gain_first,
    w_query,
    w_key,
    w_value,
    w_out,
    gain_second,
    w_control,
    w_expand,
    b_expand,
    w_reduce,
    b_reduce,
    lengths,
    grad_output,
):
    rows_local, width = tokens.shape
    pair_width = w_query.shape[1]
    slots = lax.axis_size("quarter")
    half = lax.axis_index("half")
    chunks = rows_local // LONG
    place = [lax.axis_index("quarter"), lax.axis_index("head"), half]
    place = jnp.stack(place).astype(jnp.int32)
    gain_first = gain_first[None]
    gain_second = gain_second[None]
    parts = gather_head(pack_weights(w_query, w_key, w_value, w_out))
    experts = w_control.shape[1]
    swapped = jnp.concatenate([w_control[:, slots:], w_control[:, :slots]], axis=1)
    control = jnp.repeat(jnp.where(half == 0, w_control, swapped), QUEUE, axis=1)
    cotangents = exchange(pack_rows(grad_output, slots), "quarter")

    forwards, members = [], []
    for chunk in range(chunks):
        *saved, second = forward_part(
            chunk, place, lengths, tokens, gain_first, parts, gain_second
        )
        gain_first = after(gain_first, second)
        forwards.append(saved)
        second = after(second, cotangents)
        members.append(exchange(second, "quarter"))
    mixings, arrivals, last = [], [], second
    for chunk in range(chunks):
        mixing, stats, kept, sent = mixing_part(
            chunk, control, members[chunk], cotangents
        )
        mixings.append(mixing)
        last = sent
        arrivals.append((kept, partner(sent, "half", 1), stats, partner(stats, "half", 1)))
    weights, combined, answers, sums, saved_experts = [], [], [], [], []
    for chunk in range(chunks):
        kept, *others = arrivals[chunk]
        messages, weight = combine_part(chunk, after(kept, last), *others)
        weights.append(weight)
        combined.append(messages)
        last = messages
        if chunk:
            sums.append(column_part(chunk - 1, combined[-2], answers[-1]))
        messages = exchange(messages, "quarter")
        flat = messages.reshape(-1, width)
        replies, *saved = expert_part(
            chunk, flat, w_expand, b_expand, w_reduce, b_reduce
        )
        last = replies
        saved_experts.append((flat, *saved))
        replies = exchange(replies.reshape(messages.shape), "quarter")
        answers.append(replies)
    own, other, bias_e, bias_r = expert_weights(place, saved_experts)
    backs, merged, controls = [], None, []
    for chunk in range(chunks):
        if chunk == chunks - 1:
            sums.append(column_part(chunk, combined[-1], answers[-1]))
        back, merged, grad_control = unmix_part(
            chunk,
            place,
            control,
            mixings[chunk],
            weights[chunk],
            members[chunk],
            cotangents,
            (answers[chunk], partner(sums[chunk][1], "half", 1)),
            (sums[chunk][0], partner(sums[chunk][0], "half", 1)),
            merged,
        )
        backs.append(exchange(back, "quarter"))
        controls.append(grad_control)
    own = add_low(own, partner(other, "head", 1))
    backs[0] = after(backs[0], back, own)
    across = partner(own, "head", 2)
    placed = (own, across, partner(own, "head", 1), partner(across, "head", 1))

    pairs = tuple(reversed(range(len(parts))))
    early, late = pairs[: len(pairs) // 2], pairs[len(pairs) // 2 :]
    before, gains, groups, grads, resids = None, [], [], [], []
    for chunk in range(chunks):
        *saved, resid = forwards[chunk]
        back = backs[chunk]
        if chunk == chunks - 1:
            if gains:
                merged = after(merged, gains[-1])
            merged = exchange(merged, "quarter")
            start = (back, resid, grad_output, gain_second)
            first_weights, first_grads, (gain, low) = backward_part(
                chunk, early, start, None, parts, saved, before, True
            )
            joint = add_low(first_weights[2], partner(first_weights[3], "head", 1))
            pieces = [partner(joint, "head", 2)]
            second_weights, second_grads, _ = backward_part(
                chunk, late, None, after(low, joint, across), parts, saved, before, True
            )
            groups.append((early, late))
            grads.append((first_grads, second_grads))
        else:
            start = (back, resid, grad_output, gain_second)
            before, chunk_grads, (gain, low) = backward_part(
                chunk, pairs, start, None, parts, saved, before, False
            )
            groups.append((pairs,))
            grads.append((chunk_grads,))
        gains.append(gain)
        resids.append(low)
    resids[-1] = after(resids[-1], *pieces)
    hidden = bias_e.shape[1]
    sent = -(-(experts + 2) // 8) * 8
    smalls = (*controls, *gains, bias_e, bias_r)
    grad_tokens, small = finish_part(
        tokens, gain_first, smalls, sent, parts, groups, grads, resids
    )

    pieces.append(partner(after(second_weights[1], *pieces), "head", 1))
    packed = tail_pack([second_weights[0]] + pieces)
    smalls = [small] + [partner(small, "head", index) for index in range(1, len(parts))]
    packed = after(packed, merged, *placed)
    pieces = exchange(packed, "quarter").reshape(slots, -1, pair_width)
    total = tail_sum(after(pieces, small))
    output = output_part([saved[5] for saved in forwards], after(merged, total))
    small, grad_expand_bias, grad_reduce_bias = small_sum(smalls, sent, hidden)
    pieces = tail_join(after(total, output), partner(total, "half", 1), small, partner(small, "half", 1), slots)
    pieces = exchange(pieces, "quarter")
    share = parts[0].shape[0] // slots
    *weights, gain_first, gain_second, control = gather_weights(pieces, share, width, experts)
    grad_query, grad_key, grad_value, grad_w_out = weights
    grad_expand, grad_reduce = place_weights(place, *placed)
    return (
        output,
        grad_tokens,
        gain_first[0],
        grad_query,
        grad_key,
        grad_value,
        grad_w_out,
        gain_second[0],
        control.T,
        grad_expand,
        grad_expand_bias,
        grad_reduce,
        grad_reduce_bias,
    )


def solution(mesh):
    in_specs = (
        P(SEQ + ("head",), None),
        P(),
        P(None, "head"),
        P(None, "head"),
        P(None, "head"),
        P("head", None),
        P(),
        P(),
        P(SEQ, None, None),
        P(SEQ, None),
        P(SEQ, None, None),
        P(SEQ, None),
        P(SEQ, None),
        P(SEQ + ("head",), None),
    )
    out_specs = (
        P(SEQ + ("head",), None),
        P(SEQ + ("head",), None),
        P(),
        P(None, "head"),
        P(None, "head"),
        P(None, "head"),
        P("head", None),
        P(),
        P(),
        P(SEQ, None, None),
        P(SEQ, None),
        P(SEQ, None, None),
        P(SEQ, None),
    )
    devices = mesh.devices
    count, heads = devices.shape
    mesh = jax.sharding.Mesh(devices.reshape(2, count // 2, heads), SEQ + ("head",))
    return jax.shard_map(body, mesh=mesh, in_specs=in_specs, out_specs=out_specs, check_vma=False)
```
